32 devices in a mesh: dp: 8 (over y, x, core), tensor: 4 (over z).
Axes of the slice: x: 2, y: 2, z: 4, core: 2. Of those that a mesh axis runs over, the one named last changes fastest.
Arguments:
- tokens: bfloat16 [8, 1024, 1024], P('dp', 'tensor'), may hold values from -6 to 6
- segment_ids: int32 [8, 1024], P('dp'), may hold values from 0 to 128, as said below
- gain_attn: float32 [1024], replicated, may hold values from 0.5 to 1.5
- query_key_value_weight: bfloat16 [3, 1024, 1024], P(None, None, 'tensor'), may hold values from -0.25 to 0.25
- output_weight: bfloat16 [1024, 1024], P('tensor'), may hold values from -1.5 to 1.5
- gain_mlp: float32 [1024], replicated, may hold values from 0.5 to 1.5
- gate_up_weight: bfloat16 [2, 1024, 2624], P(None, None, 'tensor'), may hold values from -0.1875 to 0.1875
- down_weight: bfloat16 [2624, 1024], P('tensor'), may hold values from -0.25 to 0.25
- cotangent: bfloat16 [8, 1024, 1024], P('dp', 'tensor'), may hold values from -24 to 24
Outputs:
- layer_out: bfloat16 [8, 1024, 1024], P('dp', 'tensor')
- input_grad: bfloat16 [8, 1024, 1024], P('dp', 'tensor')
- grad_gain_attn: float32 [1024], replicated
- query_key_value_gradient: float32 [3, 1024, 1024], P(None, None, 'tensor')
- output_weight_gradient: float32 [1024, 1024], P('tensor')
- grad_gain_mlp: float32 [1024], replicated
- grad_gateup: float32 [2, 1024, 2624], P(None, None, 'tensor')
- down_weight_gradient: float32 [2624, 1024], P('tensor')
The draws below stay inside these ranges and needn't reach their ends.
Inputs may be any that keep to these rules, and one draw needn't show every extreme that they name: `segment_ids`: segment ids never fall along a sequence and start at 0; each sequence holds one document of exactly 896 tokens, and every other token is a document of one token.
All inputs are finite; a program needn't handle non-finite values.
Results may differ from the reference program's by a relative error of at most 0.015.
Values may be sent and summed in bfloat16 or wider, within the bound.
No kernel may reach another device: no remote copies, remote signals or barrier semaphores. Data moves between devices by JAX's collectives and lax.ppermute only.
A program may use at most 128 MiB of HBM per device.

```python
import math
import jax
import jax.numpy as jnp
from jax import lax

D = 1024
HEADS = 16
HD = 64
FF = 2624
LEN = 1024
SEQS_ALL = 8


def draw_segment_ids(key, part):
    key = jax.random.fold_in(key, 11)
    long_len = LEN - LEN // 8
    starts = jax.random.randint(key, (SEQS_ALL, 1), 0, LEN - long_len + 1)
    places = jnp.arange(LEN, dtype=jnp.int32)[None, :]
    inside = (places > starts) & (places < starts + long_len)
    boundary = jnp.logical_not(inside) & (places > 0)
    return jnp.cumsum(boundary.astype(jnp.int32), axis=1).astype(jnp.int32)


def draw_cotangent(key, part):
    key = jax.random.fold_in(key, 23)
    main_key, row_key = jax.random.split(key)
    seq_rise = 3.0 ** (jnp.arange(SEQS_ALL, dtype=jnp.float32) / max(SEQS_ALL - 1, 1))
    row_scale = jnp.exp(jax.random.uniform(row_key, (SEQS_ALL, LEN, 1), minval=-0.7, maxval=0.7))
    values = jax.random.truncated_normal(main_key, -4.0, 4.0, (SEQS_ALL, LEN, D))
    return (values * row_scale * seq_rise[:, None, None]).astype(jnp.bfloat16)


def block_scale(rng, extent, cuts, smallest, high):
    def one(axis_at, parts):
        heights = jax.random.uniform(jax.random.fold_in(jax.random.fold_in(rng, 6), axis_at), (parts,), jnp.float32, smallest / len(cuts), high / len(cuts))
        return jnp.repeat(jnp.exp(heights), extent[axis_at] // parts).reshape((-1,) + (1,) * (len(extent) - axis_at - 1))

    level = one(*cuts[0])
    for cut in cuts[1:]:
        level = level * one(*cut)
    return level


def bell_draw(key, shape, spread, most, pieces=(), kind=jnp.bfloat16):
    drawn = jax.random.normal(key, shape, jnp.float32) * spread
    if len(pieces) > 0:
        drawn = block_scale(key, shape, pieces, -0.22, 0.18) * drawn
    return jnp.clip(drawn, min=-most, max=most).astype(kind)


def setup_inputs(seed: int = 0) -> dict:
    arg_keys = jax.random.split(jax.random.key(seed), 10)
    tokens = bell_draw(arg_keys[0], (SEQS_ALL, LEN, D), 1.0, 6.0, ((0, 8), (1, 4)))
    segment_ids = draw_segment_ids(jax.random.fold_in(arg_keys[9], 71), 0)
    gain_attn = jnp.clip(1.0 + 0.1 * jax.random.normal(arg_keys[2], (D,), jnp.float32), 0.5, 1.5)
    query_key_value_weight = bell_draw(arg_keys[3], (3, D, HEADS * HD), (D // 2) ** -0.5, 0.25, ((2, 4),))
    output_weight = bell_draw(arg_keys[4], (HEADS * HD, D), (HEADS * HD // 64) ** -0.5, 1.5, ((0, 4),))
    gain_mlp = jnp.clip(1.0 + 0.1 * jax.random.normal(arg_keys[5], (D,), jnp.float32), 0.5, 1.5)
    gate_up_weight = bell_draw(arg_keys[6], (2, D, FF), D ** -0.5, 0.1875, ((2, 4),))
    down_weight = bell_draw(arg_keys[7], (FF, D), (FF // 4) ** -0.5, 0.25, ((0, 4),))
    cotangent = draw_cotangent(jax.random.fold_in(arg_keys[9], 71), 0)
    return {"tokens": tokens, "segment_ids": segment_ids, "gain_attn": gain_attn, "query_key_value_weight": query_key_value_weight, "output_weight": output_weight, "gain_mlp": gain_mlp, "gate_up_weight": gate_up_weight, "down_weight": down_weight, "cotangent": cotangent}


@jax.custom_vjp
def low(v):
    return lax.optimization_barrier(v.astype(jnp.bfloat16)).astype(jnp.float32)

@jax.custom_vjp
def low_back(v):
    return v

def low_keep(v):
    return (low(v), None)

def low_pass(kept, grad):
    return (grad,)

def back_keep(v):
    return (v, None)

def back_low(kept, grad):
    return (low(grad),)
low.defvjp(low_keep, low_pass)
low_back.defvjp(back_keep, back_low)
highest = lax.Precision.HIGHEST
epsilon = 1e-05
rope_base = 160000.0

def product(left, right):
    return jnp.dot(left, right, precision=highest)

def layer_norm(values, gain):
    centered = values - lax.optimization_barrier(jnp.mean(values, axis=-1, keepdims=True))
    variance = lax.optimization_barrier(jnp.mean(centered * centered, axis=-1, keepdims=True))
    return centered * lax.rsqrt(variance + epsilon) * gain

def rope_tables(segments):
    length = segments.shape[-1]
    before = lax.optimization_barrier(jnp.sum((segments[..., None, :] < segments[..., :, None]).astype(jnp.int32), axis=-1))
    positions = jnp.arange(length, dtype=jnp.int32) - before
    half_size = HD // 2
    inverse = jnp.exp(jnp.arange(half_size, dtype=jnp.float32) * (-2.0 * math.log(rope_base) / HD))
    angles = positions.astype(jnp.float32)[..., None] * inverse
    angles = jnp.concatenate([angles, angles], axis=-1)
    return (jnp.cos(angles), jnp.sin(angles))

def rotate_half(values):
    half_size = values.shape[-1] // 2
    return jnp.concatenate([-values[..., half_size:], values[..., :half_size]], axis=-1)

def apply_rope(values, cos_table, sin_table):
    return values * cos_table + rotate_half(values) * sin_table

def forward(tokens, segments, cos_table, sin_table, gain_attn, query_key_value_weight, output_weight, gain_mlp, gate_up_weight, down_weight):
    length = tokens.shape[0]
    normed_attn = low(layer_norm(tokens, gain_attn))

    def project(column):
        return low_back(product(normed_attn, query_key_value_weight[column])).reshape(length, HEADS, HD)
    cos_heads = cos_table[:, None, :]
    sin_heads = sin_table[:, None, :]
    queries = low(apply_rope(project(0), cos_heads, sin_heads))
    keys = low(apply_rope(project(1), cos_heads, sin_heads))
    values = low(project(2))
    same_doc = segments[:, None] == segments[None, :]
    scale_factor = 1.0 / math.sqrt(HD)

    def one_head(inputs):
        head_query, head_key, head_value = inputs
        scores = product(head_query, head_key.T) * scale_factor
        scores = low_back(jnp.where(same_doc, scores, -1000000000.0))
        largest = lax.optimization_barrier(jnp.max(scores, axis=-1, keepdims=True))
        weights = jnp.exp(scores - largest)
        probabilities = low(weights / lax.optimization_barrier(jnp.sum(weights, axis=-1, keepdims=True)))
        return product(probabilities, head_value)
    per_head = lax.map(jax.checkpoint(one_head), (jnp.swapaxes(queries, 0, 1), jnp.swapaxes(keys, 0, 1), jnp.swapaxes(values, 0, 1)))
    attention_result = jnp.swapaxes(per_head, 0, 1).reshape(length, HEADS * HD)
    attention_result = low(low_back(attention_result))
    branch = low_back(product(attention_result, output_weight))
    hidden_state = tokens + branch
    normed_mlp = low(layer_norm(hidden_state, gain_mlp))
    gate_proj = low_back(product(normed_mlp, gate_up_weight[0]))
    up_proj = low_back(product(normed_mlp, gate_up_weight[1]))
    activation_output = low(jax.nn.gelu(gate_proj, approximate=False) * up_proj)
    return hidden_state + low_back(product(activation_output, down_weight))

def reference(tokens, segment_ids, gain_attn, query_key_value_weight, output_weight, gain_mlp, gate_up_weight, down_weight, cotangent):
    params_f = (gain_attn.astype(jnp.float32), query_key_value_weight.astype(jnp.float32), output_weight.astype(jnp.float32), gain_mlp.astype(jnp.float32), gate_up_weight.astype(jnp.float32), down_weight.astype(jnp.float32))
    starting = tuple((jnp.zeros(weight.shape, jnp.float32) for weight in params_f))

    def one_sequence(totals, sliced):
        seq_tokens, seq_segments, seq_cot = sliced
        cos_table, sin_table = rope_tables(seq_segments)

        def closed(inputs, *params):
            return forward(inputs, seq_segments, cos_table, sin_table, *params)
        output, pullback = jax.vjp(closed, seq_tokens.astype(jnp.float32), *params_f)
        gradients = pullback(seq_cot.astype(jnp.float32))
        totals = tuple((total + grad for total, grad in zip(totals, gradients[1:])))
        return (totals, (output.astype(jnp.bfloat16), gradients[0].astype(jnp.bfloat16)))
    totals, outputs = lax.scan(one_sequence, starting, (tokens, segment_ids, cotangent))
    return (outputs[0], outputs[1], totals[0], totals[1], totals[2], totals[3], totals[4], totals[5])
```

```python
import math

import jax
import jax.numpy as jnp
from jax import lax
from jax.experimental import pallas as pl
from jax.experimental.pallas import tpu as pltpu
from jax.sharding import Mesh, PartitionSpec as P

HD = 64
EPSILON = 1e-05
ROPE_BASE = 160000.0
BF = jnp.bfloat16
F32 = jnp.float32


def normalize(values):
    centered = values - jnp.mean(values, axis=-1, keepdims=True)
    variance = jnp.mean(centered * centered, axis=-1, keepdims=True)
    inverse = lax.rsqrt(variance + EPSILON)
    return (centered * inverse, inverse)


def norm_back(grad, normal, inverse, gain):
    scaled = grad * gain
    return inverse * (
        scaled
        - jnp.mean(scaled, axis=-1, keepdims=True)
        - normal * jnp.mean(scaled * normal, axis=-1, keepdims=True)
    )


def nt(left, right):
    return lax.dot_general(left, right, (((1,), (1,)), ((), ())), preferred_element_type=F32)


def nn(left, right):
    return jnp.dot(left, right, preferred_element_type=F32)


def tn(left, right):
    return lax.dot_general(left, right, (((0,), (0,)), ((), ())), preferred_element_type=F32)


def swap_halves(values):
    lane = lax.broadcasted_iota(jnp.int32, values.shape, 1)
    width = values.shape[1]
    ahead = pltpu.roll(values, width - HD // 2, 1)
    behind = pltpu.roll(values, HD // 2, 1)
    return jnp.where(lane % HD < HD // 2, ahead, behind)


def project_kernel(n_ref, w_ref, cos_ref, sin_ref, q_ref, k_ref, v_ref):
    rows = n_ref[...]
    cos, sin = cos_ref[...], sin_ref[...]
    for c, out in ((0, q_ref), (1, k_ref), (2, v_ref)):
        wide = nn(rows, w_ref[c])
        if c == 2:
            out[...] = wide.astype(BF)
            continue
        for at in range(0, wide.shape[1], 128):
            part = wide[:, at : at + 128]
            turned = (part * cos + swap_halves(part) * sin).astype(BF)
            if c == 0:
                turned = turned * (1.0 / math.sqrt(HD))
            out[:, at : at + 128] = turned


def project(rows, weight, cos, sin):
    length, width = rows.shape
    cols = weight.shape[2]
    block = 256
    return pl.pallas_call(
        project_kernel,
        grid=(length // block,),
        in_specs=[
            pl.BlockSpec((block, width), lambda i: (i, 0)),
            pl.BlockSpec((3, width, cols), lambda i: (0, 0, 0)),
            pl.BlockSpec((block, 128), lambda i: (i, 0)),
            pl.BlockSpec((block, 128), lambda i: (i, 0)),
        ],
        out_specs=[pl.BlockSpec((block, cols), lambda i: (i, 0))] * 3,
        out_shape=[jax.ShapeDtypeStruct((length, cols), BF)] * 3,
        compiler_params=pltpu.CompilerParams(vmem_limit_bytes=40 * 2**20),
        cost_estimate=pl.CostEstimate(
            flops=6 * length * width * cols, bytes_accessed=5 * 2**20, transcendentals=0
        ),
    )(rows, weight, cos, sin)


def half_mask(values, half):
    lane = lax.broadcasted_iota(jnp.int32, values.shape, 1)
    return jnp.where((lane // HD) == half, values, jnp.zeros_like(values))


def row_blocks(count):
    at = 0
    while at < count:
        size = min(256, count - at)
        yield at, size
        at += size


def attend_kernel(doc, q_ref, k_ref, v_ref, o_ref, l_ref):
    keys = k_ref[:doc, :]
    values_t = v_ref[:doc, :].T
    for at, size in row_blocks(doc):
        queries = q_ref[at : at + size, :]
        mixed = []
        for half in range(2):
            scores = nt(keys, half_mask(queries, half))
            largest = jnp.max(scores, axis=0, keepdims=True)
            weights = jnp.exp(scores - largest)
            total = jnp.sum(weights, axis=0, keepdims=True)
            mix = nn(values_t[half * HD : half * HD + HD], weights.astype(BF))
            mixed.append(mix * (1.0 / total))
            l_ref[0, half : half + 1, at : at + size] = largest + jnp.log(total)
        o_ref[at : at + size, :] = jnp.concatenate(mixed, axis=0).T.astype(BF)
    o_ref[doc:, :] = v_ref[doc:, :]


def attend(queries, keys, values, doc):
    length, cols = queries.shape
    pairs = cols // 128
    spec = pl.BlockSpec((length, 128), lambda p: (0, p))
    return pl.pallas_call(
        lambda *refs: attend_kernel(doc, *refs),
        grid=(pairs,),
        in_specs=[spec] * 3,
        out_specs=[spec, pl.BlockSpec((1, 2, doc), lambda p: (p, 0, 0))],
        out_shape=[
            jax.ShapeDtypeStruct((length, cols), BF),
            jax.ShapeDtypeStruct((pairs, 2, doc), F32),
        ],
        compiler_params=pltpu.CompilerParams(vmem_limit_bytes=48 * 2**20),
        cost_estimate=pl.CostEstimate(
            flops=8 * doc * doc * cols, bytes_accessed=2 * 2**20, transcendentals=doc * doc * 4
        ),
    )(queries, keys, values)


def attend_back_kernel(
    doc, q_ref, k_ref, v_ref, d_ref, l_ref, cos_ref, sin_ref, dq_ref, dk_ref, dv_ref, ka_ref, va_ref
):
    keys = k_ref[:doc, :]
    keys_t = keys.T
    values = v_ref[:doc, :]
    first = True
    for at, size in row_blocks(doc):
        queries = q_ref[at : at + size, :]
        grads = d_ref[at : at + size, :]
        back = []
        for half in range(2):
            query = half_mask(queries, half)
            grad = half_mask(grads, half)
            probs = jnp.exp(nt(keys, query) - l_ref[0, half : half + 1, at : at + size])
            prob_grad = nt(values, grad)
            centre = jnp.sum(probs * prob_grad, axis=0, keepdims=True)
            score_grad = (probs * (prob_grad - centre)).astype(BF)
            value_part = nn(probs.astype(BF), grad)
            key_part = nn(score_grad, query)
            if first:
                va_ref[...] = value_part
                ka_ref[...] = key_part
                first = False
            else:
                va_ref[...] += value_part
                ka_ref[...] += key_part
            back.append(nn(keys_t[half * HD : half * HD + HD], score_grad))
        query_grad = jnp.concatenate(back, axis=0).T * (1.0 / math.sqrt(HD))
        cos = cos_ref[at : at + size, :]
        sin = sin_ref[at : at + size, :]
        dq_ref[at : at + size, :] = (query_grad * cos - swap_halves(query_grad) * sin).astype(BF)
    key_grad = ka_ref[...]
    cos = cos_ref[:doc, :]
    sin = sin_ref[:doc, :]
    dk_ref[:doc, :] = (key_grad * cos - swap_halves(key_grad) * sin).astype(BF)
    dv_ref[:doc, :] = va_ref[...].astype(BF)
    rest = dq_ref.shape[0] - doc
    dq_ref[doc:, :] = jnp.zeros((rest, 128), BF)
    dk_ref[doc:, :] = jnp.zeros((rest, 128), BF)
    dv_ref[doc:, :] = d_ref[doc:, :]


def attend_back(queries, keys, values, grads, logs, cos, sin, doc):
    length, cols = queries.shape
    pairs = cols // 128
    spec = pl.BlockSpec((length, 128), lambda p: (0, p))
    table = pl.BlockSpec((length, 128), lambda p: (0, 0))
    return pl.pallas_call(
        lambda *refs: attend_back_kernel(doc, *refs),
        grid=(pairs,),
        in_specs=[spec] * 4
        + [pl.BlockSpec((1, 2, doc), lambda p: (p, 0, 0))]
        + [table] * 2,
        out_specs=[spec] * 3,
        out_shape=[jax.ShapeDtypeStruct((length, cols), BF)] * 3,
        scratch_shapes=[pltpu.VMEM((doc, 128), F32), pltpu.VMEM((doc, 128), F32)],
        compiler_params=pltpu.CompilerParams(vmem_limit_bytes=48 * 2**20),
        cost_estimate=pl.CostEstimate(
            flops=20 * doc * doc * cols, bytes_accessed=5 * 2**20, transcendentals=doc * doc * 4
        ),
    )(queries, keys, values, grads, logs, cos, sin)


def shift(value, by, count):
    return lax.ppermute(value, "tensor", [(i, (i + by) % count) for i in range(count)])


def flip(value, axis, bit, count):
    return lax.ppermute(value, axis, [(i, i ^ bit) for i in range(count)])


def bits_of(count, turned):
    bits = [1 << b for b in range(count.bit_length() - 1)]
    return bits[::-1] if turned else bits


def gather_chips(value, count, turned):
    held = {0: value}
    for bit in bits_of(count, turned):
        held.update({i ^ bit: flip(v, "chip", bit, count) for i, v in list(held.items())})
    return [held[i] for i in range(count)]


def scatter_chips(blocks, count, turned):
    held = dict(enumerate(blocks))
    for bit in bits_of(count, turned):
        held = {
            i: (v.astype(F32) + flip(held[i ^ bit], "chip", bit, count).astype(F32)).astype(BF)
            for i, v in held.items()
            if not i & bit
        }
    return held[0]


def total_all(value, sizes):
    for axis, count in sizes:
        for bit in bits_of(count, False):
            value = value + flip(value, axis, bit, count)
    return value


def rotate(value, by):
    length = value.shape[0]
    return lax.dynamic_slice_in_dim(jnp.concatenate([value, value]), by, length)


def make(chips, cores, ranks):
    def on_device(
        tokens,
        segment_ids,
        gain_attn,
        query_key_value_weight,
        output_weight,
        gain_mlp,
        gate_up_weight,
        down_weight,
        cotangent,
    ):
        length = segment_ids.shape[1]
        own_rows, width = tokens.shape[1:]
        doc = length - length // 8
        rank = lax.axis_index("tensor")
        core = lax.axis_index("core")
        chip = lax.axis_index("chip")
        segments = segment_ids[0]
        middle = segments[length // 2]
        start = jnp.sum((segments < middle).astype(jnp.int32))
        mine_at = rank * own_rows
        into_doc = (start - mine_at) % length
        from_doc = (mine_at - start) % length

        places = jnp.arange(length, dtype=jnp.int32)
        places = jnp.where(places < doc, places, 0)
        half = HD // 2
        freq = jnp.exp(jnp.arange(half, dtype=F32) * (-2.0 * math.log(ROPE_BASE) / HD))
        angles = places.astype(F32)[:, None] * jnp.concatenate([freq] * 4)[None, :]
        cos_table = jnp.cos(angles)
        lane = jnp.arange(2 * HD, dtype=jnp.int32)
        sin_table = jnp.sin(angles) * jnp.where(lane % HD < half, -1.0, 1.0)

        hidden = down_weight.shape[0]
        share = hidden // cores
        per = -(-share // chips)
        piece = -(-per // 8) * 8
        hidden_t = jnp.concatenate([jnp.swapaxes(gate_up_weight, 1, 2), down_weight[None]])
        half_t = lax.dynamic_slice_in_dim(hidden_t, core * share, share, axis=1)
        half_t = jnp.pad(half_t, ((0, 0), (0, chips * per - share), (0, 0)))
        half_t = half_t.reshape(3, chips, per, width)
        half_t = jnp.pad(half_t, ((0, 0), (0, 0), (0, piece - per), (0, 0)))
        own = [
            lax.dynamic_index_in_dim(half_t, chip ^ i, axis=1, keepdims=False)
            for i in range(chips)
        ]
        gate_up_sent = own[0][:2]
        down_sent = own[0][2]
        gate_up_came = [shift(gate_up_sent, -k, ranks) for k in range(1, ranks)]
        down_came = jnp.concatenate([shift(down_sent, -k, ranks) for k in range(1, ranks)])
        gates = gather_chips(jnp.concatenate([g[0] for g in gate_up_came]), chips, False)
        ups = gather_chips(jnp.concatenate([g[1] for g in gate_up_came]), chips, True)
        cut = down_came.shape[0] // 16 * 8
        downs_a = gather_chips(down_came[:cut], chips, False)
        downs_b = gather_chips(down_came[cut:], chips, True)
        gate = jnp.concatenate([v for i in range(chips) for v in (own[i][0], gates[i])])
        up = jnp.concatenate([v for i in range(chips) for v in (own[i][1], ups[i])])
        down = jnp.concatenate(
            [v for i in range(chips) for v in (own[i][2], downs_a[i], downs_b[i])]
        )
        heads_rows = output_weight.shape[0]
        out_piece = heads_rows // (cores * chips)
        out_mine = lax.dynamic_slice_in_dim(
            output_weight, (core * chips + chip) * out_piece, out_piece
        )
        out_all = lax.all_gather(out_mine, ("tensor", "core", "chip"), axis=0, tiled=True)
        out_all = out_all.reshape(ranks, heads_rows, width)
        outs = [
            lax.dynamic_index_in_dim(out_all, (rank - k) % ranks, axis=0, keepdims=False)
            for k in range(ranks)
        ]
        out_weight = jnp.concatenate(outs)

        token_f = tokens[0].astype(F32)
        cot = cotangent[0]
        cot_pair = jnp.concatenate([cot, flip(cot, "core", 1, cores)])
        normal_attn, inverse_attn = normalize(token_f)
        normed_attn = (normal_attn * gain_attn).astype(BF)
        normed_rows = jnp.concatenate(
            [normed_attn] + [shift(normed_attn, -k, ranks) for k in range(1, ranks)]
        )
        normed_doc = rotate(normed_rows, into_doc)
        queries, keys, values = project(normed_doc, query_key_value_weight, cos_table, sin_table)
        mixture, logs = attend(queries, keys, values, doc)
        mixture = rotate(mixture, from_doc).reshape(ranks, own_rows, heads_rows)
        attention = jnp.concatenate(
            [mixture[0]] + [shift(mixture[k], k, ranks) for k in range(1, ranks)], axis=1
        )
        hidden_state = token_f + nn(attention, out_weight)
        normal_mlp, inverse_mlp = normalize(hidden_state)
        normed_mlp = (normal_mlp * gain_mlp).astype(BF)

        normed_pair = jnp.concatenate([normed_mlp, flip(normed_mlp, "core", 1, cores)])
        gate_proj = nt(normed_pair, gate)
        up_proj = nt(normed_pair, up)
        hid_grad = nt(cot_pair, down)
        cdf = 0.5 * (1.0 + lax.erf(gate_proj * (1.0 / math.sqrt(2.0))))
        pdf = jnp.exp(-0.5 * gate_proj * gate_proj) * (1.0 / math.sqrt(2.0 * math.pi))
        act = gate_proj * cdf
        hid = (act * up_proj).astype(BF)
        gate_grad = (hid_grad * up_proj * (cdf + gate_proj * pdf)).astype(BF)
        up_grad = (hid_grad * act).astype(BF)
        in_part = nn(gate_grad, gate) + nn(up_grad, up)
        normed_mlp_grad = in_part[:own_rows] + flip(
            in_part[own_rows:].astype(BF), "core", 1, cores
        ).astype(F32)
        down_grad = tn(hid, cot_pair).astype(BF)
        gate_w_grad = tn(gate_grad, normed_pair).astype(BF)
        up_w_grad = tn(up_grad, normed_pair).astype(BF)
        mlp_part = nn(hid, down)
        mlp_out = mlp_part[:own_rows] + flip(
            mlp_part[own_rows:].astype(BF), "core", 1, cores
        ).astype(F32)
        layer_out = (hidden_state + mlp_out).astype(BF)

        gain_mlp_part = jnp.sum(normed_mlp_grad * normal_mlp, axis=0)
        hidden_grad = cot.astype(F32) + norm_back(
            normed_mlp_grad, normal_mlp, inverse_mlp, gain_mlp
        )
        branch_grad = hidden_grad.astype(BF)
        attended_grad = nt(branch_grad, out_weight).astype(BF)
        attended_rows = jnp.concatenate(
            [attended_grad[:, :heads_rows]]
            + [
                shift(attended_grad[:, k * heads_rows : (k + 1) * heads_rows], -k, ranks)
                for k in range(1, ranks)
            ]
        )
        attended_doc = rotate(attended_rows, into_doc)
        out_w_grad = tn(attention, branch_grad).astype(BF)
        dq, dk, dv = attend_back(
            queries, keys, values, attended_doc, logs, cos_table, sin_table, doc
        )
        normed_attn_part = (
            nt(dq, query_key_value_weight[0])
            + nt(dk, query_key_value_weight[1])
            + nt(dv, query_key_value_weight[2])
        )
        gain_attn_part = jnp.sum(normed_attn_part * normed_doc.astype(F32), axis=0) / gain_attn
        part_rows = rotate(normed_attn_part.astype(BF), from_doc).reshape(ranks, own_rows, width)
        normed_attn_grad = part_rows[0].astype(F32)
        for k in range(1, ranks):
            normed_attn_grad = normed_attn_grad + shift(part_rows[k], k, ranks).astype(F32)
        input_grad = (
            hidden_grad + norm_back(normed_attn_grad, normal_attn, inverse_attn, gain_attn)
        ).astype(BF)
        gains = total_all(
            jnp.concatenate([gain_attn_part, gain_mlp_part]),
            (("core", cores), ("chip", chips), ("tensor", ranks)),
        )
        grad_gain_attn, grad_gain_mlp = gains[:width], gains[width:]

        def scatter_hidden(grad, turned):
            blocks = grad.reshape(chips, ranks * piece, width)
            here = scatter_chips([blocks[i] for i in range(chips)], chips, turned)
            here = here.reshape(ranks, piece, width)
            total = here[0].astype(F32)
            for k in range(1, ranks):
                total = total + shift(here[k], k, ranks).astype(F32)
            return total.astype(BF)

        pieces = jnp.stack(
            [
                scatter_hidden(gate_w_grad, False),
                scatter_hidden(up_w_grad, True),
                scatter_hidden(down_grad, False),
            ]
        )
        every = lax.all_gather(pieces, ("core", "chip"), axis=0, tiled=False)
        every = every[:, :, :per].reshape(cores, chips, 3, per, width)
        every = jnp.moveaxis(every, 2, 0).reshape(3, cores, chips * per, width)[:, :, :share]
        every = every.reshape(3, hidden, width).astype(F32)
        grad_gateup = jnp.swapaxes(every[:2], 1, 2)
        down_weight_gradient = every[2]

        back_order = [(ranks - k) % ranks for k in range(ranks)]
        out_blocks = out_w_grad.reshape(ranks, heads_rows, width)
        out_blocks = jnp.concatenate([out_blocks[k] for k in back_order])
        out_blocks = rotate(out_blocks, ((ranks - rank) % ranks) * heads_rows)
        out_here = lax.psum_scatter(
            out_blocks, ("tensor", "core", "chip"), scatter_dimension=0, tiled=True
        )
        output_weight_gradient = lax.all_gather(
            out_here, ("core", "chip"), axis=0, tiled=True
        ).astype(F32)

        qkv_grad = jnp.stack([tn(normed_doc, g) for g in (dq, dk, dv)]).astype(BF)
        qkv_here = lax.psum_scatter(qkv_grad, ("core", "chip"), scatter_dimension=1, tiled=True)
        query_key_value_gradient = lax.all_gather(
            qkv_here, ("core", "chip"), axis=1, tiled=True
        ).astype(F32)
        return (
            layer_out[None],
            input_grad[None],
            grad_gain_attn,
            query_key_value_gradient,
            output_weight_gradient,
            grad_gain_mlp,
            grad_gateup,
            down_weight_gradient,
        )

    return on_device


def solution(mesh):
    ranks = mesh.shape["tensor"]
    cores = 2
    chips = mesh.shape["dp"] // cores
    split = Mesh(mesh.devices.reshape(chips, cores, ranks), ("chip", "core", "tensor"))
    dp = ("chip", "core")
    rows = P(dp, "tensor", None)
    last = P(None, None, "tensor")
    first = P("tensor", None)
    return jax.shard_map(
        make(chips, cores, ranks),
        mesh=split,
        in_specs=(rows, P(dp, None), P(), last, first, P(), last, first, rows),
        out_specs=(rows, rows, P(), last, first, P(), last, first),
        check_vma=False,
    )
```

```python
import math

import jax
import jax.numpy as jnp
from jax import lax
from jax.experimental import pallas as pl
from jax.experimental.pallas import tpu as pltpu
from jax.sharding import Mesh, PartitionSpec as P

HD = 64
EPSILON = 1e-05
ROPE_BASE = 160000.0
BF = jnp.bfloat16
F32 = jnp.float32


def normalize(values):
    centered = values - jnp.mean(values, axis=-1, keepdims=True)
    variance = jnp.mean(centered * centered, axis=-1, keepdims=True)
    inverse = lax.rsqrt(variance + EPSILON)
    return (centered * inverse, inverse)


def norm_back(grad, normal, inverse, gain):
    scaled = grad * gain
    return inverse * (
        scaled
        - jnp.mean(scaled, axis=-1, keepdims=True)
        - normal * jnp.mean(scaled * normal, axis=-1, keepdims=True)
    )


def nt(left, right):
    return lax.dot_general(left, right, (((1,), (1,)), ((), ())), preferred_element_type=F32)


def nn(left, right):
    return jnp.dot(left, right, preferred_element_type=F32)


def tn(left, right):
    return lax.dot_general(left, right, (((0,), (0,)), ((), ())), preferred_element_type=F32)


def swap_halves(values):
    lane = lax.broadcasted_iota(jnp.int32, values.shape, 1)
    width = values.shape[1]
    ahead = pltpu.roll(values, width - HD // 2, 1)
    behind = pltpu.roll(values, HD // 2, 1)
    return jnp.where(lane % HD < HD // 2, ahead, behind)


def project_kernel(n_ref, w_ref, cos_ref, sin_ref, q_ref, k_ref, v_ref):
    rows = n_ref[...]
    cos, sin = cos_ref[...], sin_ref[...]
    for c, out in ((0, q_ref), (1, k_ref), (2, v_ref)):
        wide = nn(rows, w_ref[c])
        if c == 2:
            out[...] = wide.astype(BF)
            continue
        for at in range(0, wide.shape[1], 128):
            part = wide[:, at : at + 128]
            turned = (part * cos + swap_halves(part) * sin).astype(BF)
            if c == 0:
                turned = turned * (1.0 / math.sqrt(HD))
            out[:, at : at + 128] = turned


def project(rows, weight, cos, sin):
    length, width = rows.shape
    cols = weight.shape[2]
    block = 256
    return pl.pallas_call(
        project_kernel,
        grid=(length // block,),
        in_specs=[
            pl.BlockSpec((block, width), lambda i: (i, 0)),
            pl.BlockSpec((3, width, cols), lambda i: (0, 0, 0)),
            pl.BlockSpec((block, 128), lambda i: (i, 0)),
            pl.BlockSpec((block, 128), lambda i: (i, 0)),
        ],
        out_specs=[pl.BlockSpec((block, cols), lambda i: (i, 0))] * 3,
        out_shape=[jax.ShapeDtypeStruct((length, cols), BF)] * 3,
        compiler_params=pltpu.CompilerParams(vmem_limit_bytes=40 * 2**20),
        cost_estimate=pl.CostEstimate(
            flops=6 * length * width * cols, bytes_accessed=5 * 2**20, transcendentals=0
        ),
    )(rows, weight, cos, sin)


def half_mask(values, half):
    lane = lax.broadcasted_iota(jnp.int32, values.shape, 1)
    return jnp.where((lane // HD) == half, values, jnp.zeros_like(values))


def row_blocks(count):
    at = 0
    while at < count:
        size = min(256, count - at)
        yield at, size
        at += size


def attend_kernel(doc, q_ref, k_ref, v_ref, o_ref, l_ref):
    keys = k_ref[:doc, :]
    values_t = v_ref[:doc, :].T
    for at, size in row_blocks(doc):
        queries = q_ref[at : at + size, :]
        mixed = []
        for half in range(2):
            scores = nt(keys, half_mask(queries, half))
            largest = jnp.max(scores, axis=0, keepdims=True)
            weights = jnp.exp(scores - largest)
            total = jnp.sum(weights, axis=0, keepdims=True)
            mix = nn(values_t[half * HD : half * HD + HD], weights.astype(BF))
            mixed.append(mix * (1.0 / total))
            l_ref[0, half : half + 1, at : at + size] = largest + jnp.log(total)
        o_ref[at : at + size, :] = jnp.concatenate(mixed, axis=0).T.astype(BF)
    o_ref[doc:, :] = v_ref[doc:, :]


def attend(queries, keys, values, doc):
    length, cols = queries.shape
    pairs = cols // 128
    spec = pl.BlockSpec((length, 128), lambda p: (0, p))
    return pl.pallas_call(
        lambda *refs: attend_kernel(doc, *refs),
        grid=(pairs,),
        in_specs=[spec] * 3,
        out_specs=[spec, pl.BlockSpec((1, 2, doc), lambda p: (p, 0, 0))],
        out_shape=[
            jax.ShapeDtypeStruct((length, cols), BF),
            jax.ShapeDtypeStruct((pairs, 2, doc), F32),
        ],
        compiler_params=pltpu.CompilerParams(vmem_limit_bytes=48 * 2**20),
        cost_estimate=pl.CostEstimate(
            flops=8 * doc * doc * cols, bytes_accessed=2 * 2**20, transcendentals=doc * doc * 4
        ),
    )(queries, keys, values)


def attend_back_kernel(
    doc, q_ref, k_ref, v_ref, d_ref, l_ref, cos_ref, sin_ref, dq_ref, dk_ref, dv_ref, ka_ref, va_ref
):
    keys = k_ref[:doc, :]
    keys_t = keys.T
    values = v_ref[:doc, :]
    first = True
    for at, size in row_blocks(doc):
        queries = q_ref[at : at + size, :]
        grads = d_ref[at : at + size, :]
        back = []
        for half in range(2):
            query = half_mask(queries, half)
            grad = half_mask(grads, half)
            probs = jnp.exp(nt(keys, query) - l_ref[0, half : half + 1, at : at + size])
            prob_grad = nt(values, grad)
            centre = jnp.sum(probs * prob_grad, axis=0, keepdims=True)
            score_grad = (probs * (prob_grad - centre)).astype(BF)
            value_part = nn(probs.astype(BF), grad)
            key_part = nn(score_grad, query)
            if first:
                va_ref[...] = value_part
                ka_ref[...] = key_part
                first = False
            else:
                va_ref[...] += value_part
                ka_ref[...] += key_part
            back.append(nn(keys_t[half * HD : half * HD + HD], score_grad))
        query_grad = jnp.concatenate(back, axis=0).T * (1.0 / math.sqrt(HD))
        cos = cos_ref[at : at + size, :]
        sin = sin_ref[at : at + size, :]
        dq_ref[at : at + size, :] = (query_grad * cos - swap_halves(query_grad) * sin).astype(BF)
    key_grad = ka_ref[...]
    cos = cos_ref[:doc, :]
    sin = sin_ref[:doc, :]
    dk_ref[:doc, :] = (key_grad * cos - swap_halves(key_grad) * sin).astype(BF)
    dv_ref[:doc, :] = va_ref[...].astype(BF)
    rest = dq_ref.shape[0] - doc
    dq_ref[doc:, :] = jnp.zeros((rest, 128), BF)
    dk_ref[doc:, :] = jnp.zeros((rest, 128), BF)
    dv_ref[doc:, :] = d_ref[doc:, :]


def attend_back(queries, keys, values, grads, logs, cos, sin, doc):
    length, cols = queries.shape
    pairs = cols // 128
    spec = pl.BlockSpec((length, 128), lambda p: (0, p))
    table = pl.BlockSpec((length, 128), lambda p: (0, 0))
    return pl.pallas_call(
        lambda *refs: attend_back_kernel(doc, *refs),
        grid=(pairs,),
        in_specs=[spec] * 4
        + [pl.BlockSpec((1, 2, doc), lambda p: (p, 0, 0))]
        + [table] * 2,
        out_specs=[spec] * 3,
        out_shape=[jax.ShapeDtypeStruct((length, cols), BF)] * 3,
        scratch_shapes=[pltpu.VMEM((doc, 128), F32), pltpu.VMEM((doc, 128), F32)],
        compiler_params=pltpu.CompilerParams(vmem_limit_bytes=48 * 2**20),
        cost_estimate=pl.CostEstimate(
            flops=20 * doc * doc * cols, bytes_accessed=5 * 2**20, transcendentals=doc * doc * 4
        ),
    )(queries, keys, values, grads, logs, cos, sin)


def assemble_kernel(cores, chips, share, per, piece, out_piece, in_ref, gu_ref, d_ref, held):
    hidden = cores * share
    for m, first in ((0, 0), (1, piece), (2, 2 * piece + out_piece)):
        for c in range(cores):
            for j in range(chips):
                at = c * share + j * per
                rows = in_ref[c * chips + j].astype(F32)
                held[at : at + piece, :] = rows[first : first + piece, :]
        if m == 2:
            d_ref[...] = held[:hidden, :]
        else:
            gu_ref[m] = held[...].T[:, :hidden]


def assemble(every, cores, chips, share, per, piece, out_piece):
    devices, rows, width = every.shape
    hidden = cores * share
    block = 256
    tall = -(-((cores - 1) * share + (chips - 1) * per + piece) // 128) * 128
    return pl.pallas_call(
        lambda *refs: assemble_kernel(cores, chips, share, per, piece, out_piece, *refs),
        grid=(width // block,),
        in_specs=[pl.BlockSpec((devices, rows, block), lambda i: (0, 0, i))],
        out_specs=[
            pl.BlockSpec((2, block, hidden), lambda i: (0, i, 0)),
            pl.BlockSpec((hidden, block), lambda i: (0, i)),
        ],
        out_shape=[
            jax.ShapeDtypeStruct((2, width, hidden), F32),
            jax.ShapeDtypeStruct((hidden, width), F32),
        ],
        scratch_shapes=[pltpu.VMEM((tall, block), F32)],
        compiler_params=pltpu.CompilerParams(vmem_limit_bytes=40 * 2**20),
        cost_estimate=pl.CostEstimate(flops=0, bytes_accessed=12 * 2**20, transcendentals=0),
    )(every)


def shift(value, by, count):
    return lax.ppermute(value, "tensor", [(i, (i + by) % count) for i in range(count)])


def flip(value, axis, bit, count):
    return lax.ppermute(value, axis, [(i, i ^ bit) for i in range(count)])


def bits_of(count, turned):
    bits = [1 << b for b in range(count.bit_length() - 1)]
    return bits[::-1] if turned else bits


def halving(value, chip, count, turned):
    bits = count.bit_length() - 1
    held = value.reshape((2,) * bits + (-1,) + value.shape[-1:])
    order = list(range(bits))
    if not turned:
        order = order[::-1]
    left = list(range(bits))
    for axis in order:
        bit = bits - 1 - axis
        mine = (chip >> bit) & 1
        at = left.index(axis)
        left.remove(axis)
        kept = lax.dynamic_index_in_dim(held, mine, at, keepdims=False)
        sent = lax.dynamic_index_in_dim(held, 1 - mine, at, keepdims=False)
        came = flip(sent, "chip", 1 << bit, count)
        tied = yield came
        came = came if tied is None else tied
        held = (kept.astype(F32) + came.astype(F32)).astype(BF)
    yield held


def finish(steps, tied):
    last = next(steps) if tied is None else steps.send(tied)
    for value in steps:
        last = value
    return last


def total_all(value, sizes):
    for axis, count in sizes:
        for bit in bits_of(count, False):
            value = value + flip(value, axis, bit, count)
    return value


def rotate(value, by):
    length = value.shape[0]
    return lax.dynamic_slice_in_dim(jnp.concatenate([value, value]), by, length)


def make(chips, cores, ranks):
    def on_device(
        tokens,
        segment_ids,
        gain_attn,
        query_key_value_weight,
        output_weight,
        gain_mlp,
        gate_up_weight,
        down_weight,
        cotangent,
    ):
        length = segment_ids.shape[1]
        own_rows, width = tokens.shape[1:]
        doc = length - length // 8
        rank = lax.axis_index("tensor")
        core = lax.axis_index("core")
        chip = lax.axis_index("chip")
        segments = segment_ids[0]
        middle = segments[length // 2]
        start = jnp.sum((segments < middle).astype(jnp.int32))
        mine_at = rank * own_rows
        into_doc = (start - mine_at) % length
        from_doc = (mine_at - start) % length

        places = jnp.arange(length, dtype=jnp.int32)
        places = jnp.where(places < doc, places, 0)
        half = HD // 2
        freq = jnp.exp(jnp.arange(half, dtype=F32) * (-2.0 * math.log(ROPE_BASE) / HD))
        angles = places.astype(F32)[:, None] * jnp.concatenate([freq] * 4)[None, :]
        cos_table = jnp.cos(angles)
        lane = jnp.arange(2 * HD, dtype=jnp.int32)
        sin_table = jnp.sin(angles) * jnp.where(lane % HD < half, -1.0, 1.0)

        hidden = down_weight.shape[0]
        share = hidden // cores
        per = -(-share // chips)
        piece = -(-per // 8) * 8
        heads_rows = output_weight.shape[0]
        out_piece = heads_rows // (cores * chips)
        hidden_t = jnp.concatenate([jnp.swapaxes(gate_up_weight, 1, 2), down_weight[None]])
        half_t = lax.dynamic_slice_in_dim(hidden_t, core * share, share, axis=1)
        half_t = jnp.pad(half_t, ((0, 0), (0, chips * per - share), (0, 0)))
        half_t = half_t.reshape(3, chips, per, width)
        half_t = jnp.pad(half_t, ((0, 0), (0, 0), (0, piece - per), (0, 0)))
        mine = lax.dynamic_index_in_dim(half_t, chip, axis=1, keepdims=False)
        out_mine = lax.dynamic_slice_in_dim(
            output_weight, (core * chips + chip) * out_piece, out_piece
        )
        gate_up_mine = mine[:2].reshape(2 * piece, width)
        down_out_mine = jnp.concatenate([mine[2], out_mine])
        gate_up_came = [shift(gate_up_mine, -k, ranks) for k in range(1, ranks)]

        token_f = tokens[0].astype(F32)
        normal_attn, inverse_attn = normalize(token_f)
        normed_attn = (normal_attn * gain_attn).astype(BF)
        normed_sent, *gate_up_came = lax.optimization_barrier((normed_attn, *gate_up_came))
        normed_came = [shift(normed_sent, -k, ranks) for k in range(1, ranks)]
        down_out_sent, *normed_came = lax.optimization_barrier((down_out_mine, *normed_came))
        down_out_came = [shift(down_out_sent, -k, ranks) for k in range(1, ranks)]
        others = ranks - 1
        gate_up_all = lax.all_gather(jnp.concatenate(gate_up_came), "chip")
        gate_up_all = gate_up_all.reshape(chips, others, 2, piece, width)
        down_out_all = lax.all_gather(jnp.concatenate(down_out_came), "chip")
        down_out_all = down_out_all.reshape(chips, others, piece + out_piece, width)

        def whole(own, rest):
            joined = jnp.concatenate([own[:, None], rest], axis=1)
            return joined.reshape(chips * ranks * piece, width)

        gate = whole(half_t[0], gate_up_all[:, :, 0])
        up = whole(half_t[1], gate_up_all[:, :, 1])
        down = whole(half_t[2], down_out_all[:, :, :piece])
        out_half = jnp.swapaxes(down_out_all[:, :, piece:], 0, 1)
        out_half = out_half.reshape(others, heads_rows // cores, width)
        out_other = flip(out_half, "core", 1, cores)
        out_rest = jnp.concatenate(
            [
                jnp.where(core == 0, out_half, out_other),
                jnp.where(core == 0, out_other, out_half),
            ],
            axis=1,
        )
        out_weight = jnp.concatenate(
            [output_weight] + [out_rest[ranks - 1 - k] for k in range(1, ranks)]
        )

        cot = cotangent[0]
        cot_pair = jnp.concatenate([cot, flip(cot, "core", 1, cores)])
        normed_rows = jnp.concatenate([normed_attn] + normed_came)
        normed_doc = rotate(normed_rows, into_doc)
        queries, keys, values = project(normed_doc, query_key_value_weight, cos_table, sin_table)
        mixture, logs = attend(queries, keys, values, doc)
        mixture = rotate(mixture, from_doc).reshape(ranks, own_rows, heads_rows)
        attention = jnp.concatenate(
            [mixture[0]] + [shift(mixture[k], k, ranks) for k in range(1, ranks)], axis=1
        )
        hidden_state = token_f + nn(attention, out_weight)
        normal_mlp, inverse_mlp = normalize(hidden_state)
        normed_mlp = (normal_mlp * gain_mlp).astype(BF)

        normed_pair = jnp.concatenate([normed_mlp, flip(normed_mlp, "core", 1, cores)])
        gate_proj = nt(normed_pair, gate)
        up_proj = nt(normed_pair, up)
        hid_grad = nt(cot_pair, down)
        cdf = 0.5 * (1.0 + lax.erf(gate_proj * (1.0 / math.sqrt(2.0))))
        pdf = jnp.exp(-0.5 * gate_proj * gate_proj) * (1.0 / math.sqrt(2.0 * math.pi))
        act = gate_proj * cdf
        hid = (act * up_proj).astype(BF)
        gate_grad = (hid_grad * up_proj * (cdf + gate_proj * pdf)).astype(BF)
        up_grad = (hid_grad * act).astype(BF)
        in_part = nn(gate_grad, gate) + nn(up_grad, up)
        down_grad = tn(hid, cot_pair).astype(BF)
        gate_w_grad = tn(gate_grad, normed_pair).astype(BF)
        up_w_grad = tn(up_grad, normed_pair).astype(BF)
        down_sum = halving(down_grad, chip, chips, False)
        next(down_sum)
        in_part, gate_w_grad, up_w_grad = lax.optimization_barrier(
            (in_part, gate_w_grad, up_w_grad)
        )
        gate_sum = halving(gate_w_grad, chip, chips, False)
        up_sum = halving(up_w_grad, chip, chips, True)
        came = [next(gate_sum), next(up_sum)]
        normed_mlp_grad = in_part[:own_rows] + flip(
            in_part[own_rows:].astype(BF), "core", 1, cores
        ).astype(F32)
        mlp_part = nn(hid, down)
        mlp_out = mlp_part[:own_rows] + flip(
            mlp_part[own_rows:].astype(BF), "core", 1, cores
        ).astype(F32)
        layer_out = (hidden_state + mlp_out).astype(BF)

        gain_mlp_part = jnp.sum(normed_mlp_grad * normal_mlp, axis=0)
        hidden_grad = cot.astype(F32) + norm_back(
            normed_mlp_grad, normal_mlp, inverse_mlp, gain_mlp
        )
        branch_grad = hidden_grad.astype(BF)
        attended_grad = nt(branch_grad, out_weight).astype(BF)
        attended_rows = jnp.concatenate(
            [attended_grad[:, :heads_rows]]
            + [
                shift(attended_grad[:, k * heads_rows : (k + 1) * heads_rows], -k, ranks)
                for k in range(1, ranks)
            ]
        )
        attended_doc = rotate(attended_rows, into_doc)
        out_w_grad = tn(attention, branch_grad).astype(BF)
        attended_doc, *came = lax.optimization_barrier((attended_doc, *came))
        gate_here = finish(gate_sum, came[0])
        up_here = finish(up_sum, came[1])
        down_here = finish(down_sum, None)
        dq, dk, dv = attend_back(
            queries, keys, values, attended_doc, logs, cos_table, sin_table, doc
        )
        normed_attn_part = (
            nt(dq, query_key_value_weight[0])
            + nt(dk, query_key_value_weight[1])
            + nt(dv, query_key_value_weight[2])
        )
        gain_attn_part = jnp.sum(normed_attn_part * normed_doc.astype(F32), axis=0) / gain_attn
        part_rows = rotate(normed_attn_part.astype(BF), from_doc).reshape(ranks, own_rows, width)
        normed_attn_grad = part_rows[0].astype(F32)
        for k in range(1, ranks):
            normed_attn_grad = normed_attn_grad + shift(part_rows[k], k, ranks).astype(F32)
        input_grad = (
            hidden_grad + norm_back(normed_attn_grad, normal_attn, inverse_attn, gain_attn)
        ).astype(BF)
        gains = total_all(
            jnp.concatenate([gain_attn_part, gain_mlp_part]),
            (("core", cores), ("chip", chips), ("tensor", ranks)),
        )
        grad_gain_attn, grad_gain_mlp = gains[:width], gains[width:]

        def sum_ranks(here):
            total = here[0].astype(F32)
            for k in range(1, ranks):
                total = total + shift(here[k], k, ranks).astype(F32)
            return total.astype(BF)

        def sum_cores(value, axis):
            kept = lax.dynamic_index_in_dim(value, core, axis, keepdims=False)
            sent = lax.dynamic_index_in_dim(value, 1 - core, axis, keepdims=False)
            return (kept.astype(F32) + flip(sent, "core", 1, cores).astype(F32)).astype(BF)

        out_blocks = out_w_grad.reshape(ranks, cores, chips, out_piece, width)
        out_blocks = jnp.stack([out_blocks[(ranks - k) % ranks] for k in range(ranks)])
        out_blocks = jnp.swapaxes(sum_cores(out_blocks, 1), 0, 1)
        out_here = finish(halving(out_blocks, chip, chips, True), None)
        down_total = sum_ranks(down_here.reshape(ranks, piece, width))
        rest_total = sum_ranks(
            jnp.concatenate(
                [
                    gate_here.reshape(ranks, piece, width),
                    up_here.reshape(ranks, piece, width),
                    out_here.reshape(ranks, out_piece, width),
                ],
                axis=1,
            )
        )
        qkv_grad = jnp.stack([tn(normed_doc, g) for g in (dq, dk, dv)]).astype(BF)
        qkv_rows = width // (cores * chips)
        qkv_blocks = qkv_grad.reshape(3, cores, chips, qkv_rows, heads_rows)
        qkv_blocks = jnp.swapaxes(sum_cores(qkv_blocks, 1), 0, 1)
        qkv_here = finish(halving(qkv_blocks, chip, chips, False), None)
        pieces = jnp.concatenate([rest_total, down_total, qkv_here.reshape(-1, width)])
        every = lax.all_gather(pieces, ("core", "chip"))
        hidden_rows = 3 * piece + out_piece
        grad_gateup, down_weight_gradient = assemble(
            every[:, :hidden_rows], cores, chips, share, per, piece, out_piece
        )
        output_weight_gradient = every[:, 2 * piece : 2 * piece + out_piece].astype(F32)
        output_weight_gradient = output_weight_gradient.reshape(heads_rows, width)
        query_key_value_gradient = every[:, hidden_rows:].reshape(
            cores * chips, 3, qkv_rows, heads_rows
        )
        query_key_value_gradient = (
            jnp.swapaxes(query_key_value_gradient, 0, 1)
            .astype(F32)
            .reshape(3, width, heads_rows)
        )
        return (
            layer_out[None],
            input_grad[None],
            grad_gain_attn,
            query_key_value_gradient,
            output_weight_gradient,
            grad_gain_mlp,
            grad_gateup,
            down_weight_gradient,
        )

    return on_device


def solution(mesh):
    ranks = mesh.shape["tensor"]
    cores = 2
    chips = mesh.shape["dp"] // cores
    split = Mesh(mesh.devices.reshape(chips, cores, ranks), ("chip", "core", "tensor"))
    dp = ("chip", "core")
    rows = P(dp, "tensor", None)
    last = P(None, None, "tensor")
    first = P("tensor", None)
    return jax.shard_map(
        make(chips, cores, ranks),
        mesh=split,
        in_specs=(rows, P(dp, None), P(), last, first, P(), last, first, rows),
        out_specs=(rows, rows, P(), last, first, P(), last, first),
        check_vma=False,
    )
```

```python
import math

import jax
import jax.numpy as jnp
from jax import lax
from jax.experimental import pallas as pl
from jax.experimental.pallas import tpu as pltpu
from jax.sharding import Mesh, PartitionSpec as P

HD = 64
EPSILON = 1e-05
ROPE_BASE = 160000.0
BF = jnp.bfloat16
F32 = jnp.float32


def normalize(values):
    centered = values - jnp.mean(values, axis=-1, keepdims=True)
    variance = jnp.mean(centered * centered, axis=-1, keepdims=True)
    inverse = lax.rsqrt(variance + EPSILON)
    return (centered * inverse, inverse)


def norm_back(grad, normal, inverse, gain):
    scaled = grad * gain
    return inverse * (
        scaled
        - jnp.mean(scaled, axis=-1, keepdims=True)
        - normal * jnp.mean(scaled * normal, axis=-1, keepdims=True)
    )


def nt(left, right):
    return lax.dot_general(left, right, (((1,), (1,)), ((), ())), preferred_element_type=F32)


def nn(left, right):
    return jnp.dot(left, right, preferred_element_type=F32)


def tn(left, right):
    return lax.dot_general(left, right, (((0,), (0,)), ((), ())), preferred_element_type=F32)


def swap_halves(values):
    lane = lax.broadcasted_iota(jnp.int32, values.shape, 1)
    width = values.shape[1]
    ahead = pltpu.roll(values, width - HD // 2, 1)
    behind = pltpu.roll(values, HD // 2, 1)
    return jnp.where(lane % HD < HD // 2, ahead, behind)


def project_kernel(n_ref, w_ref, cos_ref, sin_ref, q_ref, k_ref, v_ref):
    rows = n_ref[...]
    cos, sin = cos_ref[...], sin_ref[...]
    for c, out in ((0, q_ref), (1, k_ref), (2, v_ref)):
        wide = nn(rows, w_ref[c])
        if c == 2:
            out[...] = wide.astype(BF)
            continue
        for at in range(0, wide.shape[1], 128):
            part = wide[:, at : at + 128]
            turned = (part * cos + swap_halves(part) * sin).astype(BF)
            if c == 0:
                turned = turned * (1.0 / math.sqrt(HD))
            out[:, at : at + 128] = turned


def project(rows, weight, cos, sin):
    length, width = rows.shape
    cols = weight.shape[2]
    block = 256
    return pl.pallas_call(
        project_kernel,
        grid=(length // block,),
        in_specs=[
            pl.BlockSpec((block, width), lambda i: (i, 0)),
            pl.BlockSpec((3, width, cols), lambda i: (0, 0, 0)),
            pl.BlockSpec((block, 128), lambda i: (i, 0)),
            pl.BlockSpec((block, 128), lambda i: (i, 0)),
        ],
        out_specs=[pl.BlockSpec((block, cols), lambda i: (i, 0))] * 3,
        out_shape=[jax.ShapeDtypeStruct((length, cols), BF)] * 3,
        compiler_params=pltpu.CompilerParams(vmem_limit_bytes=40 * 2**20),
        cost_estimate=pl.CostEstimate(
            flops=6 * length * width * cols, bytes_accessed=5 * 2**20, transcendentals=0
        ),
    )(rows, weight, cos, sin)


def half_mask(values, half):
    lane = lax.broadcasted_iota(jnp.int32, values.shape, 1)
    return jnp.where((lane // HD) == half, values, jnp.zeros_like(values))


def row_blocks(count):
    at = 0
    while at < count:
        size = min(256, count - at)
        yield at, size
        at += size


def turn(value, by):
    return pltpu.roll(value.astype(F32), by, 0)


def attend_kernel(doc, by_ref, q_ref, k_ref, v_ref, o_ref, l_ref, qd_ref, kd_ref, vd_ref, od_ref):
    length = q_ref.shape[0]
    into = lax.rem(length - by_ref[0], length)
    qd_ref[...] = turn(q_ref[...], into).astype(BF)
    kd_ref[...] = turn(k_ref[...], into).astype(BF)
    values = turn(v_ref[...], into)
    vd_ref[...] = values.astype(BF)
    od_ref[doc:, :] = values[doc:, :]
    keys = kd_ref[:doc, :]
    values_t = values[:doc, :].T.astype(BF)
    for at, size in row_blocks(doc):
        queries = qd_ref[at : at + size, :]
        mixed = []
        for half in range(2):
            scores = nt(keys, half_mask(queries, half))
            largest = jnp.max(scores, axis=0, keepdims=True)
            weights = jnp.exp(scores - largest)
            total = jnp.sum(weights, axis=0, keepdims=True)
            mix = nn(values_t[half * HD : half * HD + HD], weights.astype(BF))
            mixed.append(mix * (1.0 / total))
            l_ref[0, half : half + 1, at : at + size] = largest + jnp.log(total)
        od_ref[at : at + size, :] = jnp.concatenate(mixed, axis=0).T
    o_ref[...] = turn(od_ref[...], by_ref[0]).astype(BF)


def attend(by, queries, keys, values, doc):
    length, cols = queries.shape
    pairs = cols // 128
    spec = pl.BlockSpec((length, 128), lambda p: (0, p))
    return pl.pallas_call(
        lambda *refs: attend_kernel(doc, *refs),
        grid=(pairs,),
        in_specs=[pl.BlockSpec(memory_space=pltpu.SMEM)] + [spec] * 3,
        out_specs=[spec, pl.BlockSpec((1, 2, doc), lambda p: (p, 0, 0))] + [spec] * 3,
        out_shape=[
            jax.ShapeDtypeStruct((length, cols), BF),
            jax.ShapeDtypeStruct((pairs, 2, doc), F32),
        ]
        + [jax.ShapeDtypeStruct((length, cols), BF)] * 3,
        scratch_shapes=[pltpu.VMEM((length, 128), F32)],
        compiler_params=pltpu.CompilerParams(vmem_limit_bytes=48 * 2**20),
        cost_estimate=pl.CostEstimate(
            flops=8 * doc * doc * cols, bytes_accessed=2 * 2**20, transcendentals=doc * doc * 4
        ),
    )(by, queries, keys, values)


def attend_back_kernel(
    doc, by_ref, q_ref, k_ref, v_ref, d_ref, l_ref, cos_ref, sin_ref,
    dq_ref, dk_ref, dv_ref, qa_ref, ka_ref, va_ref, dd_ref,
):
    length = q_ref.shape[0]
    into = lax.rem(length - by_ref[0], length)
    turned = turn(d_ref[...], into)
    dd_ref[...] = turned.astype(BF)
    zero = jnp.zeros((length - doc, 128), F32)
    qa_ref[doc:, :] = zero
    ka_ref[doc:, :] = zero
    va_ref[doc:, :] = turned[doc:, :]
    keys = k_ref[:doc, :]
    keys_t = keys.T
    values = v_ref[:doc, :]
    first = True
    for at, size in row_blocks(doc):
        queries = q_ref[at : at + size, :]
        grads = dd_ref[at : at + size, :]
        back = []
        for half in range(2):
            query = half_mask(queries, half)
            grad = half_mask(grads, half)
            probs = jnp.exp(nt(keys, query) - l_ref[0, half : half + 1, at : at + size])
            prob_grad = nt(values, grad)
            centre = jnp.sum(probs * prob_grad, axis=0, keepdims=True)
            score_grad = (probs * (prob_grad - centre)).astype(BF)
            value_part = nn(probs.astype(BF), grad)
            key_part = nn(score_grad, query)
            if first:
                va_ref[:doc, :] = value_part
                ka_ref[:doc, :] = key_part
                first = False
            else:
                va_ref[:doc, :] += value_part
                ka_ref[:doc, :] += key_part
            back.append(nn(keys_t[half * HD : half * HD + HD], score_grad))
        qa_ref[at : at + size, :] = jnp.concatenate(back, axis=0).T * (1.0 / math.sqrt(HD))
    cos, sin = cos_ref[...], sin_ref[...]
    for held, out in ((qa_ref, dq_ref), (ka_ref, dk_ref)):
        grad = turn(held[...], by_ref[0])
        out[...] = (grad * cos - swap_halves(grad) * sin).astype(BF)
    dv_ref[...] = turn(va_ref[...], by_ref[0]).astype(BF)


def attend_back(by, queries, keys, values, grads, logs, cos, sin, doc):
    length, cols = queries.shape
    pairs = cols // 128
    spec = pl.BlockSpec((length, 128), lambda p: (0, p))
    table = pl.BlockSpec((length, 128), lambda p: (0, 0))
    return pl.pallas_call(
        lambda *refs: attend_back_kernel(doc, *refs),
        grid=(pairs,),
        in_specs=[pl.BlockSpec(memory_space=pltpu.SMEM)]
        + [spec] * 4
        + [pl.BlockSpec((1, 2, doc), lambda p: (p, 0, 0))]
        + [table] * 2,
        out_specs=[spec] * 3,
        out_shape=[jax.ShapeDtypeStruct((length, cols), BF)] * 3,
        scratch_shapes=[pltpu.VMEM((length, 128), F32)] * 3 + [pltpu.VMEM((length, 128), BF)],
        compiler_params=pltpu.CompilerParams(vmem_limit_bytes=48 * 2**20),
        cost_estimate=pl.CostEstimate(
            flops=20 * doc * doc * cols, bytes_accessed=5 * 2**20, transcendentals=doc * doc * 4
        ),
    )(by, queries, keys, values, grads, logs, cos, sin)


def assemble_kernel(sizes, in_ref, gu_ref, d_ref, o_ref, qkv_ref, held):
    cores, chips, share, per, piece, out_piece, qkv_part = sizes
    hidden = cores * share
    firsts = (0, piece, 2 * piece + out_piece)
    for m, first in enumerate(firsts):
        for device in range(cores * chips):
            at = device // chips * share + device % chips * per
            rows = in_ref[device].astype(F32)
            held[at : at + piece, :] = rows[first : first + piece, :]
            if m == 0:
                o_ref[device] = rows[2 * piece : 2 * piece + out_piece, :]
                last = 3 * piece + out_piece
                for c in range(3):
                    start = last + c * qkv_part
                    qkv_ref[c, device, 0] = rows[start : start + qkv_part, :]
        if m == 2:
            d_ref[...] = held[:hidden, :]
        else:
            gu_ref[m] = held[:hidden, :]


def assemble(every, sizes):
    cores, chips, share, per, piece, out_piece, qkv_part = sizes
    devices, rows, width = every.shape
    hidden = cores * share
    block = 256
    groups = width // block
    tall = -(-((cores - 1) * share + (chips - 1) * per + piece) // 8) * 8
    return pl.pallas_call(
        lambda *refs: assemble_kernel(sizes, *refs),
        grid=(groups,),
        in_specs=[pl.BlockSpec((devices, rows, block), lambda i: (0, 0, i))],
        out_specs=[
            pl.BlockSpec((2, hidden, block), lambda i: (0, 0, i)),
            pl.BlockSpec((hidden, block), lambda i: (0, i)),
            pl.BlockSpec((devices, out_piece, block), lambda i: (0, 0, i)),
            pl.BlockSpec((3, devices, 1, qkv_part, block), lambda i: (0, 0, i, 0, 0)),
        ],
        out_shape=[
            jax.ShapeDtypeStruct((2, hidden, width), F32),
            jax.ShapeDtypeStruct((hidden, width), F32),
            jax.ShapeDtypeStruct((devices, out_piece, width), F32),
            jax.ShapeDtypeStruct((3, devices, groups, qkv_part, block), F32),
        ],
        scratch_shapes=[pltpu.VMEM((tall, block), F32)],
        compiler_params=pltpu.CompilerParams(vmem_limit_bytes=40 * 2**20),
        cost_estimate=pl.CostEstimate(flops=0, bytes_accessed=18 * 2**20, transcendentals=0),
    )(every)


def shift(value, by, count):
    return lax.ppermute(value, "tensor", [(i, (i + by) % count) for i in range(count)])


def flip(value, axis, bit, count):
    return lax.ppermute(value, axis, [(i, i ^ bit) for i in range(count)])


def bits_of(count):
    return [1 << b for b in range(count.bit_length() - 1)]


def gather_ranks(value, count):
    ups, downs = [value], [value]
    for step in range(1, count):
        ups.append(lax.ppermute(ups[-1], "tensor", [(z, z + 1) for z in range(step - 1, count - 1)]))
        downs.append(lax.ppermute(downs[-1], "tensor", [(z, z - 1) for z in range(1, count - step + 1)]))
    return [downs[k] + ups[count - k] for k in range(1, count)]


def scatter_ranks(blocks, count):
    up, down = blocks[count - 1], blocks[1]
    for step in range(1, count):
        up = lax.ppermute(up, "tensor", [(z, z + 1) for z in range(step)])
        down = lax.ppermute(down, "tensor", [(z, z - 1) for z in range(count - step, count)])
        if step < count - 1:
            up = (up.astype(F32) + blocks[count - 1 - step].astype(F32)).astype(BF)
            down = (down.astype(F32) + blocks[step + 1].astype(F32)).astype(BF)
    return blocks[0].astype(F32) + up.astype(F32) + down.astype(F32)


class Halving:
    def __init__(self, value, chip, count, turned):
        self.chip, self.count = chip, count
        self.bits = count.bit_length() - 1
        self.held = value.reshape((2,) * self.bits + (-1,) + value.shape[-1:])
        order = list(range(self.bits))
        self.order = order if turned else order[::-1]
        self.left = list(range(self.bits))

    def send(self):
        axis = self.order.pop(0)
        bit = self.bits - 1 - axis
        mine = (self.chip >> bit) & 1
        at = self.left.index(axis)
        self.left.remove(axis)
        self.kept = lax.dynamic_index_in_dim(self.held, mine, at, keepdims=False)
        sent = lax.dynamic_index_in_dim(self.held, 1 - mine, at, keepdims=False)
        self.came = flip(sent, "chip", 1 << bit, self.count)

    def take(self):
        self.held = (self.kept.astype(F32) + self.came.astype(F32)).astype(BF)

    def finish(self):
        while self.order:
            self.send()
            self.take()
        return self.held


def tie(value, sums):
    tied = lax.optimization_barrier((value, *(s.came for s in sums)))
    for s, came in zip(sums, tied[1:]):
        s.came = came
        s.take()
    return tied[0]


def total_all(value, sizes):
    for axis, count in sizes:
        for bit in bits_of(count):
            value = value + flip(value, axis, bit, count)
    return value


def make(chips, cores, ranks):
    def on_device(
        tokens,
        segment_ids,
        gain_attn,
        query_key_value_weight,
        output_weight,
        gain_mlp,
        gate_up_weight,
        down_weight,
        cotangent,
    ):
        length = segment_ids.shape[1]
        own_rows, width = tokens.shape[1:]
        doc = length - length // 8
        others = ranks - 1
        rank = lax.axis_index("tensor")
        core = lax.axis_index("core")
        chip = lax.axis_index("chip")
        hold = lax.optimization_barrier

        hidden = down_weight.shape[0]
        share = hidden // cores
        per = -(-share // chips)
        piece = -(-per // 8) * 8
        heads_rows = output_weight.shape[0]
        out_piece = heads_rows // (cores * chips)
        gate_t, up_t = jnp.swapaxes(gate_up_weight, 1, 2)

        def part(weight, j):
            padded = jnp.pad(weight, ((0, chips * per + piece - share), (0, 0)))
            rows = lax.dynamic_slice_in_dim(padded, core * share + j * per, piece)
            at = lax.broadcasted_iota(jnp.int32, rows.shape, 0)
            return jnp.where((at < per) & (j * per + at < share), rows, jnp.zeros_like(rows))

        gate_mine = part(gate_t, chip)
        out_mine = lax.dynamic_slice_in_dim(
            output_weight, (core * chips + chip) * out_piece, out_piece
        )
        rest_mine = jnp.concatenate([part(up_t, chip), out_mine, part(down_weight, chip)])

        gate_came = jnp.concatenate([shift(gate_mine, -k, ranks) for k in range(1, ranks)])
        token_f = tokens[0].astype(F32)
        normal_attn, inverse_attn = normalize(token_f)
        normed_attn = (normal_attn * gain_attn).astype(BF)
        rest_sent, gate_came = hold((rest_mine, gate_came))
        gate_all = lax.all_gather(gate_came, "chip").reshape(chips, others * piece, width)
        rest_came = jnp.concatenate(gather_ranks(rest_sent, ranks))
        normed_sent, rest_came = hold((normed_attn, rest_came))
        rest_all = lax.all_gather(rest_came, "chip").reshape(chips, others, -1, width)
        normed_came = gather_ranks(normed_sent, ranks)
        normed_rows = jnp.concatenate([normed_attn] + normed_came)

        segments = segment_ids[0]
        middle = segments[length // 2]
        start = jnp.sum((segments < middle).astype(jnp.int32))
        by = (start - rank * own_rows) % length
        places = (jnp.arange(length, dtype=jnp.int32) - by) % length
        places = jnp.where(places < doc, places, 0)
        half = HD // 2
        freq = jnp.exp(jnp.arange(half, dtype=F32) * (-2.0 * math.log(ROPE_BASE) / HD))
        angles = places.astype(F32)[:, None] * jnp.concatenate([freq] * 4)[None, :]
        cos_table = jnp.cos(angles)
        lane = jnp.arange(2 * HD, dtype=jnp.int32)
        sin_table = jnp.sin(angles) * jnp.where(lane % HD < half, -1.0, 1.0)
        by = by[None]

        cot = cotangent[0]
        cot_pair = jnp.concatenate([cot, flip(cot, "core", 1, cores)])
        normed_rows, cos_table, sin_table, cot_pair = hold(
            (normed_rows, cos_table, sin_table, cot_pair)
        )

        queries, keys, values = project(normed_rows, query_key_value_weight, cos_table, sin_table)
        mixture, logs, queries, keys, values = attend(by, queries, keys, values, doc)
        mixture = mixture.reshape(ranks, own_rows, heads_rows)
        attention = jnp.concatenate(
            [mixture[0]] + [shift(mixture[k], k, ranks) for k in range(1, ranks)], axis=1
        )
        attention, gate_all, rest_all = hold((attention, gate_all, rest_all))

        def whole(weight, rest):
            blocks = []
            for j in range(chips):
                blocks += [part(weight, j), rest[j].reshape(-1, width)]
            return jnp.concatenate(blocks)

        out_half = jnp.swapaxes(rest_all[:, :, piece : piece + out_piece], 0, 1)
        out_half = out_half.reshape(others, heads_rows // cores, width)
        out_other = flip(out_half, "core", 1, cores)
        out_rest = jnp.concatenate(
            [
                jnp.where(core == 0, out_half, out_other),
                jnp.where(core == 0, out_other, out_half),
            ],
            axis=1,
        )
        out_weight = jnp.concatenate(
            [output_weight] + [out_rest[others - k] for k in range(1, ranks)]
        )
        hidden_state = token_f + nn(attention, out_weight)
        normal_mlp, inverse_mlp = normalize(hidden_state)
        normed_mlp = (normal_mlp * gain_mlp).astype(BF)
        gate = whole(gate_t, gate_all)
        up = whole(up_t, rest_all[:, :, :piece])
        down = whole(down_weight, rest_all[:, :, piece + out_piece :])

        normed_pair = jnp.concatenate([normed_mlp, flip(normed_mlp, "core", 1, cores)])
        gate_proj = nt(normed_pair, gate)
        up_proj = nt(normed_pair, up)
        cdf = 0.5 * (1.0 + lax.erf(gate_proj * (1.0 / math.sqrt(2.0))))
        pdf = jnp.exp(-0.5 * gate_proj * gate_proj) * (1.0 / math.sqrt(2.0 * math.pi))
        act = gate_proj * cdf
        hid = (act * up_proj).astype(BF)
        down_grad = tn(hid, cot_pair).astype(BF).reshape(chips, ranks * piece, width)
        cut = ranks * piece // 2
        down_sums = [
            Halving(down_grad[:, :cut], chip, chips, False),
            Halving(down_grad[:, cut:], chip, chips, True),
        ]
        for s in down_sums:
            s.send()
        hid_grad = nt(cot_pair, down)
        gate_grad = (hid_grad * up_proj * (cdf + gate_proj * pdf)).astype(BF)
        up_grad = (hid_grad * act).astype(BF)
        gate_sum = Halving(tn(gate_grad, normed_pair).astype(BF), chip, chips, False)
        up_sum = Halving(tn(up_grad, normed_pair).astype(BF), chip, chips, True)
        gate_grad, gate_sum.held, up_sum.held = hold((gate_grad, gate_sum.held, up_sum.held))
        gate_grad = tie(gate_grad, down_sums)
        gate_sum.send()
        up_sum.send()
        in_other = nn(gate_grad[own_rows:], gate) + nn(up_grad[own_rows:], up)
        in_came = flip(in_other.astype(BF), "core", 1, cores)
        in_part = nn(gate_grad[:own_rows], gate) + nn(up_grad[:own_rows], up)
        normed_mlp_grad = in_part + in_came.astype(F32)
        gain_mlp_part = jnp.sum(normed_mlp_grad * normal_mlp, axis=0)
        hidden_grad = cot.astype(F32) + norm_back(
            normed_mlp_grad, normal_mlp, inverse_mlp, gain_mlp
        )
        branch_grad = hidden_grad.astype(BF)

        attended_grad = nt(branch_grad, out_weight).astype(BF)
        attended_came = [
            shift(attended_grad[:, k * heads_rows : (k + 1) * heads_rows], -k, ranks)
            for k in range(1, ranks)
        ]
        mlp_part = nn(hid, down)
        mlp_out = mlp_part[:own_rows] + flip(
            mlp_part[own_rows:].astype(BF), "core", 1, cores
        ).astype(F32)
        layer_out = (hidden_state + mlp_out).astype(BF)

        def sum_cores(value, axis):
            kept = lax.dynamic_index_in_dim(value, core, axis, keepdims=False)
            sent = lax.dynamic_index_in_dim(value, 1 - core, axis, keepdims=False)
            return (kept.astype(F32) + flip(sent, "core", 1, cores).astype(F32)).astype(BF)

        out_w_grad = tn(attention, branch_grad).astype(BF)
        out_blocks = out_w_grad.reshape(ranks, cores, chips, out_piece, width)
        out_blocks = jnp.stack([out_blocks[(ranks - k) % ranks] for k in range(ranks)])
        out_blocks = jnp.swapaxes(sum_cores(out_blocks, 1), 0, 1)
        down_here = jnp.concatenate(
            [s.finish().reshape(-1, width) for s in down_sums]
        )
        attended_rows = jnp.concatenate([attended_grad[:, :heads_rows]] + attended_came)
        attended_rows, layer_out, out_blocks, down_here = hold(
            (attended_rows, layer_out, out_blocks, down_here)
        )

        def sum_ranks(here):
            rows = here.shape[1]
            flat = here.reshape(ranks * rows, width)
            twice = jnp.concatenate([flat, flat])
            flat = lax.dynamic_slice_in_dim(twice, (ranks - rank) % ranks * rows, ranks * rows)
            return lax.psum_scatter(flat, "tensor", scatter_dimension=0, tiled=True)

        down_total = sum_ranks(down_here.reshape(ranks, piece, width))
        attended_rows = tie(attended_rows, [gate_sum, up_sum])
        out_sum = Halving(out_blocks, chip, chips, True)
        gate_sum.send()
        up_sum.send()
        out_sum.send()
        dq, dk, dv = attend_back(
            by, queries, keys, values, attended_rows, logs, cos_table, sin_table, doc
        )
        normed_attn_part = (
            nt(dq, query_key_value_weight[0])
            + nt(dk, query_key_value_weight[1])
            + nt(dv, query_key_value_weight[2])
        )
        gain_attn_part = jnp.sum(normed_attn_part * normed_rows.astype(F32), axis=0) / gain_attn
        part_rows = normed_attn_part.astype(BF).reshape(ranks, own_rows, width)
        qkv_grad = jnp.stack([tn(normed_rows, g) for g in (dq, dk, dv)]).astype(BF)
        part_rows, qkv_grad, gain_attn_part = hold((part_rows, qkv_grad, gain_attn_part))
        part_rows = tie(part_rows, [gate_sum, up_sum, out_sum])
        rest_total = sum_ranks(
            jnp.concatenate(
                [
                    gate_sum.finish().reshape(ranks, piece, width),
                    up_sum.finish().reshape(ranks, piece, width),
                    out_sum.finish().reshape(ranks, out_piece, width),
                ],
                axis=1,
            )
        )
        normed_attn_grad = scatter_ranks(part_rows, ranks)
        input_grad = (
            hidden_grad + norm_back(normed_attn_grad, normal_attn, inverse_attn, gain_attn)
        ).astype(BF)

        qkv_rows = width // (cores * chips)
        qkv_blocks = qkv_grad.reshape(3, cores, chips, qkv_rows, heads_rows)
        qkv_blocks = jnp.swapaxes(sum_cores(qkv_blocks, 1), 0, 1)
        qkv_here = Halving(qkv_blocks, chip, chips, False).finish()
        gains = total_all(
            jnp.concatenate([gain_attn_part, gain_mlp_part]),
            (("core", cores), ("chip", chips), ("tensor", ranks)),
        )
        qkv_here, gains = hold((qkv_here, gains))
        grad_gain_attn, grad_gain_mlp = gains[:width], gains[width:]
        groups = width // heads_rows
        qkv_part = qkv_rows // groups
        qkv_here = qkv_here.reshape(3, groups, qkv_part, heads_rows)
        qkv_here = jnp.concatenate(
            [qkv_here[:, g].reshape(3 * qkv_part, heads_rows) for g in range(groups)], axis=1
        )
        pieces = jnp.concatenate([rest_total, down_total, qkv_here])
        every = lax.all_gather(pieces, ("core", "chip"))
        grads = assemble(every, (cores, chips, share, per, piece, out_piece, qkv_part))
        grad_gateup = jnp.swapaxes(grads[0], 1, 2)
        down_weight_gradient = grads[1]
        output_weight_gradient = grads[2].reshape(heads_rows, width)
        query_key_value_gradient = grads[3].reshape(3, width, heads_rows)
        return (
            layer_out[None],
            input_grad[None],
            grad_gain_attn,
            query_key_value_gradient,
            output_weight_gradient,
            grad_gain_mlp,
            grad_gateup,
            down_weight_gradient,
        )

    return on_device


def solution(mesh):
    ranks = mesh.shape["tensor"]
    cores = 2
    chips = mesh.shape["dp"] // cores
    split = Mesh(mesh.devices.reshape(chips, cores, ranks), ("chip", "core", "tensor"))
    dp = ("chip", "core")
    rows = P(dp, "tensor", None)
    last = P(None, None, "tensor")
    first = P("tensor", None)
    return jax.shard_map(
        make(chips, cores, ranks),
        mesh=split,
        in_specs=(rows, P(dp, None), P(), last, first, P(), last, first, rows),
        out_specs=(rows, rows, P(), last, first, P(), last, first),
        check_vma=False,
    )
```

```python
import math

import jax
import jax.numpy as jnp
from jax import lax
from jax.experimental import pallas as pl
from jax.experimental.pallas import tpu as pltpu
from jax.sharding import Mesh, PartitionSpec as P

HD = 64
EPSILON = 1e-05
ROPE_BASE = 160000.0
BF = jnp.bfloat16
F32 = jnp.float32


def normalize(values):
    centered = values - jnp.mean(values, axis=-1, keepdims=True)
    variance = jnp.mean(centered * centered, axis=-1, keepdims=True)
    inverse = lax.rsqrt(variance + EPSILON)
    return (centered * inverse, inverse)


def norm_back(grad, normal, inverse, gain):
    scaled = grad * gain
    return inverse * (
        scaled
        - jnp.mean(scaled, axis=-1, keepdims=True)
        - normal * jnp.mean(scaled * normal, axis=-1, keepdims=True)
    )


def nt(left, right):
    return lax.dot_general(left, right, (((1,), (1,)), ((), ())), preferred_element_type=F32)


def nn(left, right):
    return jnp.dot(left, right, preferred_element_type=F32)


def tn(left, right):
    return lax.dot_general(left, right, (((0,), (0,)), ((), ())), preferred_element_type=F32)


def swap_halves(values):
    lane = lax.broadcasted_iota(jnp.int32, values.shape, 1)
    width = values.shape[1]
    ahead = pltpu.roll(values, width - HD // 2, 1)
    behind = pltpu.roll(values, HD // 2, 1)
    return jnp.where(lane % HD < HD // 2, ahead, behind)


def project_kernel(ranks, rank_ref, *refs):
    own_ref, *came = refs[: 2 * ranks - 1]
    w_ref, cos_ref, sin_ref, n_ref, q_ref, k_ref, v_ref = refs[2 * ranks - 1 :]
    ups, downs = came[: ranks - 1], came[ranks - 1 :]
    step = pl.program_id(0)

    @pl.when(step == 0)
    def _():
        n_ref[...] = own_ref[...]

    for k in range(1, ranks):
        below = rank_ref[0] + k < ranks

        @pl.when((step == k) & below)
        def _():
            n_ref[...] = downs[k - 1][...]

        @pl.when((step == k) & jnp.logical_not(below))
        def _():
            n_ref[...] = ups[ranks - k - 1][...]

    rows = n_ref[...]
    cos, sin = cos_ref[...], sin_ref[...]
    for c, out in ((0, q_ref), (1, k_ref), (2, v_ref)):
        wide = nn(rows, w_ref[c])
        if c == 2:
            out[...] = wide.astype(BF)
            continue
        for at in range(0, wide.shape[1], 128):
            part = wide[:, at : at + 128]
            turned = (part * cos + swap_halves(part) * sin).astype(BF)
            if c == 0:
                turned = turned * (1.0 / math.sqrt(HD))
            out[:, at : at + 128] = turned


def project(rank, own, ups, downs, weight, cos, sin):
    block, width = own.shape
    ranks = len(ups) + 1
    length = ranks * block
    cols = weight.shape[2]
    return pl.pallas_call(
        lambda *refs: project_kernel(ranks, *refs),
        grid=(ranks,),
        in_specs=[pl.BlockSpec(memory_space=pltpu.SMEM)]
        + [pl.BlockSpec((block, width), lambda i: (0, 0))] * (2 * ranks - 1)
        + [
            pl.BlockSpec((3, width, cols), lambda i: (0, 0, 0)),
            pl.BlockSpec((block, 128), lambda i: (i, 0)),
            pl.BlockSpec((block, 128), lambda i: (i, 0)),
        ],
        out_specs=[pl.BlockSpec((block, width), lambda i: (i, 0))]
        + [pl.BlockSpec((block, cols), lambda i: (i, 0))] * 3,
        out_shape=[jax.ShapeDtypeStruct((length, width), BF)]
        + [jax.ShapeDtypeStruct((length, cols), BF)] * 3,
        compiler_params=pltpu.CompilerParams(vmem_limit_bytes=40 * 2**20),
        cost_estimate=pl.CostEstimate(
            flops=6 * length * width * cols, bytes_accessed=9 * 2**20, transcendentals=0
        ),
    )(rank, own, *ups, *downs, weight, cos, sin)


def half_mask(values, half):
    lane = lax.broadcasted_iota(jnp.int32, values.shape, 1)
    return jnp.where((lane // HD) == half, values, jnp.zeros_like(values))


def row_blocks(count):
    at = 0
    while at < count:
        size = min(256, count - at)
        yield at, size
        at += size


def turn(value, by):
    return pltpu.roll(value.astype(F32), by, 0)


def attend_kernel(doc, by_ref, q_ref, k_ref, v_ref, o_ref, l_ref, qd_ref, kd_ref, vd_ref, od_ref):
    length = q_ref.shape[0]
    into = lax.rem(length - by_ref[0], length)
    qd_ref[...] = turn(q_ref[...], into).astype(BF)
    kd_ref[...] = turn(k_ref[...], into).astype(BF)
    values = turn(v_ref[...], into)
    vd_ref[...] = values.astype(BF)
    od_ref[doc:, :] = values[doc:, :]
    keys = kd_ref[:doc, :]
    values_t = values[:doc, :].T.astype(BF)
    for at, size in row_blocks(doc):
        queries = qd_ref[at : at + size, :]
        mixed = []
        for half in range(2):
            scores = nt(keys, half_mask(queries, half))
            largest = jnp.max(scores, axis=0, keepdims=True)
            weights = jnp.exp(scores - largest)
            total = jnp.sum(weights, axis=0, keepdims=True)
            mix = nn(values_t[half * HD : half * HD + HD], weights.astype(BF))
            mixed.append(mix * (1.0 / total))
            l_ref[0, half : half + 1, at : at + size] = largest + jnp.log(total)
        od_ref[at : at + size, :] = jnp.concatenate(mixed, axis=0).T
    o_ref[...] = turn(od_ref[...], by_ref[0]).astype(BF)


def attend(by, queries, keys, values, doc):
    length, cols = queries.shape
    pairs = cols // 128
    spec = pl.BlockSpec((length, 128), lambda p: (0, p))
    return pl.pallas_call(
        lambda *refs: attend_kernel(doc, *refs),
        grid=(pairs,),
        in_specs=[pl.BlockSpec(memory_space=pltpu.SMEM)] + [spec] * 3,
        out_specs=[spec, pl.BlockSpec((1, 2, doc), lambda p: (p, 0, 0))] + [spec] * 3,
        out_shape=[
            jax.ShapeDtypeStruct((length, cols), BF),
            jax.ShapeDtypeStruct((pairs, 2, doc), F32),
        ]
        + [jax.ShapeDtypeStruct((length, cols), BF)] * 3,
        scratch_shapes=[pltpu.VMEM((length, 128), F32)],
        compiler_params=pltpu.CompilerParams(vmem_limit_bytes=48 * 2**20),
        cost_estimate=pl.CostEstimate(
            flops=8 * doc * doc * cols, bytes_accessed=2 * 2**20, transcendentals=doc * doc * 4
        ),
    )(by, queries, keys, values)


def attend_back_kernel(
    doc, by_ref, q_ref, k_ref, v_ref, d_ref, l_ref, cos_ref, sin_ref,
    dq_ref, dk_ref, dv_ref, qa_ref, ka_ref, va_ref, dd_ref,
):
    length = q_ref.shape[0]
    into = lax.rem(length - by_ref[0], length)
    turned = turn(d_ref[...], into)
    dd_ref[...] = turned.astype(BF)
    zero = jnp.zeros((length - doc, 128), F32)
    qa_ref[doc:, :] = zero
    ka_ref[doc:, :] = zero
    va_ref[doc:, :] = turned[doc:, :]
    keys = k_ref[:doc, :]
    keys_t = keys.T
    values = v_ref[:doc, :]
    first = True
    for at, size in row_blocks(doc):
        queries = q_ref[at : at + size, :]
        grads = dd_ref[at : at + size, :]
        back = []
        for half in range(2):
            query = half_mask(queries, half)
            grad = half_mask(grads, half)
            probs = jnp.exp(nt(keys, query) - l_ref[0, half : half + 1, at : at + size])
            prob_grad = nt(values, grad)
            centre = jnp.sum(probs * prob_grad, axis=0, keepdims=True)
            score_grad = (probs * (prob_grad - centre)).astype(BF)
            value_part = nn(probs.astype(BF), grad)
            key_part = nn(score_grad, query)
            if first:
                va_ref[:doc, :] = value_part
                ka_ref[:doc, :] = key_part
                first = False
            else:
                va_ref[:doc, :] += value_part
                ka_ref[:doc, :] += key_part
            back.append(nn(keys_t[half * HD : half * HD + HD], score_grad))
        qa_ref[at : at + size, :] = jnp.concatenate(back, axis=0).T * (1.0 / math.sqrt(HD))
    cos, sin = cos_ref[...], sin_ref[...]
    for held, out in ((qa_ref, dq_ref), (ka_ref, dk_ref)):
        grad = turn(held[...], by_ref[0])
        out[...] = (grad * cos - swap_halves(grad) * sin).astype(BF)
    dv_ref[...] = turn(va_ref[...], by_ref[0]).astype(BF)


def attend_back(by, queries, keys, values, grads, logs, cos, sin, doc):
    length, cols = queries.shape
    pairs = cols // 128
    spec = pl.BlockSpec((length, 128), lambda p: (0, p))
    table = pl.BlockSpec((length, 128), lambda p: (0, 0))
    return pl.pallas_call(
        lambda *refs: attend_back_kernel(doc, *refs),
        grid=(pairs,),
        in_specs=[pl.BlockSpec(memory_space=pltpu.SMEM)]
        + [spec] * 4
        + [pl.BlockSpec((1, 2, doc), lambda p: (p, 0, 0))]
        + [table] * 2,
        out_specs=[spec] * 3,
        out_shape=[jax.ShapeDtypeStruct((length, cols), BF)] * 3,
        scratch_shapes=[pltpu.VMEM((length, 128), F32)] * 3 + [pltpu.VMEM((length, 128), BF)],
        compiler_params=pltpu.CompilerParams(vmem_limit_bytes=48 * 2**20),
        cost_estimate=pl.CostEstimate(
            flops=20 * doc * doc * cols, bytes_accessed=5 * 2**20, transcendentals=doc * doc * 4
        ),
    )(by, queries, keys, values, grads, logs, cos, sin)


def assemble_kernel(sizes, in_ref, gu_ref, d_ref, o_ref, qkv_ref, held):
    cores, chips, share, per, piece, out_piece, qkv_part = sizes
    hidden = cores * share
    firsts = (0, piece, 2 * piece + out_piece)
    for m, first in enumerate(firsts):
        for device in range(cores * chips):
            at = device // chips * share + device % chips * per
            rows = in_ref[device].astype(F32)
            held[at : at + piece, :] = rows[first : first + piece, :]
            if m == 0:
                o_ref[device] = rows[2 * piece : 2 * piece + out_piece, :]
                last = 3 * piece + out_piece
                for c in range(3):
                    start = last + c * qkv_part
                    qkv_ref[c, device, 0] = rows[start : start + qkv_part, :]
        if m == 2:
            d_ref[...] = held[:hidden, :]
        else:
            gu_ref[m] = held[:hidden, :]


def assemble(every, sizes):
    cores, chips, share, per, piece, out_piece, qkv_part = sizes
    devices, rows, width = every.shape
    hidden = cores * share
    block = 256
    groups = width // block
    tall = -(-((cores - 1) * share + (chips - 1) * per + piece) // 8) * 8
    return pl.pallas_call(
        lambda *refs: assemble_kernel(sizes, *refs),
        grid=(groups,),
        in_specs=[pl.BlockSpec((devices, rows, block), lambda i: (0, 0, i))],
        out_specs=[
            pl.BlockSpec((2, hidden, block), lambda i: (0, 0, i)),
            pl.BlockSpec((hidden, block), lambda i: (0, i)),
            pl.BlockSpec((devices, out_piece, block), lambda i: (0, 0, i)),
            pl.BlockSpec((3, devices, 1, qkv_part, block), lambda i: (0, 0, i, 0, 0)),
        ],
        out_shape=[
            jax.ShapeDtypeStruct((2, hidden, width), F32),
            jax.ShapeDtypeStruct((hidden, width), F32),
            jax.ShapeDtypeStruct((devices, out_piece, width), F32),
            jax.ShapeDtypeStruct((3, devices, groups, qkv_part, block), F32),
        ],
        scratch_shapes=[pltpu.VMEM((tall, block), F32)],
        compiler_params=pltpu.CompilerParams(vmem_limit_bytes=40 * 2**20),
        cost_estimate=pl.CostEstimate(flops=0, bytes_accessed=18 * 2**20, transcendentals=0),
    )(every)


def shift(value, by, count):
    return lax.ppermute(value, "tensor", [(i, (i + by) % count) for i in range(count)])


def flip(value, axis, bit, count):
    return lax.ppermute(value, axis, [(i, i ^ bit) for i in range(count)])


def bits_of(count):
    return [1 << b for b in range(count.bit_length() - 1)]


def relay_ranks(value, count):
    ups, downs = [value], [value]
    for step in range(1, count):
        ups.append(lax.ppermute(ups[-1], "tensor", [(z, z + 1) for z in range(step - 1, count - 1)]))
        downs.append(lax.ppermute(downs[-1], "tensor", [(z, z - 1) for z in range(1, count - step + 1)]))
    return ups[1:], downs[1:]


def scatter_ranks(blocks, count):
    up, down = blocks[count - 1], blocks[1]
    for step in range(1, count):
        up = lax.ppermute(up, "tensor", [(z, z + 1) for z in range(step)])
        down = lax.ppermute(down, "tensor", [(z, z - 1) for z in range(count - step, count)])
        if step < count - 1:
            up = (up.astype(F32) + blocks[count - 1 - step].astype(F32)).astype(BF)
            down = (down.astype(F32) + blocks[step + 1].astype(F32)).astype(BF)
    return blocks[0].astype(F32) + up.astype(F32) + down.astype(F32)


class Halving:
    def __init__(self, value, chip, count, turned):
        self.chip, self.count = chip, count
        self.bits = count.bit_length() - 1
        self.held = value.reshape((2,) * self.bits + (-1,) + value.shape[-1:])
        order = list(range(self.bits))
        self.order = order if turned else order[::-1]
        self.left = list(range(self.bits))

    def send(self):
        axis = self.order.pop(0)
        bit = self.bits - 1 - axis
        mine = (self.chip >> bit) & 1
        at = self.left.index(axis)
        self.left.remove(axis)
        self.kept = lax.dynamic_index_in_dim(self.held, mine, at, keepdims=False)
        sent = lax.dynamic_index_in_dim(self.held, 1 - mine, at, keepdims=False)
        self.came = flip(sent, "chip", 1 << bit, self.count)

    def take(self):
        self.held = (self.kept.astype(F32) + self.came.astype(F32)).astype(BF)

    def finish(self):
        while self.order:
            self.send()
            self.take()
        return self.held


def tie(value, sums):
    tied = lax.optimization_barrier((value, *(s.came for s in sums)))
    for s, came in zip(sums, tied[1:]):
        s.came = came
        s.take()
    return tied[0]


def total_all(value, sizes):
    for axis, count in sizes:
        for bit in bits_of(count):
            value = value + flip(value, axis, bit, count)
    return value


def make(chips, cores, ranks):
    def on_device(
        tokens,
        segment_ids,
        gain_attn,
        query_key_value_weight,
        output_weight,
        gain_mlp,
        gate_up_weight,
        down_weight,
        cotangent,
    ):
        length = segment_ids.shape[1]
        own_rows, width = tokens.shape[1:]
        doc = length - length // 8
        others = ranks - 1
        rank = lax.axis_index("tensor")
        core = lax.axis_index("core")
        chip = lax.axis_index("chip")
        hold = lax.optimization_barrier

        hidden = down_weight.shape[0]
        share = hidden // cores
        per = -(-share // chips)
        piece = -(-per // 8) * 8
        heads_rows = output_weight.shape[0]
        out_piece = heads_rows // (cores * chips)
        gate_t, up_t = jnp.swapaxes(gate_up_weight, 1, 2)

        def part(weight, j):
            padded = jnp.pad(weight, ((0, chips * per + piece - share), (0, 0)))
            rows = lax.dynamic_slice_in_dim(padded, core * share + j * per, piece)
            at = lax.broadcasted_iota(jnp.int32, rows.shape, 0)
            return jnp.where((at < per) & (j * per + at < share), rows, jnp.zeros_like(rows))

        out_mine = lax.dynamic_slice_in_dim(
            output_weight, (core * chips + chip) * out_piece, out_piece
        )
        gate_out_mine = jnp.concatenate([part(gate_t, chip), out_mine])
        up_down_mine = jnp.concatenate([part(up_t, chip), part(down_weight, chip)])

        gate_out_came = jnp.concatenate([shift(gate_out_mine, -k, ranks) for k in range(1, ranks)])
        token_f = tokens[0].astype(F32)
        normal_attn, inverse_attn = normalize(token_f)
        normed_attn = (normal_attn * gain_attn).astype(BF)
        up_down_sent, normed_sent, gate_out_came = hold((up_down_mine, normed_attn, gate_out_came))
        gate_out_all = lax.all_gather(gate_out_came, "chip").reshape(chips, others, -1, width)
        ups, downs = relay_ranks(up_down_sent, ranks)
        up_down_came = jnp.concatenate([downs[k] + ups[others - 1 - k] for k in range(others)])
        up_down_all = lax.all_gather(up_down_came, "chip").reshape(chips, others, -1, width)
        normed_ups, normed_downs = relay_ranks(normed_sent, ranks)

        segments = segment_ids[0]
        middle = segments[length // 2]
        start = jnp.sum((segments < middle).astype(jnp.int32))
        by = (start - rank * own_rows) % length
        places = (jnp.arange(length, dtype=jnp.int32) - by) % length
        places = jnp.where(places < doc, places, 0)
        half = HD // 2
        freq = jnp.exp(jnp.arange(half, dtype=F32) * (-2.0 * math.log(ROPE_BASE) / HD))
        angles = places.astype(F32)[:, None] * jnp.concatenate([freq] * 4)[None, :]
        cos_table = jnp.cos(angles)
        lane = jnp.arange(2 * HD, dtype=jnp.int32)
        sin_table = jnp.sin(angles) * jnp.where(lane % HD < half, -1.0, 1.0)
        by = by[None]

        cot = cotangent[0]
        cot_pair = jnp.concatenate([cot, flip(cot, "core", 1, cores)])
        normed_attn, cos_table, sin_table, cot_pair = hold(
            (normed_attn, cos_table, sin_table, cot_pair)
        )

        normed_rows, queries, keys, values = project(
            rank[None],
            normed_attn,
            normed_ups,
            normed_downs,
            query_key_value_weight,
            cos_table,
            sin_table,
        )
        mixture, logs, queries, keys, values = attend(by, queries, keys, values, doc)
        mixture = mixture.reshape(ranks, own_rows, heads_rows)
        mixture_own, gate_out_all = hold((mixture[0], gate_out_all))
        attention = jnp.concatenate(
            [mixture_own] + [shift(mixture[k], k, ranks) for k in range(1, ranks)], axis=1
        )
        attention, up_down_all = hold((attention, up_down_all))

        def whole(weight, rest):
            blocks = []
            for j in range(chips):
                blocks += [part(weight, j), rest[j].reshape(-1, width)]
            return jnp.concatenate(blocks)

        out_half = jnp.swapaxes(gate_out_all[:, :, piece:], 0, 1)
        out_half = out_half.reshape(others, heads_rows // cores, width)
        out_other = flip(out_half, "core", 1, cores)
        out_rest = jnp.concatenate(
            [
                jnp.where(core == 0, out_half, out_other),
                jnp.where(core == 0, out_other, out_half),
            ],
            axis=1,
        )
        out_weight = jnp.concatenate(
            [output_weight] + [out_rest[others - k] for k in range(1, ranks)]
        )
        hidden_state = token_f + nn(attention, out_weight)
        normal_mlp, inverse_mlp = normalize(hidden_state)
        normed_mlp = (normal_mlp * gain_mlp).astype(BF)
        gate = whole(gate_t, gate_out_all[:, :, :piece])
        up = whole(up_t, up_down_all[:, :, :piece])
        down = whole(down_weight, up_down_all[:, :, piece:])

        normed_pair = jnp.concatenate([normed_mlp, flip(normed_mlp, "core", 1, cores)])
        gate_proj = nt(normed_pair, gate)
        up_proj = nt(normed_pair, up)
        cdf = 0.5 * (1.0 + lax.erf(gate_proj * (1.0 / math.sqrt(2.0))))
        pdf = jnp.exp(-0.5 * gate_proj * gate_proj) * (1.0 / math.sqrt(2.0 * math.pi))
        act = gate_proj * cdf
        hid = (act * up_proj).astype(BF)
        down_grad = tn(hid, cot_pair).astype(BF).reshape(chips, ranks * piece, width)
        cot_pair, down_grad = hold((cot_pair, down_grad))
        cut = ranks * piece // 2
        down_sums = [
            Halving(down_grad[:, :cut], chip, chips, False),
            Halving(down_grad[:, cut:], chip, chips, True),
        ]
        for s in down_sums:
            s.send()
        hid_grad = nt(cot_pair, down)
        gate_grad = (hid_grad * up_proj * (cdf + gate_proj * pdf)).astype(BF)
        up_grad = (hid_grad * act).astype(BF)
        gate_sum = Halving(tn(gate_grad, normed_pair).astype(BF), chip, chips, False)
        up_sum = Halving(tn(up_grad, normed_pair).astype(BF), chip, chips, True)
        gate_grad, gate_sum.held, up_sum.held = hold((gate_grad, gate_sum.held, up_sum.held))
        gate_sum.send()
        up_sum.send()
        in_other = nn(gate_grad[own_rows:], gate) + nn(up_grad[own_rows:], up)
        in_came = flip(in_other.astype(BF), "core", 1, cores)
        in_part = nn(gate_grad[:own_rows], gate) + nn(up_grad[:own_rows], up)
        normed_mlp_grad = in_part + in_came.astype(F32)
        gain_mlp_part = jnp.sum(normed_mlp_grad * normal_mlp, axis=0)
        hidden_grad = cot.astype(F32) + norm_back(
            normed_mlp_grad, normal_mlp, inverse_mlp, gain_mlp
        )
        branch_grad = tie(hidden_grad.astype(BF), down_sums)

        attended_grad = nt(branch_grad, out_weight).astype(BF)
        attended_came = [
            shift(attended_grad[:, k * heads_rows : (k + 1) * heads_rows], -k, ranks)
            for k in range(1, ranks)
        ]
        mlp_part = nn(hid, down)
        mlp_out = mlp_part[:own_rows] + flip(
            mlp_part[own_rows:].astype(BF), "core", 1, cores
        ).astype(F32)
        layer_out = (hidden_state + mlp_out).astype(BF)

        def sum_cores(value, axis):
            kept = lax.dynamic_index_in_dim(value, core, axis, keepdims=False)
            sent = lax.dynamic_index_in_dim(value, 1 - core, axis, keepdims=False)
            return (kept.astype(F32) + flip(sent, "core", 1, cores).astype(F32)).astype(BF)

        out_w_grad = tn(attention, branch_grad).astype(BF)
        out_blocks = out_w_grad.reshape(ranks, cores, chips, out_piece, width)
        out_blocks = jnp.stack([out_blocks[(ranks - k) % ranks] for k in range(ranks)])
        out_blocks = jnp.swapaxes(sum_cores(out_blocks, 1), 0, 1)
        down_here = jnp.concatenate(
            [s.finish().reshape(-1, width) for s in down_sums]
        )
        attended_rows = jnp.concatenate([attended_grad[:, :heads_rows]] + attended_came)
        attended_rows, layer_out, out_blocks, down_here = hold(
            (attended_rows, layer_out, out_blocks, down_here)
        )

        def sum_ranks(here):
            rows = here.shape[1]
            flat = here.reshape(ranks * rows, width)
            twice = jnp.concatenate([flat, flat])
            flat = lax.dynamic_slice_in_dim(twice, (ranks - rank) % ranks * rows, ranks * rows)
            return lax.psum_scatter(flat, "tensor", scatter_dimension=0, tiled=True)

        down_total = sum_ranks(down_here.reshape(ranks, piece, width))
        out_sum = Halving(out_blocks, chip, chips, True)
        out_sum.send()
        dq, dk, dv = attend_back(
            by, queries, keys, values, attended_rows, logs, cos_table, sin_table, doc
        )
        dq = tie(dq, [gate_sum, up_sum])
        gate_sum.send()
        up_sum.send()
        normed_attn_part = (
            nt(dq, query_key_value_weight[0])
            + nt(dk, query_key_value_weight[1])
            + nt(dv, query_key_value_weight[2])
        )
        gain_attn_part = jnp.sum(normed_attn_part * normed_rows.astype(F32), axis=0) / gain_attn
        part_rows = normed_attn_part.astype(BF).reshape(ranks, own_rows, width)
        qkv_grad = jnp.stack([tn(normed_rows, g) for g in (dq, dk, dv)]).astype(BF)
        part_rows, qkv_grad, gain_attn_part = hold((part_rows, qkv_grad, gain_attn_part))
        part_rows = tie(part_rows, [gate_sum, up_sum, out_sum])
        rest_total = sum_ranks(
            jnp.concatenate(
                [
                    gate_sum.finish().reshape(ranks, piece, width),
                    up_sum.finish().reshape(ranks, piece, width),
                    out_sum.finish().reshape(ranks, out_piece, width),
                ],
                axis=1,
            )
        )
        normed_attn_grad = scatter_ranks(part_rows, ranks)
        input_grad = (
            hidden_grad + norm_back(normed_attn_grad, normal_attn, inverse_attn, gain_attn)
        ).astype(BF)

        qkv_rows = width // (cores * chips)
        qkv_blocks = qkv_grad.reshape(3, cores, chips, qkv_rows, heads_rows)
        qkv_blocks = jnp.swapaxes(sum_cores(qkv_blocks, 1), 0, 1)
        qkv_here = Halving(qkv_blocks, chip, chips, False).finish()
        gains = total_all(
            jnp.concatenate([gain_attn_part, gain_mlp_part]),
            (("core", cores), ("chip", chips), ("tensor", ranks)),
        )
        qkv_here, gains, input_grad = hold((qkv_here, gains, input_grad))
        grad_gain_attn, grad_gain_mlp = gains[:width], gains[width:]
        groups = width // heads_rows
        qkv_part = qkv_rows // groups
        qkv_here = qkv_here.reshape(3, groups, qkv_part, heads_rows)
        qkv_here = jnp.concatenate(
            [qkv_here[:, g].reshape(3 * qkv_part, heads_rows) for g in range(groups)], axis=1
        )
        pieces = jnp.concatenate([rest_total, down_total, qkv_here])
        every = lax.all_gather(pieces, ("core", "chip"))
        grads = assemble(every, (cores, chips, share, per, piece, out_piece, qkv_part))
        grad_gateup = jnp.swapaxes(grads[0], 1, 2)
        down_weight_gradient = grads[1]
        output_weight_gradient = grads[2].reshape(heads_rows, width)
        query_key_value_gradient = grads[3].reshape(3, width, heads_rows)
        return (
            layer_out[None],
            input_grad[None],
            grad_gain_attn,
            query_key_value_gradient,
            output_weight_gradient,
            grad_gain_mlp,
            grad_gateup,
            down_weight_gradient,
        )

    return on_device


def solution(mesh):
    ranks = mesh.shape["tensor"]
    cores = 2
    chips = mesh.shape["dp"] // cores
    split = Mesh(mesh.devices.reshape(chips, cores, ranks), ("chip", "core", "tensor"))
    dp = ("chip", "core")
    rows = P(dp, "tensor", None)
    last = P(None, None, "tensor")
    first = P("tensor", None)
    return jax.shard_map(
        make(chips, cores, ranks),
        mesh=split,
        in_specs=(rows, P(dp, None), P(), last, first, P(), last, first, rows),
        out_specs=(rows, rows, P(), last, first, P(), last, first),
        check_vma=False,
    )
```

```python
import math

import jax
import jax.numpy as jnp
from jax import lax
from jax.experimental import pallas as pl
from jax.experimental.pallas import tpu as pltpu
from jax.sharding import Mesh, PartitionSpec as P

HD = 64
EPSILON = 1e-05
ROPE_BASE = 160000.0
BF = jnp.bfloat16
F32 = jnp.float32


def normalize(values):
    centered = values - jnp.mean(values, axis=-1, keepdims=True)
    variance = jnp.mean(centered * centered, axis=-1, keepdims=True)
    inverse = lax.rsqrt(variance + EPSILON)
    return (centered * inverse, inverse)


def norm_back(grad, normal, inverse, gain):
    scaled = grad * gain
    return inverse * (
        scaled
        - jnp.mean(scaled, axis=-1, keepdims=True)
        - normal * jnp.mean(scaled * normal, axis=-1, keepdims=True)
    )


def nt(left, right):
    return lax.dot_general(left, right, (((1,), (1,)), ((), ())), preferred_element_type=F32)


def nn(left, right):
    return jnp.dot(left, right, preferred_element_type=F32)


def tn(left, right):
    return lax.dot_general(left, right, (((0,), (0,)), ((), ())), preferred_element_type=F32)


def swap_halves(values):
    lane = lax.broadcasted_iota(jnp.int32, values.shape, 1)
    width = values.shape[1]
    ahead = pltpu.roll(values, width - HD // 2, 1)
    behind = pltpu.roll(values, HD // 2, 1)
    return jnp.where(lane % HD < HD // 2, ahead, behind)


def project_kernel(ranks, rank_ref, *refs):
    own_ref, *came = refs[: 2 * ranks - 1]
    w_ref, cos_ref, sin_ref, n_ref, q_ref, k_ref, v_ref = refs[2 * ranks - 1 :]
    ups, downs = came[: ranks - 1], came[ranks - 1 :]
    step = pl.program_id(0)

    @pl.when(step == 0)
    def _():
        n_ref[...] = own_ref[...]

    for k in range(1, ranks):
        below = rank_ref[0] + k < ranks

        @pl.when((step == k) & below)
        def _():
            n_ref[...] = downs[k - 1][...]

        @pl.when((step == k) & jnp.logical_not(below))
        def _():
            n_ref[...] = ups[ranks - k - 1][...]

    rows = n_ref[...]
    cos, sin = cos_ref[...], sin_ref[...]
    for c, out in ((0, q_ref), (1, k_ref), (2, v_ref)):
        wide = nn(rows, w_ref[c])
        if c == 2:
            out[...] = wide.astype(BF)
            continue
        for at in range(0, wide.shape[1], 128):
            part = wide[:, at : at + 128]
            turned = (part * cos + swap_halves(part) * sin).astype(BF)
            if c == 0:
                turned = turned * (1.0 / math.sqrt(HD))
            out[:, at : at + 128] = turned


def project(rank, own, ups, downs, weight, cos, sin):
    block, width = own.shape
    ranks = len(ups) + 1
    length = ranks * block
    cols = weight.shape[2]
    return pl.pallas_call(
        lambda *refs: project_kernel(ranks, *refs),
        grid=(ranks,),
        in_specs=[pl.BlockSpec(memory_space=pltpu.SMEM)]
        + [pl.BlockSpec((block, width), lambda i: (0, 0))] * (2 * ranks - 1)
        + [
            pl.BlockSpec((3, width, cols), lambda i: (0, 0, 0)),
            pl.BlockSpec((block, 128), lambda i: (i, 0)),
            pl.BlockSpec((block, 128), lambda i: (i, 0)),
        ],
        out_specs=[pl.BlockSpec((block, width), lambda i: (i, 0))]
        + [pl.BlockSpec((block, cols), lambda i: (i, 0))] * 3,
        out_shape=[jax.ShapeDtypeStruct((length, width), BF)]
        + [jax.ShapeDtypeStruct((length, cols), BF)] * 3,
        compiler_params=pltpu.CompilerParams(vmem_limit_bytes=40 * 2**20),
        cost_estimate=pl.CostEstimate(
            flops=6 * length * width * cols, bytes_accessed=9 * 2**20, transcendentals=0
        ),
    )(rank, own, *ups, *downs, weight, cos, sin)


def half_mask(values, half):
    lane = lax.broadcasted_iota(jnp.int32, values.shape, 1)
    return jnp.where((lane // HD) == half, values, jnp.zeros_like(values))


def row_blocks(count):
    at = 0
    while at < count:
        size = min(256, count - at)
        yield at, size
        at += size


def turn(value, by):
    return pltpu.roll(value.astype(F32), by, 0)


def attend_kernel(doc, by_ref, q_ref, k_ref, v_ref, o_ref, l_ref, qd_ref, kd_ref, vd_ref, od_ref):
    length = q_ref.shape[0]
    into = lax.rem(length - by_ref[0], length)
    qd_ref[...] = turn(q_ref[...], into).astype(BF)
    kd_ref[...] = turn(k_ref[...], into).astype(BF)
    values = turn(v_ref[...], into)
    vd_ref[...] = values.astype(BF)
    od_ref[doc:, :] = values[doc:, :]
    keys = kd_ref[:doc, :]
    values_t = values[:doc, :].T.astype(BF)
    for at, size in row_blocks(doc):
        queries = qd_ref[at : at + size, :]
        mixed = []
        for half in range(2):
            scores = nt(keys, half_mask(queries, half))
            largest = jnp.max(scores, axis=0, keepdims=True)
            weights = jnp.exp(scores - largest)
            total = jnp.sum(weights, axis=0, keepdims=True)
            mix = nn(values_t[half * HD : half * HD + HD], weights.astype(BF))
            mixed.append(mix * (1.0 / total))
            l_ref[0, half : half + 1, at : at + size] = largest + jnp.log(total)
        od_ref[at : at + size, :] = jnp.concatenate(mixed, axis=0).T
    o_ref[...] = turn(od_ref[...], by_ref[0]).astype(BF)


def attend(by, queries, keys, values, doc):
    length, cols = queries.shape
    pairs = cols // 128
    spec = pl.BlockSpec((length, 128), lambda p: (0, p))
    return pl.pallas_call(
        lambda *refs: attend_kernel(doc, *refs),
        grid=(pairs,),
        in_specs=[pl.BlockSpec(memory_space=pltpu.SMEM)] + [spec] * 3,
        out_specs=[spec, pl.BlockSpec((1, 2, doc), lambda p: (p, 0, 0))] + [spec] * 3,
        out_shape=[
            jax.ShapeDtypeStruct((length, cols), BF),
            jax.ShapeDtypeStruct((pairs, 2, doc), F32),
        ]
        + [jax.ShapeDtypeStruct((length, cols), BF)] * 3,
        scratch_shapes=[pltpu.VMEM((length, 128), F32)],
        compiler_params=pltpu.CompilerParams(vmem_limit_bytes=48 * 2**20),
        cost_estimate=pl.CostEstimate(
            flops=8 * doc * doc * cols, bytes_accessed=2 * 2**20, transcendentals=doc * doc * 4
        ),
    )(by, queries, keys, values)


def attend_back_kernel(
    doc, by_ref, q_ref, k_ref, v_ref, d_ref, l_ref, cos_ref, sin_ref,
    dq_ref, dk_ref, dv_ref, qa_ref, ka_ref, va_ref, dd_ref,
):
    length = q_ref.shape[0]
    into = lax.rem(length - by_ref[0], length)
    turned = turn(d_ref[...], into)
    dd_ref[...] = turned.astype(BF)
    zero = jnp.zeros((length - doc, 128), F32)
    qa_ref[doc:, :] = zero
    ka_ref[doc:, :] = zero
    va_ref[doc:, :] = turned[doc:, :]
    keys = k_ref[:doc, :]
    keys_t = keys.T
    values = v_ref[:doc, :]
    first = True
    for at, size in row_blocks(doc):
        queries = q_ref[at : at + size, :]
        grads = dd_ref[at : at + size, :]
        back = []
        for half in range(2):
            query = half_mask(queries, half)
            grad = half_mask(grads, half)
            probs = jnp.exp(nt(keys, query) - l_ref[0, half : half + 1, at : at + size])
            prob_grad = nt(values, grad)
            centre = jnp.sum(probs * prob_grad, axis=0, keepdims=True)
            score_grad = (probs * (prob_grad - centre)).astype(BF)
            value_part = nn(probs.astype(BF), grad)
            key_part = nn(score_grad, query)
            if first:
                va_ref[:doc, :] = value_part
                ka_ref[:doc, :] = key_part
                first = False
            else:
                va_ref[:doc, :] += value_part
                ka_ref[:doc, :] += key_part
            back.append(nn(keys_t[half * HD : half * HD + HD], score_grad))
        qa_ref[at : at + size, :] = jnp.concatenate(back, axis=0).T * (1.0 / math.sqrt(HD))
    cos, sin = cos_ref[...], sin_ref[...]
    for held, out in ((qa_ref, dq_ref), (ka_ref, dk_ref)):
        grad = turn(held[...], by_ref[0])
        out[...] = (grad * cos - swap_halves(grad) * sin).astype(BF)
    dv_ref[...] = turn(va_ref[...], by_ref[0]).astype(BF)


def attend_back(by, queries, keys, values, grads, logs, cos, sin, doc):
    length, cols = queries.shape
    pairs = cols // 128
    spec = pl.BlockSpec((length, 128), lambda p: (0, p))
    table = pl.BlockSpec((length, 128), lambda p: (0, 0))
    return pl.pallas_call(
        lambda *refs: attend_back_kernel(doc, *refs),
        grid=(pairs,),
        in_specs=[pl.BlockSpec(memory_space=pltpu.SMEM)]
        + [spec] * 4
        + [pl.BlockSpec((1, 2, doc), lambda p: (p, 0, 0))]
        + [table] * 2,
        out_specs=[spec] * 3,
        out_shape=[jax.ShapeDtypeStruct((length, cols), BF)] * 3,
        scratch_shapes=[pltpu.VMEM((length, 128), F32)] * 3 + [pltpu.VMEM((length, 128), BF)],
        compiler_params=pltpu.CompilerParams(vmem_limit_bytes=48 * 2**20),
        cost_estimate=pl.CostEstimate(
            flops=0, bytes_accessed=2**20, transcendentals=0
        ),
    )(by, queries, keys, values, grads, logs, cos, sin)


def feed_kernel(
    sizes, n_ref, c_ref, own_ref, gate_ref, rest_ref,
    dg_ref, du_ref, dd_ref, in_ref, in_other_ref, out_ref, out_other_ref, in_held, out_held,
):
    piece, out_piece, ranks, group, steps = sizes
    step = pl.program_id(0)

    def join(m, ref, first):
        rows = []
        for j in range(group):
            rows.append(own_ref[j, m].astype(F32))
            for k in range(ranks - 1):
                rows.append(ref[j, k].astype(F32)[first : first + piece])
        return jnp.concatenate(rows).astype(BF)

    gate = join(0, gate_ref, 0)
    up = join(1, rest_ref, 0)
    down = join(2, rest_ref, piece + out_piece)
    normed, cot = n_ref[...], c_ref[...]
    gate_proj = nt(normed, gate)
    up_proj = nt(normed, up)
    hid_grad = nt(cot, down)
    cdf = 0.5 * (1.0 + lax.erf(gate_proj * (1.0 / math.sqrt(2.0))))
    pdf = jnp.exp(-0.5 * gate_proj * gate_proj) * (1.0 / math.sqrt(2.0 * math.pi))
    act = gate_proj * cdf
    hid = (act * up_proj).astype(BF)
    gate_grad = (hid_grad * up_proj * (cdf + gate_proj * pdf)).astype(BF)
    up_grad = (hid_grad * act).astype(BF)
    for ref, left, right in ((dg_ref, gate_grad, normed), (du_ref, up_grad, normed), (dd_ref, hid, cot)):
        ref[...] = tn(left, right).astype(BF).reshape(ref.shape)
    in_part = nn(gate_grad, gate) + nn(up_grad, up)
    out_part = nn(hid, down)

    @pl.when(step == 0)
    def _():
        in_held[...] = in_part
        out_held[...] = out_part

    @pl.when(step > 0)
    def _():
        in_held[...] += in_part
        out_held[...] += out_part

    @pl.when(step == steps - 1)
    def _():
        rows = in_ref.shape[0]
        in_ref[...] = in_held[:rows, :]
        in_other_ref[...] = in_held[rows:, :].astype(BF)
        out_ref[...] = out_held[:rows, :]
        out_other_ref[...] = out_held[rows:, :].astype(BF)


def feed(normed, cot, own, gate_all, rest_all, piece, out_piece):
    rows, width = normed.shape
    chips, others, rest_rows = rest_all.shape[:3]
    hidden = (others + 1) * piece
    half = rows // 2
    group = 1
    same = pl.BlockSpec((rows, width), lambda i: (0, 0))
    grad = pl.BlockSpec((group, hidden, width), lambda i: (i, 0, 0))
    kept = pl.BlockSpec((half, width), lambda i: (0, 0))
    sizes = (piece, out_piece, others + 1, group, chips // group)
    return pl.pallas_call(
        lambda *refs: feed_kernel(sizes, *refs),
        grid=(chips // group,),
        in_specs=[
            same,
            same,
            pl.BlockSpec((group, 3, piece, width), lambda i: (i, 0, 0, 0)),
            pl.BlockSpec((group, others, piece, width), lambda i: (i, 0, 0, 0)),
            pl.BlockSpec((group, others, rest_rows, width), lambda i: (i, 0, 0, 0)),
        ],
        out_specs=[grad] * 3 + [kept] * 4,
        out_shape=[jax.ShapeDtypeStruct((chips, hidden, width), BF)] * 3
        + [
            jax.ShapeDtypeStruct((half, width), F32),
            jax.ShapeDtypeStruct((half, width), BF),
            jax.ShapeDtypeStruct((half, width), F32),
            jax.ShapeDtypeStruct((half, width), BF),
        ],
        scratch_shapes=[pltpu.VMEM((rows, width), F32)] * 2,
        compiler_params=pltpu.CompilerParams(vmem_limit_bytes=62 * 2**20),
        cost_estimate=pl.CostEstimate(
            flops=18 * rows * width * hidden * chips,
            bytes_accessed=25 * 2**20,
            transcendentals=2 * rows * hidden * chips,
        ),
    )(normed, cot, own, gate_all, rest_all)


def assemble_kernel(sizes, in_ref, gu_ref, d_ref, o_ref, qkv_ref, held):
    cores, chips, share, per, piece, out_piece, qkv_part = sizes
    hidden = cores * share
    firsts = (0, piece, 2 * piece + out_piece)
    for m, first in enumerate(firsts):
        for device in range(cores * chips):
            at = device // chips * share + device % chips * per
            rows = in_ref[device].astype(F32)
            held[at : at + piece, :] = rows[first : first + piece, :]
            if m == 0:
                o_ref[device] = rows[2 * piece : 2 * piece + out_piece, :]
                last = 3 * piece + out_piece + 8
                for c in range(3):
                    start = last + c * qkv_part
                    qkv_ref[c, device, 0] = rows[start : start + qkv_part, :]
        if m == 2:
            d_ref[...] = held[:hidden, :]
        else:
            gu_ref[m] = held[:hidden, :]


def assemble(every, sizes):
    cores, chips, share, per, piece, out_piece, qkv_part = sizes
    devices, rows, width = every.shape
    hidden = cores * share
    block = 256
    groups = width // block
    tall = -(-((cores - 1) * share + (chips - 1) * per + piece) // 8) * 8
    return pl.pallas_call(
        lambda *refs: assemble_kernel(sizes, *refs),
        grid=(groups,),
        in_specs=[pl.BlockSpec((devices, rows, block), lambda i: (0, 0, i))],
        out_specs=[
            pl.BlockSpec((2, hidden, block), lambda i: (0, 0, i)),
            pl.BlockSpec((hidden, block), lambda i: (0, i)),
            pl.BlockSpec((devices, out_piece, block), lambda i: (0, 0, i)),
            pl.BlockSpec((3, devices, 1, qkv_part, block), lambda i: (0, 0, i, 0, 0)),
        ],
        out_shape=[
            jax.ShapeDtypeStruct((2, hidden, width), F32),
            jax.ShapeDtypeStruct((hidden, width), F32),
            jax.ShapeDtypeStruct((devices, out_piece, width), F32),
            jax.ShapeDtypeStruct((3, devices, groups, qkv_part, block), F32),
        ],
        scratch_shapes=[pltpu.VMEM((tall, block), F32)],
        compiler_params=pltpu.CompilerParams(vmem_limit_bytes=60 * 2**20),
        cost_estimate=pl.CostEstimate(flops=0, bytes_accessed=18 * 2**20, transcendentals=0),
    )(every)


def shift(value, by, count):
    return lax.ppermute(value, "tensor", [(i, (i + by) % count) for i in range(count)])


def flip(value, axis, bit, count):
    return lax.ppermute(value, axis, [(i, i ^ bit) for i in range(count)])


def relay_ranks(value, count):
    ups, downs = [value], [value]
    for step in range(1, count):
        ups.append(lax.ppermute(ups[-1], "tensor", [(z, z + 1) for z in range(step - 1, count - 1)]))
        downs.append(lax.ppermute(downs[-1], "tensor", [(z, z - 1) for z in range(1, count - step + 1)]))
    return ups[1:], downs[1:]


def scatter_ranks(blocks, count):
    up, down = blocks[count - 1], blocks[1]
    for step in range(1, count):
        up = lax.ppermute(up, "tensor", [(z, z + 1) for z in range(step)])
        down = lax.ppermute(down, "tensor", [(z, z - 1) for z in range(count - step, count)])
        if step < count - 1:
            up = (up.astype(F32) + blocks[count - 1 - step].astype(F32)).astype(BF)
            down = (down.astype(F32) + blocks[step + 1].astype(F32)).astype(BF)
    return blocks[0].astype(F32) + up.astype(F32) + down.astype(F32)


class Halving:
    def __init__(self, value, chip, count, turned):
        self.chip, self.count, self.came = chip, count, None
        self.bits = count.bit_length() - 1
        self.held = value.reshape((2,) * self.bits + (-1,) + value.shape[-1:])
        order = list(range(self.bits))
        self.order = order if turned else order[::-1]
        self.left = list(range(self.bits))

    def send(self):
        axis = self.order.pop(0)
        bit = self.bits - 1 - axis
        mine = (self.chip >> bit) & 1
        at = self.left.index(axis)
        self.left.remove(axis)
        self.kept = lax.dynamic_index_in_dim(self.held, mine, at, keepdims=False)
        sent = lax.dynamic_index_in_dim(self.held, 1 - mine, at, keepdims=False)
        self.came = flip(sent, "chip", 1 << bit, self.count)

    def take(self):
        self.held = (self.kept.astype(F32) + self.came.astype(F32)).astype(BF)
        self.came = None

    def finish(self):
        if self.came is not None:
            self.take()
        while self.order:
            self.send()
            self.take()
        return self.held


def tie(value, sums):
    tied = lax.optimization_barrier((value, *(s.came for s in sums)))
    for s, came in zip(sums, tied[1:]):
        s.came = came
        s.take()
    return tied[0]


def make(chips, cores, ranks):
    def on_device(
        tokens,
        segment_ids,
        gain_attn,
        query_key_value_weight,
        output_weight,
        gain_mlp,
        gate_up_weight,
        down_weight,
        cotangent,
    ):
        length = segment_ids.shape[1]
        own_rows, width = tokens.shape[1:]
        doc = length - length // 8
        others = ranks - 1
        rank = lax.axis_index("tensor")
        core = lax.axis_index("core")
        chip = lax.axis_index("chip")
        hold = lax.optimization_barrier

        hidden = down_weight.shape[0]
        share = hidden // cores
        per = -(-share // chips)
        piece = -(-per // 8) * 8
        heads_rows = output_weight.shape[0]
        out_piece = heads_rows // (cores * chips)
        gate_t, up_t = jnp.swapaxes(gate_up_weight, 1, 2)

        def part(weight, j):
            padded = jnp.pad(weight, ((0, chips * per + piece - share), (0, 0)))
            rows = lax.dynamic_slice_in_dim(padded, core * share + j * per, piece)
            at = lax.broadcasted_iota(jnp.int32, rows.shape, 0)
            return jnp.where((at < per) & (j * per + at < share), rows, jnp.zeros_like(rows))

        gate_mine = part(gate_t, chip)
        out_mine = lax.dynamic_slice_in_dim(
            output_weight, (core * chips + chip) * out_piece, out_piece
        )
        rest_mine = jnp.concatenate([part(up_t, chip), out_mine, part(down_weight, chip)])

        gate_came = jnp.concatenate([shift(gate_mine, -k, ranks) for k in range(1, ranks)])
        token_f = tokens[0].astype(F32)
        normal_attn, inverse_attn = normalize(token_f)
        normed_attn = (normal_attn * gain_attn).astype(BF)
        rest_sent, gate_came = hold((rest_mine, gate_came))
        gate_all = lax.all_gather(gate_came, "chip").reshape(chips, others, piece, width)
        ups, downs = relay_ranks(rest_sent, ranks)
        rest_came = jnp.concatenate([downs[k] + ups[others - 1 - k] for k in range(others)])
        normed_sent, rest_came = hold((normed_attn, rest_came))
        rest_all = lax.all_gather(rest_came, "chip").reshape(chips, others, -1, width)
        normed_ups, normed_downs = relay_ranks(normed_sent, ranks)
        own = jnp.stack(
            [jnp.stack([part(w, j) for w in (gate_t, up_t, down_weight)]) for j in range(chips)]
        )

        segments = segment_ids[0]
        middle = segments[length // 2]
        start = jnp.sum((segments < middle).astype(jnp.int32))
        by = (start - rank * own_rows) % length
        places = (jnp.arange(length, dtype=jnp.int32) - by) % length
        places = jnp.where(places < doc, places, 0)
        half = HD // 2
        freq = jnp.exp(jnp.arange(half, dtype=F32) * (-2.0 * math.log(ROPE_BASE) / HD))
        angles = places.astype(F32)[:, None] * jnp.concatenate([freq] * 4)[None, :]
        cos_table = jnp.cos(angles)
        lane = jnp.arange(2 * HD, dtype=jnp.int32)
        sin_table = jnp.sin(angles) * jnp.where(lane % HD < half, -1.0, 1.0)
        by = by[None]

        cot = cotangent[0]
        cot_pair = jnp.concatenate([cot, flip(cot, "core", 1, cores)])
        normed_attn, cos_table, sin_table, cot_pair, own = hold(
            (normed_attn, cos_table, sin_table, cot_pair, own)
        )

        normed_rows, queries, keys, values = project(
            rank[None],
            normed_attn,
            normed_ups,
            normed_downs,
            query_key_value_weight,
            cos_table,
            sin_table,
        )
        mixture, logs, queries, keys, values = attend(by, queries, keys, values, doc)
        mixture = mixture.reshape(ranks, own_rows, heads_rows)
        attention = jnp.concatenate(
            [mixture[0]] + [shift(mixture[k], k, ranks) for k in range(1, ranks)], axis=1
        )
        attention, gate_all, rest_all = hold((attention, gate_all, rest_all))

        out_half = jnp.swapaxes(rest_all[:, :, piece : piece + out_piece], 0, 1)
        out_half = out_half.reshape(others, heads_rows // cores, width)
        out_other = flip(out_half, "core", 1, cores)
        out_rest = jnp.concatenate(
            [
                jnp.where(core == 0, out_half, out_other),
                jnp.where(core == 0, out_other, out_half),
            ],
            axis=1,
        )
        out_weight = jnp.concatenate(
            [output_weight] + [out_rest[others - k] for k in range(1, ranks)]
        )
        hidden_state = token_f + nn(attention, out_weight)
        normal_mlp, inverse_mlp = normalize(hidden_state)
        normed_mlp = (normal_mlp * gain_mlp).astype(BF)
        normed_pair = jnp.concatenate([normed_mlp, flip(normed_mlp, "core", 1, cores)])
        gate_w_grad, up_w_grad, down_grad, in_part, in_other, mlp_part, mlp_other = feed(
            normed_pair, cot_pair, own, gate_all, rest_all, piece, out_piece
        )
        gate_sum = Halving(gate_w_grad, chip, chips, False)
        up_sum = Halving(up_w_grad, chip, chips, True)
        gate_sum.send()
        up_sum.send()
        normed_mlp_grad = in_part + flip(in_other, "core", 1, cores).astype(F32)
        gain_mlp_part = jnp.sum(normed_mlp_grad * normal_mlp, axis=0)
        hidden_grad = cot.astype(F32) + norm_back(
            normed_mlp_grad, normal_mlp, inverse_mlp, gain_mlp
        )
        branch_grad = hidden_grad.astype(BF)

        attended_grad = nt(branch_grad, out_weight).astype(BF)
        attended_came = [
            shift(attended_grad[:, k * heads_rows : (k + 1) * heads_rows], -k, ranks)
            for k in range(1, ranks)
        ]
        mlp_out = mlp_part + flip(mlp_other, "core", 1, cores).astype(F32)
        layer_out = (hidden_state + mlp_out).astype(BF)

        def sum_cores(value, axis):
            kept = lax.dynamic_index_in_dim(value, core, axis, keepdims=False)
            sent = lax.dynamic_index_in_dim(value, 1 - core, axis, keepdims=False)
            return (kept.astype(F32) + flip(sent, "core", 1, cores).astype(F32)).astype(BF)

        out_w_grad = tn(attention, branch_grad).astype(BF)
        out_blocks = out_w_grad.reshape(ranks, cores, chips, out_piece, width)
        out_blocks = jnp.stack([out_blocks[(ranks - k) % ranks] for k in range(ranks)])
        out_blocks = jnp.swapaxes(sum_cores(out_blocks, 1), 0, 1)
        cut = ranks * piece // 2
        down_sums = [
            Halving(down_grad[:, :cut], chip, chips, False),
            Halving(down_grad[:, cut:], chip, chips, True),
        ]
        attended_rows = jnp.concatenate([attended_grad[:, :heads_rows]] + attended_came)
        attended_rows, layer_out, out_blocks = hold((attended_rows, layer_out, out_blocks))

        def in_rank_order(here):
            rows = here.shape[1]
            flat = here.reshape(ranks * rows, width)
            twice = jnp.concatenate([flat, flat])
            return lax.dynamic_slice_in_dim(twice, (ranks - rank) % ranks * rows, ranks * rows)

        sums = [Halving(out_blocks, chip, chips, True)] + down_sums
        for s in sums:
            s.send()
        dq, dk, dv = attend_back(
            by, queries, keys, values, attended_rows, logs, cos_table, sin_table, doc
        )
        dq = tie(dq, [gate_sum, up_sum])
        gate_sum.send()
        up_sum.send()
        normed_attn_part = (
            nt(dq, query_key_value_weight[0])
            + nt(dk, query_key_value_weight[1])
            + nt(dv, query_key_value_weight[2])
        )
        gain_attn_part = jnp.sum(normed_attn_part * normed_rows.astype(F32), axis=0) / gain_attn
        part_rows = normed_attn_part.astype(BF).reshape(ranks, own_rows, width)
        qkv_grad = jnp.stack([tn(normed_rows, g) for g in (dq, dk, dv)]).astype(BF)
        part_rows, qkv_grad, gain_attn_part = hold((part_rows, qkv_grad, gain_attn_part))
        gate_up_here = in_rank_order(
            jnp.concatenate(
                [
                    gate_sum.finish().reshape(ranks, piece, width),
                    up_sum.finish().reshape(ranks, piece, width),
                ],
                axis=1,
            )
        )
        gate_up_total = lax.psum_scatter(gate_up_here, "tensor", scatter_dimension=0, tiled=True)
        tie(gate_up_here, sums)
        gain_rows = jnp.pad(jnp.stack([gain_attn_part, gain_mlp_part]), ((0, 6), (0, 0))).astype(BF)
        out_here = sums[0].finish().reshape(ranks, out_piece, width)
        down_here = jnp.concatenate([s.finish() for s in sums[1:]]).reshape(ranks, piece, width)
        rest_total = scatter_ranks(
            [jnp.concatenate([out_here[k], down_here[k], gain_rows]) for k in range(ranks)], ranks
        ).astype(BF)
        normed_attn_grad = scatter_ranks(part_rows, ranks)
        input_grad = (
            hidden_grad + norm_back(normed_attn_grad, normal_attn, inverse_attn, gain_attn)
        ).astype(BF)

        qkv_rows = width // (cores * chips)
        qkv_blocks = qkv_grad.reshape(3, cores, chips, qkv_rows, heads_rows)
        qkv_blocks = jnp.swapaxes(sum_cores(qkv_blocks, 1), 0, 1)
        qkv_here = Halving(qkv_blocks, chip, chips, False).finish()
        groups = width // heads_rows
        qkv_part = qkv_rows // groups
        qkv_here = qkv_here.reshape(3, groups, qkv_part, heads_rows)
        qkv_here = jnp.concatenate(
            [qkv_here[:, g].reshape(3 * qkv_part, heads_rows) for g in range(groups)], axis=1
        )
        pieces = jnp.concatenate([gate_up_total, rest_total, qkv_here])
        every = lax.all_gather(pieces, ("core", "chip"))
        grads = assemble(every, (cores, chips, share, per, piece, out_piece, qkv_part))
        at = 3 * piece + out_piece
        grad_gain_attn, grad_gain_mlp = jnp.sum(every[:, at : at + 2].astype(F32), axis=0)
        grad_gateup = jnp.swapaxes(grads[0], 1, 2)
        down_weight_gradient = grads[1]
        output_weight_gradient = grads[2].reshape(heads_rows, width)
        query_key_value_gradient = grads[3].reshape(3, width, heads_rows)
        return (
            layer_out[None],
            input_grad[None],
            grad_gain_attn,
            query_key_value_gradient,
            output_weight_gradient,
            grad_gain_mlp,
            grad_gateup,
            down_weight_gradient,
        )

    return on_device


def solution(mesh):
    ranks = mesh.shape["tensor"]
    cores = 2
    chips = mesh.shape["dp"] // cores
    split = Mesh(mesh.devices.reshape(chips, cores, ranks), ("chip", "core", "tensor"))
    dp = ("chip", "core")
    rows = P(dp, "tensor", None)
    last = P(None, None, "tensor")
    first = P("tensor", None)
    return jax.shard_map(
        make(chips, cores, ranks),
        mesh=split,
        in_specs=(rows, P(dp, None), P(), last, first, P(), last, first, rows),
        out_specs=(rows, rows, P(), last, first, P(), last, first),
        check_vma=False,
    )
```

```python
import math

import jax
import jax.numpy as jnp
from jax import lax
from jax.experimental import pallas as pl
from jax.experimental.pallas import tpu as pltpu
from jax.sharding import Mesh, PartitionSpec as P

HD = 64
EPSILON = 1e-05
ROPE_BASE = 160000.0
BF = jnp.bfloat16
F32 = jnp.float32


def normalize(values):
    centered = values - jnp.mean(values, axis=-1, keepdims=True)
    variance = jnp.mean(centered * centered, axis=-1, keepdims=True)
    inverse = lax.rsqrt(variance + EPSILON)
    return (centered * inverse, inverse)


def norm_back(grad, normal, inverse, gain):
    scaled = grad * gain
    return inverse * (
        scaled
        - jnp.mean(scaled, axis=-1, keepdims=True)
        - normal * jnp.mean(scaled * normal, axis=-1, keepdims=True)
    )


def nt(left, right):
    return lax.dot_general(left, right, (((1,), (1,)), ((), ())), preferred_element_type=F32)


def nn(left, right):
    return jnp.dot(left, right, preferred_element_type=F32)


def tn(left, right):
    return lax.dot_general(left, right, (((0,), (0,)), ((), ())), preferred_element_type=F32)


def swap_halves(values):
    lane = lax.broadcasted_iota(jnp.int32, values.shape, 1)
    width = values.shape[1]
    ahead = pltpu.roll(values, width - HD // 2, 1)
    behind = pltpu.roll(values, HD // 2, 1)
    return jnp.where(lane % HD < HD // 2, ahead, behind)


def project_kernel(ranks, rank_ref, *refs):
    own_ref, *came = refs[: 2 * ranks - 1]
    w_ref, cos_ref, sin_ref, n_ref, q_ref, k_ref, v_ref = refs[2 * ranks - 1 :]
    ups, downs = came[: ranks - 1], came[ranks - 1 :]
    step = pl.program_id(0)

    @pl.when(step == 0)
    def _():
        n_ref[...] = own_ref[...]

    for k in range(1, ranks):
        below = rank_ref[0] + k < ranks

        @pl.when((step == k) & below)
        def _():
            n_ref[...] = downs[k - 1][...]

        @pl.when((step == k) & jnp.logical_not(below))
        def _():
            n_ref[...] = ups[ranks - k - 1][...]

    rows = n_ref[...]
    cos, sin = cos_ref[...], sin_ref[...]
    for c, out in ((0, q_ref), (1, k_ref), (2, v_ref)):
        wide = nn(rows, w_ref[c])
        if c == 2:
            out[...] = wide.astype(BF)
            continue
        for at in range(0, wide.shape[1], 128):
            part = wide[:, at : at + 128]
            turned = (part * cos + swap_halves(part) * sin).astype(BF)
            if c == 0:
                turned = turned * (1.0 / math.sqrt(HD))
            out[:, at : at + 128] = turned


def project(rank, own, ups, downs, weight, cos, sin):
    block, width = own.shape
    ranks = len(ups) + 1
    length = ranks * block
    cols = weight.shape[2]
    return pl.pallas_call(
        lambda *refs: project_kernel(ranks, *refs),
        grid=(ranks,),
        in_specs=[pl.BlockSpec(memory_space=pltpu.SMEM)]
        + [pl.BlockSpec((block, width), lambda i: (0, 0))] * (2 * ranks - 1)
        + [
            pl.BlockSpec((3, width, cols), lambda i: (0, 0, 0)),
            pl.BlockSpec((block, 128), lambda i: (i, 0)),
            pl.BlockSpec((block, 128), lambda i: (i, 0)),
        ],
        out_specs=[pl.BlockSpec((block, width), lambda i: (i, 0))]
        + [pl.BlockSpec((block, cols), lambda i: (i, 0))] * 3,
        out_shape=[jax.ShapeDtypeStruct((length, width), BF)]
        + [jax.ShapeDtypeStruct((length, cols), BF)] * 3,
        compiler_params=pltpu.CompilerParams(vmem_limit_bytes=40 * 2**20),
        cost_estimate=pl.CostEstimate(
            flops=6 * length * width * cols, bytes_accessed=9 * 2**20, transcendentals=0
        ),
    )(rank, own, *ups, *downs, weight, cos, sin)


def half_mask(values, half):
    lane = lax.broadcasted_iota(jnp.int32, values.shape, 1)
    return jnp.where((lane // HD) == half, values, jnp.zeros_like(values))


def row_blocks(count):
    at = 0
    while at < count:
        size = min(256, count - at)
        yield at, size
        at += size


def turn(value, by):
    return pltpu.roll(value.astype(F32), by, 0)


def attend_kernel(doc, by_ref, q_ref, k_ref, v_ref, o_ref, l_ref, qd_ref, kd_ref, vd_ref, od_ref):
    length = q_ref.shape[0]
    into = lax.rem(length - by_ref[0], length)
    qd_ref[...] = turn(q_ref[...], into).astype(BF)
    kd_ref[...] = turn(k_ref[...], into).astype(BF)
    values = turn(v_ref[...], into)
    vd_ref[...] = values.astype(BF)
    od_ref[doc:, :] = values[doc:, :]
    keys = kd_ref[:doc, :]
    values_t = values[:doc, :].T.astype(BF)
    for at, size in row_blocks(doc):
        queries = qd_ref[at : at + size, :]
        mixed = []
        for half in range(2):
            scores = nt(keys, half_mask(queries, half))
            largest = jnp.max(scores, axis=0, keepdims=True)
            weights = jnp.exp(scores - largest)
            total = jnp.sum(weights, axis=0, keepdims=True)
            mix = nn(values_t[half * HD : half * HD + HD], weights.astype(BF))
            mixed.append(mix * (1.0 / total))
            l_ref[0, half : half + 1, at : at + size] = largest + jnp.log(total)
        od_ref[at : at + size, :] = jnp.concatenate(mixed, axis=0).T
    o_ref[...] = turn(od_ref[...], by_ref[0]).astype(BF)


def attend(by, queries, keys, values, doc):
    length, cols = queries.shape
    pairs = cols // 128
    spec = pl.BlockSpec((length, 128), lambda p: (0, p))
    return pl.pallas_call(
        lambda *refs: attend_kernel(doc, *refs),
        grid=(pairs,),
        in_specs=[pl.BlockSpec(memory_space=pltpu.SMEM)] + [spec] * 3,
        out_specs=[spec, pl.BlockSpec((1, 2, doc), lambda p: (p, 0, 0))] + [spec] * 3,
        out_shape=[
            jax.ShapeDtypeStruct((length, cols), BF),
            jax.ShapeDtypeStruct((pairs, 2, doc), F32),
        ]
        + [jax.ShapeDtypeStruct((length, cols), BF)] * 3,
        scratch_shapes=[pltpu.VMEM((length, 128), F32)],
        compiler_params=pltpu.CompilerParams(vmem_limit_bytes=48 * 2**20),
        cost_estimate=pl.CostEstimate(
            flops=8 * doc * doc * cols, bytes_accessed=2 * 2**20, transcendentals=doc * doc * 4
        ),
    )(by, queries, keys, values)


def attend_back_kernel(
    doc, by_ref, q_ref, k_ref, v_ref, d_ref, l_ref, cos_ref, sin_ref,
    dq_ref, dk_ref, dv_ref, qa_ref, ka_ref, va_ref, dd_ref,
):
    length = q_ref.shape[0]
    into = lax.rem(length - by_ref[0], length)
    turned = turn(d_ref[...], into)
    dd_ref[...] = turned.astype(BF)
    zero = jnp.zeros((length - doc, 128), F32)
    qa_ref[doc:, :] = zero
    ka_ref[doc:, :] = zero
    va_ref[doc:, :] = turned[doc:, :]
    keys = k_ref[:doc, :]
    keys_t = keys.T
    values = v_ref[:doc, :]
    first = True
    for at, size in row_blocks(doc):
        queries = q_ref[at : at + size, :]
        grads = dd_ref[at : at + size, :]
        back = []
        for half in range(2):
            query = half_mask(queries, half)
            grad = half_mask(grads, half)
            probs = jnp.exp(nt(keys, query) - l_ref[0, half : half + 1, at : at + size])
            prob_grad = nt(values, grad)
            centre = jnp.sum(probs * prob_grad, axis=0, keepdims=True)
            score_grad = (probs * (prob_grad - centre)).astype(BF)
            value_part = nn(probs.astype(BF), grad)
            key_part = nn(score_grad, query)
            if first:
                va_ref[:doc, :] = value_part
                ka_ref[:doc, :] = key_part
                first = False
            else:
                va_ref[:doc, :] += value_part
                ka_ref[:doc, :] += key_part
            back.append(nn(keys_t[half * HD : half * HD + HD], score_grad))
        qa_ref[at : at + size, :] = jnp.concatenate(back, axis=0).T * (1.0 / math.sqrt(HD))
    cos, sin = cos_ref[...], sin_ref[...]
    for held, out in ((qa_ref, dq_ref), (ka_ref, dk_ref)):
        grad = turn(held[...], by_ref[0])
        out[...] = (grad * cos - swap_halves(grad) * sin).astype(BF)
    dv_ref[...] = turn(va_ref[...], by_ref[0]).astype(BF)


def attend_back(by, queries, keys, values, grads, logs, cos, sin, doc):
    length, cols = queries.shape
    pairs = cols // 128
    spec = pl.BlockSpec((length, 128), lambda p: (0, p))
    table = pl.BlockSpec((length, 128), lambda p: (0, 0))
    return pl.pallas_call(
        lambda *refs: attend_back_kernel(doc, *refs),
        grid=(pairs,),
        in_specs=[pl.BlockSpec(memory_space=pltpu.SMEM)]
        + [spec] * 4
        + [pl.BlockSpec((1, 2, doc), lambda p: (p, 0, 0))]
        + [table] * 2,
        out_specs=[spec] * 3,
        out_shape=[jax.ShapeDtypeStruct((length, cols), BF)] * 3,
        scratch_shapes=[pltpu.VMEM((length, 128), F32)] * 3 + [pltpu.VMEM((length, 128), BF)],
        compiler_params=pltpu.CompilerParams(vmem_limit_bytes=48 * 2**20),
        cost_estimate=pl.CostEstimate(
            flops=0, bytes_accessed=2**20, transcendentals=0
        ),
    )(by, queries, keys, values, grads, logs, cos, sin)


def feed_kernel(
    sizes, n_ref, c_ref, own_ref, gate_ref, rest_ref,
    dgu_ref, dd_ref, in_ref, in_other_ref, out_ref, out_other_ref, in_held, out_held,
):
    piece, out_piece, ranks, group, steps = sizes
    step = pl.program_id(0)

    def join(m, ref, first):
        rows = []
        for j in range(group):
            rows.append(own_ref[j, m].astype(F32))
            for k in range(ranks - 1):
                rows.append(ref[j, k].astype(F32)[first : first + piece])
        return jnp.concatenate(rows).astype(BF)

    gate = join(0, gate_ref, 0)
    up = join(1, rest_ref, 0)
    down = join(2, rest_ref, piece + out_piece)
    normed, cot = n_ref[...], c_ref[...]
    gate_proj = nt(normed, gate)
    up_proj = nt(normed, up)
    hid_grad = nt(cot, down)
    cdf = 0.5 * (1.0 + lax.erf(gate_proj * (1.0 / math.sqrt(2.0))))
    pdf = jnp.exp(-0.5 * gate_proj * gate_proj) * (1.0 / math.sqrt(2.0 * math.pi))
    act = gate_proj * cdf
    hid = (act * up_proj).astype(BF)
    gate_grad = (hid_grad * up_proj * (cdf + gate_proj * pdf)).astype(BF)
    up_grad = (hid_grad * act).astype(BF)
    hidden = ranks * piece
    dgu_ref[0, :hidden] = tn(gate_grad, normed).astype(BF)
    dgu_ref[0, hidden:] = tn(up_grad, normed).astype(BF)
    down_grad = tn(hid, cot)
    for k in range(ranks):
        dd_ref[k, 0] = down_grad[k * piece : (k + 1) * piece].astype(BF)
    in_part = nn(gate_grad, gate) + nn(up_grad, up)
    out_part = nn(hid, down)

    @pl.when(step == 0)
    def _():
        in_held[...] = in_part
        out_held[...] = out_part

    @pl.when(step > 0)
    def _():
        in_held[...] += in_part
        out_held[...] += out_part

    @pl.when(step == steps - 1)
    def _():
        rows = in_ref.shape[0]
        in_ref[...] = in_held[:rows, :]
        in_other_ref[...] = in_held[rows:, :].astype(BF)
        out_ref[...] = out_held[:rows, :]
        out_other_ref[...] = out_held[rows:, :].astype(BF)


def feed(normed, cot, own, gate_all, rest_all, piece, out_piece):
    rows, width = normed.shape
    chips, others, rest_rows = rest_all.shape[:3]
    hidden = (others + 1) * piece
    half = rows // 2
    group = 1
    same = pl.BlockSpec((rows, width), lambda i: (0, 0))
    grads = [
        pl.BlockSpec((1, 2 * hidden, width), lambda i: (i, 0, 0)),
        pl.BlockSpec((others + 1, 1, piece, width), lambda i: (0, i, 0, 0)),
    ]
    kept = pl.BlockSpec((half, width), lambda i: (0, 0))
    sizes = (piece, out_piece, others + 1, group, chips // group)
    return pl.pallas_call(
        lambda *refs: feed_kernel(sizes, *refs),
        grid=(chips // group,),
        in_specs=[
            same,
            same,
            pl.BlockSpec((group, 3, piece, width), lambda i: (i, 0, 0, 0)),
            pl.BlockSpec((group, others, piece, width), lambda i: (i, 0, 0, 0)),
            pl.BlockSpec((group, others, rest_rows, width), lambda i: (i, 0, 0, 0)),
        ],
        out_specs=grads + [kept] * 4,
        out_shape=[
            jax.ShapeDtypeStruct((chips, 2 * hidden, width), BF),
            jax.ShapeDtypeStruct((others + 1, chips, piece, width), BF),
        ]
        + [
            jax.ShapeDtypeStruct((half, width), F32),
            jax.ShapeDtypeStruct((half, width), BF),
            jax.ShapeDtypeStruct((half, width), F32),
            jax.ShapeDtypeStruct((half, width), BF),
        ],
        scratch_shapes=[pltpu.VMEM((rows, width), F32)] * 2,
        compiler_params=pltpu.CompilerParams(vmem_limit_bytes=62 * 2**20),
        cost_estimate=pl.CostEstimate(
            flops=18 * rows * width * hidden * chips,
            bytes_accessed=25 * 2**20,
            transcendentals=2 * rows * hidden * chips,
        ),
    )(normed, cot, own, gate_all, rest_all)


def assemble_kernel(sizes, in_ref, gu_ref, d_ref, o_ref, qkv_ref, held):
    cores, chips, share, per, piece, out_piece, qkv_part = sizes
    hidden = cores * share
    firsts = (0, piece, 2 * piece + out_piece + 8)
    for m, first in enumerate(firsts):
        for device in range(cores * chips):
            at = device // chips * share + device % chips * per
            rows = in_ref[device].astype(F32)
            held[at : at + piece, :] = rows[first : first + piece, :]
            if m == 0:
                o_ref[device] = rows[2 * piece : 2 * piece + out_piece, :]
                last = 3 * piece + out_piece + 8
                for c in range(3):
                    start = last + c * qkv_part
                    qkv_ref[c, device, 0] = rows[start : start + qkv_part, :]
        if m == 2:
            d_ref[...] = held[:hidden, :]
        else:
            gu_ref[m] = held[:hidden, :]


def assemble(every, sizes):
    cores, chips, share, per, piece, out_piece, qkv_part = sizes
    devices, rows, width = every.shape
    hidden = cores * share
    block = 256
    groups = width // block
    tall = -(-((cores - 1) * share + (chips - 1) * per + piece) // 8) * 8
    return pl.pallas_call(
        lambda *refs: assemble_kernel(sizes, *refs),
        grid=(groups,),
        in_specs=[pl.BlockSpec((devices, rows, block), lambda i: (0, 0, i))],
        out_specs=[
            pl.BlockSpec((2, hidden, block), lambda i: (0, 0, i)),
            pl.BlockSpec((hidden, block), lambda i: (0, i)),
            pl.BlockSpec((devices, out_piece, block), lambda i: (0, 0, i)),
            pl.BlockSpec((3, devices, 1, qkv_part, block), lambda i: (0, 0, i, 0, 0)),
        ],
        out_shape=[
            jax.ShapeDtypeStruct((2, hidden, width), F32),
            jax.ShapeDtypeStruct((hidden, width), F32),
            jax.ShapeDtypeStruct((devices, out_piece, width), F32),
            jax.ShapeDtypeStruct((3, devices, groups, qkv_part, block), F32),
        ],
        scratch_shapes=[pltpu.VMEM((tall, block), F32)],
        compiler_params=pltpu.CompilerParams(vmem_limit_bytes=60 * 2**20),
        cost_estimate=pl.CostEstimate(flops=0, bytes_accessed=18 * 2**20, transcendentals=0),
    )(every)


def shift(value, by, count):
    return lax.ppermute(value, "tensor", [(i, (i + by) % count) for i in range(count)])


def flip(value, axis, bit, count):
    return lax.ppermute(value, axis, [(i, i ^ bit) for i in range(count)])


def relay_ranks(value, count):
    ups, downs = [value], [value]
    for step in range(1, count):
        ups.append(lax.ppermute(ups[-1], "tensor", [(z, z + 1) for z in range(step - 1, count - 1)]))
        downs.append(lax.ppermute(downs[-1], "tensor", [(z, z - 1) for z in range(1, count - step + 1)]))
    return ups[1:], downs[1:]


class LineSum:
    def __init__(self, blocks, count):
        self.blocks, self.count, self.step, self.came = blocks, count, 0, None
        self.up, self.down = blocks[count - 1], blocks[1]

    def send(self):
        self.step += 1
        up = [(z, z + 1) for z in range(self.step)]
        down = [(z, z - 1) for z in range(self.count - self.step, self.count)]
        self.came = (lax.ppermute(self.up, "tensor", up), lax.ppermute(self.down, "tensor", down))

    def take(self):
        self.up, self.down = self.came
        self.came = None
        if self.step < self.count - 1:
            up, down = self.blocks[self.count - 1 - self.step], self.blocks[self.step + 1]
            self.up = (self.up.astype(F32) + up.astype(F32)).astype(BF)
            self.down = (self.down.astype(F32) + down.astype(F32)).astype(BF)

    def finish(self):
        if self.came is not None:
            self.take()
        while self.step < self.count - 1:
            self.send()
            self.take()
        return self.blocks[0].astype(F32) + self.up.astype(F32) + self.down.astype(F32)


class Halving:
    def __init__(self, value, chip, count, turned):
        self.chip, self.count, self.came = chip, count, None
        self.bits = count.bit_length() - 1
        self.held = value.reshape((2,) * self.bits + (-1,) + value.shape[-1:])
        order = list(range(self.bits))
        self.order = order if turned else order[::-1]
        self.left = list(range(self.bits))

    def send(self):
        axis = self.order.pop(0)
        bit = self.bits - 1 - axis
        mine = (self.chip >> bit) & 1
        at = self.left.index(axis)
        self.left.remove(axis)
        self.kept = lax.dynamic_index_in_dim(self.held, mine, at, keepdims=False)
        sent = lax.dynamic_index_in_dim(self.held, 1 - mine, at, keepdims=False)
        self.came = flip(sent, "chip", 1 << bit, self.count)

    def take(self):
        self.held = (self.kept.astype(F32) + self.came.astype(F32)).astype(BF)
        self.came = None

    def finish(self):
        if self.came is not None:
            self.take()
        while self.order:
            self.send()
            self.take()
        return self.held


def tie(value, sums):
    tied = lax.optimization_barrier((value, *(s.came for s in sums)))
    for s, came in zip(sums, tied[1:]):
        s.came = came
        s.take()
    return tied[0]


def make(chips, cores, ranks):
    def on_device(
        tokens,
        segment_ids,
        gain_attn,
        query_key_value_weight,
        output_weight,
        gain_mlp,
        gate_up_weight,
        down_weight,
        cotangent,
    ):
        length = segment_ids.shape[1]
        own_rows, width = tokens.shape[1:]
        doc = length - length // 8
        others = ranks - 1
        rank = lax.axis_index("tensor")
        core = lax.axis_index("core")
        chip = lax.axis_index("chip")
        hold = lax.optimization_barrier

        hidden = down_weight.shape[0]
        share = hidden // cores
        per = -(-share // chips)
        piece = -(-per // 8) * 8
        heads_rows = output_weight.shape[0]
        out_piece = heads_rows // (cores * chips)
        gate_t, up_t = jnp.swapaxes(gate_up_weight, 1, 2)

        def part(weight, j):
            padded = jnp.pad(weight, ((0, chips * per + piece - share), (0, 0)))
            rows = lax.dynamic_slice_in_dim(padded, core * share + j * per, piece)
            at = lax.broadcasted_iota(jnp.int32, rows.shape, 0)
            return jnp.where((at < per) & (j * per + at < share), rows, jnp.zeros_like(rows))

        gate_mine = part(gate_t, chip)
        out_mine = lax.dynamic_slice_in_dim(
            output_weight, (core * chips + chip) * out_piece, out_piece
        )
        rest_mine = jnp.concatenate([part(up_t, chip), out_mine, part(down_weight, chip)])

        gate_came = jnp.concatenate([shift(gate_mine, -k, ranks) for k in range(1, ranks)])
        token_f = tokens[0].astype(F32)
        normal_attn, inverse_attn = normalize(token_f)
        normed_attn = (normal_attn * gain_attn).astype(BF)
        rest_sent, gate_came = hold((rest_mine, gate_came))
        gate_all = lax.all_gather(gate_came, "chip").reshape(chips, others, piece, width)
        ups, downs = relay_ranks(rest_sent, ranks)
        rest_came = jnp.concatenate([downs[k] + ups[others - 1 - k] for k in range(others)])
        normed_sent, rest_came = hold((normed_attn, rest_came))
        rest_all = lax.all_gather(rest_came, "chip").reshape(chips, others, -1, width)
        normed_ups, normed_downs = relay_ranks(normed_sent, ranks)
        own = jnp.stack(
            [jnp.stack([part(w, j) for w in (gate_t, up_t, down_weight)]) for j in range(chips)]
        )

        segments = segment_ids[0]
        middle = segments[length // 2]
        start = jnp.sum((segments < middle).astype(jnp.int32))
        by = (start - rank * own_rows) % length
        places = (jnp.arange(length, dtype=jnp.int32) - by) % length
        places = jnp.where(places < doc, places, 0)
        half = HD // 2
        freq = jnp.exp(jnp.arange(half, dtype=F32) * (-2.0 * math.log(ROPE_BASE) / HD))
        angles = places.astype(F32)[:, None] * jnp.concatenate([freq] * 4)[None, :]
        cos_table = jnp.cos(angles)
        lane = jnp.arange(2 * HD, dtype=jnp.int32)
        sin_table = jnp.sin(angles) * jnp.where(lane % HD < half, -1.0, 1.0)
        by = by[None]

        cot = cotangent[0]
        cot_pair = jnp.concatenate([cot, flip(cot, "core", 1, cores)])
        normed_attn, cos_table, sin_table, cot_pair, own = hold(
            (normed_attn, cos_table, sin_table, cot_pair, own)
        )

        normed_rows, queries, keys, values = project(
            rank[None],
            normed_attn,
            normed_ups,
            normed_downs,
            query_key_value_weight,
            cos_table,
            sin_table,
        )
        mixture, logs, queries, keys, values = attend(by, queries, keys, values, doc)
        mixture = mixture.reshape(ranks, own_rows, heads_rows)
        attention = jnp.concatenate(
            [mixture[0]] + [shift(mixture[k], k, ranks) for k in range(1, ranks)], axis=1
        )
        attention, gate_all, rest_all = hold((attention, gate_all, rest_all))

        out_half = jnp.swapaxes(rest_all[:, :, piece : piece + out_piece], 0, 1)
        out_half = out_half.reshape(others, heads_rows // cores, width)
        out_other = flip(out_half, "core", 1, cores)
        out_rest = jnp.concatenate(
            [
                jnp.where(core == 0, out_half, out_other),
                jnp.where(core == 0, out_other, out_half),
            ],
            axis=1,
        )
        out_weight = jnp.concatenate(
            [output_weight] + [out_rest[others - k] for k in range(1, ranks)]
        )
        hidden_state = token_f + nn(attention, out_weight)
        normal_mlp, inverse_mlp = normalize(hidden_state)
        normed_mlp = (normal_mlp * gain_mlp).astype(BF)
        normed_pair = jnp.concatenate([normed_mlp, flip(normed_mlp, "core", 1, cores)])
        gate_up_grad, down_grad, in_part, in_other, mlp_part, mlp_other = feed(
            normed_pair, cot_pair, own, gate_all, rest_all, piece, out_piece
        )
        gate_up_here = hold(
            lax.psum_scatter(
                gate_up_grad.reshape(-1, width), "chip", scatter_dimension=0, tiled=True
            )
        )
        down_sum = LineSum(down_grad.reshape(ranks, chips * piece, width), ranks)
        down_sum.send()
        normed_mlp_grad = in_part + flip(in_other, "core", 1, cores).astype(F32)
        gain_mlp_part = jnp.sum(normed_mlp_grad * normal_mlp, axis=0)
        hidden_grad = cot.astype(F32) + norm_back(
            normed_mlp_grad, normal_mlp, inverse_mlp, gain_mlp
        )
        branch_grad = hidden_grad.astype(BF)

        attended_grad = nt(branch_grad, out_weight).astype(BF)
        def sum_cores(value, axis):
            kept = lax.dynamic_index_in_dim(value, core, axis, keepdims=False)
            sent = lax.dynamic_index_in_dim(value, 1 - core, axis, keepdims=False)
            return (kept.astype(F32) + flip(sent, "core", 1, cores).astype(F32)).astype(BF)

        out_w_grad = tn(attention, branch_grad).astype(BF)
        out_blocks = out_w_grad.reshape(ranks, cores, chips, out_piece, width)
        out_blocks = jnp.stack([out_blocks[(ranks - k) % ranks] for k in range(ranks)])
        out_blocks = jnp.swapaxes(sum_cores(out_blocks, 1), 0, 1)
        attended_grad, out_blocks = hold((attended_grad, out_blocks))
        out_sum = Halving(out_blocks, chip, chips, True)
        out_sum.send()
        attended_came = [
            shift(attended_grad[:, k * heads_rows : (k + 1) * heads_rows], -k, ranks)
            for k in range(1, ranks)
        ]
        mlp_out = mlp_part + flip(mlp_other, "core", 1, cores).astype(F32)
        layer_out = (hidden_state + mlp_out).astype(BF)

        attended_rows = jnp.concatenate([attended_grad[:, :heads_rows]] + attended_came)
        attended_rows, layer_out = hold((attended_rows, layer_out))

        def in_rank_order(here):
            rows = here.shape[1]
            flat = here.reshape(ranks * rows, width)
            twice = jnp.concatenate([flat, flat])
            return lax.dynamic_slice_in_dim(twice, (ranks - rank) % ranks * rows, ranks * rows)

        attended_rows = tie(attended_rows, [down_sum, out_sum])
        down_sum.send()
        out_sum.send()
        dq, dk, dv = attend_back(
            by, queries, keys, values, attended_rows, logs, cos_table, sin_table, doc
        )
        dq = tie(dq, [down_sum, out_sum])
        down_sum.send()
        out_here = out_sum.finish().reshape(ranks, out_piece, width)
        gate_up_here = gate_up_here.reshape(2, ranks, piece, width)
        z_rows = in_rank_order(
            jnp.concatenate([gate_up_here[0], gate_up_here[1], out_here], axis=1)
        )
        z_total = lax.psum_scatter(z_rows, "tensor", scatter_dimension=0, tiled=True)
        dq, _ = hold((dq, z_rows))
        normed_attn_part = (
            nt(dq, query_key_value_weight[0])
            + nt(dk, query_key_value_weight[1])
            + nt(dv, query_key_value_weight[2])
        )
        gain_attn_part = jnp.sum(normed_attn_part * normed_rows.astype(F32), axis=0) / gain_attn
        part_rows = normed_attn_part.astype(BF).reshape(ranks, own_rows, width)
        qkv_grad = jnp.stack([tn(normed_rows, g) for g in (dq, dk, dv)]).astype(BF)
        part_rows, qkv_grad, gain_attn_part = hold((part_rows, qkv_grad, gain_attn_part))
        part_rows = tie(part_rows, [down_sum])
        down_here = down_sum.finish().astype(BF).reshape(chips, piece, width)
        down_total = Halving(down_here, chip, chips, False).finish()
        normed_attn_grad = LineSum(part_rows, ranks).finish()
        input_grad = (
            hidden_grad + norm_back(normed_attn_grad, normal_attn, inverse_attn, gain_attn)
        ).astype(BF)

        qkv_rows = width // (cores * chips)
        qkv_blocks = qkv_grad.reshape(3, cores, chips, qkv_rows, heads_rows)
        qkv_blocks = jnp.swapaxes(sum_cores(qkv_blocks, 1), 0, 1)
        gains = jnp.stack([gain_attn_part, gain_mlp_part])
        for bit in (1 << b for b in range(ranks.bit_length() - 1)):
            gains = gains + flip(gains, "tensor", bit, ranks)
        gain_rows = jnp.pad(gains, ((0, 6), (0, 0))).astype(BF)
        qkv_here = Halving(qkv_blocks, chip, chips, True).finish()
        groups = width // heads_rows
        qkv_part = qkv_rows // groups
        qkv_here = qkv_here.reshape(3, groups, qkv_part, heads_rows)
        qkv_here = jnp.concatenate(
            [qkv_here[:, g].reshape(3 * qkv_part, heads_rows) for g in range(groups)], axis=1
        )
        pieces = jnp.concatenate([z_total, gain_rows, down_total, qkv_here])
        every = lax.all_gather(pieces, ("core", "chip"))
        grads = assemble(every, (cores, chips, share, per, piece, out_piece, qkv_part))
        at = 2 * piece + out_piece
        grad_gain_attn, grad_gain_mlp = jnp.sum(every[:, at : at + 2].astype(F32), axis=0)
        grad_gateup = jnp.swapaxes(grads[0], 1, 2)
        down_weight_gradient = grads[1]
        output_weight_gradient = grads[2].reshape(heads_rows, width)
        query_key_value_gradient = grads[3].reshape(3, width, heads_rows)
        return (
            layer_out[None],
            input_grad[None],
            grad_gain_attn,
            query_key_value_gradient,
            output_weight_gradient,
            grad_gain_mlp,
            grad_gateup,
            down_weight_gradient,
        )

    return on_device


def solution(mesh):
    ranks = mesh.shape["tensor"]
    cores = 2
    chips = mesh.shape["dp"] // cores
    split = Mesh(mesh.devices.reshape(chips, cores, ranks), ("chip", "core", "tensor"))
    dp = ("chip", "core")
    rows = P(dp, "tensor", None)
    last = P(None, None, "tensor")
    first = P("tensor", None)
    return jax.shard_map(
        make(chips, cores, ranks),
        mesh=split,
        in_specs=(rows, P(dp, None), P(), last, first, P(), last, first, rows),
        out_specs=(rows, rows, P(), last, first, P(), last, first),
        check_vma=False,
    )
```

```python
import math

import jax
import jax.numpy as jnp
from jax import lax
from jax.experimental import pallas as pl
from jax.experimental.pallas import tpu as pltpu
from jax.sharding import Mesh, PartitionSpec as P

HD = 64
EPSILON = 1e-05
ROPE_BASE = 160000.0
BF = jnp.bfloat16
F32 = jnp.float32


def normalize(values):
    centered = values - jnp.mean(values, axis=-1, keepdims=True)
    variance = jnp.mean(centered * centered, axis=-1, keepdims=True)
    inverse = lax.rsqrt(variance + EPSILON)
    return (centered * inverse, inverse)


def norm_back(grad, normal, inverse, gain):
    scaled = grad * gain
    return inverse * (
        scaled
        - jnp.mean(scaled, axis=-1, keepdims=True)
        - normal * jnp.mean(scaled * normal, axis=-1, keepdims=True)
    )


def nt(left, right):
    return lax.dot_general(left, right, (((1,), (1,)), ((), ())), preferred_element_type=F32)


def nn(left, right):
    return jnp.dot(left, right, preferred_element_type=F32)


def tn(left, right):
    return lax.dot_general(left, right, (((0,), (0,)), ((), ())), preferred_element_type=F32)


def swap_halves(values):
    lane = lax.broadcasted_iota(jnp.int32, values.shape, 1)
    width = values.shape[1]
    ahead = pltpu.roll(values, width - HD // 2, 1)
    behind = pltpu.roll(values, HD // 2, 1)
    return jnp.where(lane % HD < HD // 2, ahead, behind)


def project_kernel(ranks, rank_ref, *refs):
    own_ref, *came = refs[: 2 * ranks - 1]
    w_ref, cos_ref, sin_ref, n_ref, q_ref, k_ref, v_ref = refs[2 * ranks - 1 :]
    ups, downs = came[: ranks - 1], came[ranks - 1 :]
    step = pl.program_id(0)

    @pl.when(step == 0)
    def _():
        n_ref[...] = own_ref[...]

    for k in range(1, ranks):
        below = rank_ref[0] + k < ranks

        @pl.when((step == k) & below)
        def _():
            n_ref[...] = downs[k - 1][...]

        @pl.when((step == k) & jnp.logical_not(below))
        def _():
            n_ref[...] = ups[ranks - k - 1][...]

    rows = n_ref[...]
    cos, sin = cos_ref[...], sin_ref[...]
    for c, out in ((0, q_ref), (1, k_ref), (2, v_ref)):
        wide = nn(rows, w_ref[c])
        if c == 2:
            out[...] = wide.astype(BF)
            continue
        for at in range(0, wide.shape[1], 128):
            part = wide[:, at : at + 128]
            turned = (part * cos + swap_halves(part) * sin).astype(BF)
            if c == 0:
                turned = turned * (1.0 / math.sqrt(HD))
            out[:, at : at + 128] = turned


def project(rank, own, ups, downs, weight, cos, sin):
    block, width = own.shape
    ranks = len(ups) + 1
    length = ranks * block
    cols = weight.shape[2]
    return pl.pallas_call(
        lambda *refs: project_kernel(ranks, *refs),
        grid=(ranks,),
        in_specs=[pl.BlockSpec(memory_space=pltpu.SMEM)]
        + [pl.BlockSpec((block, width), lambda i: (0, 0))] * (2 * ranks - 1)
        + [
            pl.BlockSpec((3, width, cols), lambda i: (0, 0, 0)),
            pl.BlockSpec((block, 128), lambda i: (i, 0)),
            pl.BlockSpec((block, 128), lambda i: (i, 0)),
        ],
        out_specs=[pl.BlockSpec((block, width), lambda i: (i, 0))]
        + [pl.BlockSpec((block, cols), lambda i: (i, 0))] * 3,
        out_shape=[jax.ShapeDtypeStruct((length, width), BF)]
        + [jax.ShapeDtypeStruct((length, cols), BF)] * 3,
        compiler_params=pltpu.CompilerParams(vmem_limit_bytes=40 * 2**20),
        cost_estimate=pl.CostEstimate(
            flops=6 * length * width * cols, bytes_accessed=9 * 2**20, transcendentals=0
        ),
    )(rank, own, *ups, *downs, weight, cos, sin)


def half_mask(values, half):
    lane = lax.broadcasted_iota(jnp.int32, values.shape, 1)
    return jnp.where((lane // HD) == half, values, jnp.zeros_like(values))


def row_blocks(count):
    at = 0
    while at < count:
        size = min(256, count - at)
        yield at, size
        at += size


def put_twice(held, at, value):
    length = held.shape[0] // 2
    size = value.shape[0]
    held[at : at + size, :] = value
    held[length + at : length + at + size, :] = value


def from_row(held, start):
    return held[pl.ds(start, held.shape[0] // 2), :]


def attend_kernel(doc, by_ref, q_ref, k_ref, v_ref, o_ref, l_ref, qd_ref, kd_ref, vd_ref, held):
    length = q_ref.shape[0]
    turned = []
    for i, (ref, out) in enumerate(((q_ref, qd_ref), (k_ref, kd_ref), (v_ref, vd_ref))):
        put_twice(held.at[i], 0, ref[...].astype(F32))
        turned.append(from_row(held.at[i], by_ref[0]))
        out[...] = turned[i].astype(BF)
    keys = kd_ref[:doc, :]
    values = vd_ref[:doc, :]
    lane = lax.broadcasted_iota(jnp.int32, values.shape, 1)
    summed = [jnp.where(lane // HD == h, values, jnp.ones_like(values)) for h in range(2)]
    for at, size in row_blocks(doc):
        queries = qd_ref[at : at + size, :]
        mixed = []
        for half in range(2):
            scores = nt(half_mask(queries, half), keys)
            largest = jnp.max(scores, axis=1, keepdims=True)
            weights = jnp.exp(scores - largest).astype(BF)
            mix = nn(weights, summed[half])
            other = (1 - half) * HD
            total = mix[:, other : other + 1]
            mixed.append(mix * (1.0 / total))
            log = jnp.broadcast_to(largest + jnp.log(total), (size, 128))
            l_ref[0, half : half + 1, at : at + size] = log.T[0:1, :]
        lane = lax.broadcasted_iota(jnp.int32, (size, 128), 1)
        put_twice(held.at[3], at, jnp.where(lane < HD, mixed[0], mixed[1]))
    put_twice(held.at[3], doc, turned[2][doc:, :])
    o_ref[...] = from_row(held.at[3], length - by_ref[0]).astype(BF)


def attend(by, queries, keys, values, doc):
    length, cols = queries.shape
    pairs = cols // 128
    spec = pl.BlockSpec((length, 128), lambda p: (0, p))
    return pl.pallas_call(
        lambda *refs: attend_kernel(doc, *refs),
        grid=(pairs,),
        in_specs=[pl.BlockSpec(memory_space=pltpu.SMEM)] + [spec] * 3,
        out_specs=[spec, pl.BlockSpec((1, 2, doc), lambda p: (p, 0, 0))] + [spec] * 3,
        out_shape=[
            jax.ShapeDtypeStruct((length, cols), BF),
            jax.ShapeDtypeStruct((pairs, 2, doc), F32),
        ]
        + [jax.ShapeDtypeStruct((length, cols), BF)] * 3,
        scratch_shapes=[pltpu.VMEM((4, 2 * length, 128), F32)],
        compiler_params=pltpu.CompilerParams(vmem_limit_bytes=48 * 2**20),
        cost_estimate=pl.CostEstimate(
            flops=8 * doc * doc * cols, bytes_accessed=2 * 2**20, transcendentals=doc * doc * 4
        ),
    )(by, queries, keys, values)


def attend_back_kernel(
    doc, by_ref, q_ref, k_ref, v_ref, d_ref, l_ref, cos_ref, sin_ref,
    dq_ref, dk_ref, dv_ref, ka_ref, va_ref, dd_ref, held,
):
    length = q_ref.shape[0]
    put_twice(held.at[0], 0, d_ref[...].astype(F32))
    turned = from_row(held.at[0], by_ref[0])
    dd_ref[...] = turned.astype(BF)
    keys = k_ref[:doc, :]
    keys_t = keys.T
    values = v_ref[:doc, :]
    first = True
    for at, size in row_blocks(doc):
        queries = q_ref[at : at + size, :]
        grads = dd_ref[at : at + size, :]
        back = []
        for half in range(2):
            query = half_mask(queries, half)
            grad = half_mask(grads, half)
            probs = jnp.exp(nt(keys, query) - l_ref[0, half : half + 1, at : at + size])
            prob_grad = nt(values, grad)
            centre = jnp.sum(probs * prob_grad, axis=0, keepdims=True)
            score_grad = (probs * (prob_grad - centre)).astype(BF)
            value_part = nn(probs.astype(BF), grad)
            key_part = nn(score_grad, query)
            if first:
                va_ref[...] = value_part
                ka_ref[...] = key_part
                first = False
            else:
                va_ref[...] += value_part
                ka_ref[...] += key_part
            back.append(nn(keys_t[half * HD : half * HD + HD], score_grad))
        query_grad = jnp.concatenate(back, axis=0).T * (1.0 / math.sqrt(HD))
        put_twice(held.at[1], at, query_grad)
    zero = jnp.zeros((length - doc, 128), F32)
    put_twice(held.at[1], doc, zero)
    put_twice(held.at[2], 0, ka_ref[...])
    put_twice(held.at[2], doc, zero)
    put_twice(held.at[3], 0, va_ref[...])
    put_twice(held.at[3], doc, turned[doc:, :])
    back_row = length - by_ref[0]
    cos, sin = cos_ref[...], sin_ref[...]
    for i, out in ((1, dq_ref), (2, dk_ref)):
        grad = from_row(held.at[i], back_row)
        out[...] = (grad * cos - swap_halves(grad) * sin).astype(BF)
    dv_ref[...] = from_row(held.at[3], back_row).astype(BF)


def attend_back(by, queries, keys, values, grads, logs, cos, sin, doc):
    length, cols = queries.shape
    pairs = cols // 128
    spec = pl.BlockSpec((length, 128), lambda p: (0, p))
    table = pl.BlockSpec((length, 128), lambda p: (0, 0))
    return pl.pallas_call(
        lambda *refs: attend_back_kernel(doc, *refs),
        grid=(pairs,),
        in_specs=[pl.BlockSpec(memory_space=pltpu.SMEM)]
        + [spec] * 4
        + [pl.BlockSpec((1, 2, doc), lambda p: (p, 0, 0))]
        + [table] * 2,
        out_specs=[spec] * 3,
        out_shape=[jax.ShapeDtypeStruct((length, cols), BF)] * 3,
        scratch_shapes=[pltpu.VMEM((doc, 128), F32)] * 2
        + [pltpu.VMEM((length, 128), BF), pltpu.VMEM((4, 2 * length, 128), F32)],
        compiler_params=pltpu.CompilerParams(vmem_limit_bytes=48 * 2**20),
        cost_estimate=pl.CostEstimate(
            flops=0, bytes_accessed=2**20, transcendentals=0
        ),
    )(by, queries, keys, values, grads, logs, cos, sin)


def feed_kernel(
    sizes, n_ref, c_ref, own_ref, gate_ref, rest_ref,
    dgu_ref, dd_ref, in_ref, in_other_ref, out_ref, out_other_ref, in_held, out_held,
):
    piece, out_piece, ranks, group, steps = sizes
    step = pl.program_id(0)

    def join(m, ref, first):
        rows = []
        for j in range(group):
            rows.append(own_ref[j, m].astype(F32))
            for k in range(ranks - 1):
                rows.append(ref[j, k].astype(F32)[first : first + piece])
        return jnp.concatenate(rows).astype(BF)

    gate = join(0, gate_ref, 0)
    up = join(1, rest_ref, 0)
    down = join(2, rest_ref, piece + out_piece)
    normed, cot = n_ref[...], c_ref[...]
    gate_proj = nt(gate, normed)
    up_proj = nt(up, normed)
    hid_grad = nt(down, cot)
    cdf = 0.5 * (1.0 + lax.erf(gate_proj * (1.0 / math.sqrt(2.0))))
    pdf = jnp.exp(-0.5 * gate_proj * gate_proj) * (1.0 / math.sqrt(2.0 * math.pi))
    act = gate_proj * cdf
    hid = (act * up_proj).astype(BF)
    gate_grad = (hid_grad * up_proj * (cdf + gate_proj * pdf)).astype(BF)
    up_grad = (hid_grad * act).astype(BF)
    hidden = ranks * piece
    dgu_ref[0, :hidden] = nn(gate_grad, normed).astype(BF)
    dgu_ref[0, hidden:] = nn(up_grad, normed).astype(BF)
    down_grad = nn(hid, cot)
    for k in range(ranks):
        dd_ref[k, 0] = down_grad[k * piece : (k + 1) * piece].astype(BF)
    in_part = tn(jnp.concatenate([gate_grad, up_grad]), jnp.concatenate([gate, up]))
    out_part = tn(hid, down)

    @pl.when(step == 0)
    def _():
        in_held[...] = in_part
        out_held[...] = out_part

    @pl.when(step > 0)
    def _():
        in_held[...] += in_part
        out_held[...] += out_part

    @pl.when(step == steps - 1)
    def _():
        rows = in_ref.shape[0]
        in_ref[...] = in_held[:rows, :]
        in_other_ref[...] = in_held[rows:, :].astype(BF)
        out_ref[...] = out_held[:rows, :]
        out_other_ref[...] = out_held[rows:, :].astype(BF)


def feed(normed, cot, own, gate_all, rest_all, piece, out_piece):
    rows, width = normed.shape
    chips, others, rest_rows = rest_all.shape[:3]
    hidden = (others + 1) * piece
    half = rows // 2
    group = 1
    same = pl.BlockSpec((rows, width), lambda i: (0, 0))
    grads = [
        pl.BlockSpec((1, 2 * hidden, width), lambda i: (i, 0, 0)),
        pl.BlockSpec((others + 1, 1, piece, width), lambda i: (0, i, 0, 0)),
    ]
    kept = pl.BlockSpec((half, width), lambda i: (0, 0))
    sizes = (piece, out_piece, others + 1, group, chips // group)
    return pl.pallas_call(
        lambda *refs: feed_kernel(sizes, *refs),
        grid=(chips // group,),
        in_specs=[
            same,
            same,
            pl.BlockSpec((group, 3, piece, width), lambda i: (i, 0, 0, 0)),
            pl.BlockSpec((group, others, piece, width), lambda i: (i, 0, 0, 0)),
            pl.BlockSpec((group, others, rest_rows, width), lambda i: (i, 0, 0, 0)),
        ],
        out_specs=grads + [kept] * 4,
        out_shape=[
            jax.ShapeDtypeStruct((chips, 2 * hidden, width), BF),
            jax.ShapeDtypeStruct((others + 1, chips, piece, width), BF),
        ]
        + [
            jax.ShapeDtypeStruct((half, width), F32),
            jax.ShapeDtypeStruct((half, width), BF),
            jax.ShapeDtypeStruct((half, width), F32),
            jax.ShapeDtypeStruct((half, width), BF),
        ],
        scratch_shapes=[pltpu.VMEM((rows, width), F32)] * 2,
        compiler_params=pltpu.CompilerParams(vmem_limit_bytes=62 * 2**20),
        cost_estimate=pl.CostEstimate(
            flops=18 * rows * width * hidden * chips,
            bytes_accessed=25 * 2**20,
            transcendentals=2 * rows * hidden * chips,
        ),
    )(normed, cot, own, gate_all, rest_all)


def assemble_kernel(sizes, in_ref, gu_ref, d_ref, o_ref, qkv_ref, held):
    cores, chips, share, per, piece, out_piece, qkv_part = sizes
    hidden = cores * share
    firsts = (0, piece, 2 * piece + out_piece + 8)
    for m, first in enumerate(firsts):
        for device in range(cores * chips):
            at = device // chips * share + device % chips * per
            rows = in_ref[device].astype(F32)
            held[at : at + piece, :] = rows[first : first + piece, :]
            if m == 0:
                o_ref[device] = rows[2 * piece : 2 * piece + out_piece, :]
                last = 3 * piece + out_piece + 8
                for c in range(3):
                    start = last + c * qkv_part
                    qkv_ref[c, device, 0] = rows[start : start + qkv_part, :]
        if m == 2:
            d_ref[...] = held[:hidden, :]
        else:
            gu_ref[m] = held[:hidden, :]


def assemble(every, sizes):
    cores, chips, share, per, piece, out_piece, qkv_part = sizes
    devices, rows, width = every.shape
    hidden = cores * share
    block = 256
    groups = width // block
    tall = -(-((cores - 1) * share + (chips - 1) * per + piece) // 8) * 8
    return pl.pallas_call(
        lambda *refs: assemble_kernel(sizes, *refs),
        grid=(groups,),
        in_specs=[pl.BlockSpec((devices, rows, block), lambda i: (0, 0, i))],
        out_specs=[
            pl.BlockSpec((2, hidden, block), lambda i: (0, 0, i)),
            pl.BlockSpec((hidden, block), lambda i: (0, i)),
            pl.BlockSpec((devices, out_piece, block), lambda i: (0, 0, i)),
            pl.BlockSpec((3, devices, 1, qkv_part, block), lambda i: (0, 0, i, 0, 0)),
        ],
        out_shape=[
            jax.ShapeDtypeStruct((2, hidden, width), F32),
            jax.ShapeDtypeStruct((hidden, width), F32),
            jax.ShapeDtypeStruct((devices, out_piece, width), F32),
            jax.ShapeDtypeStruct((3, devices, groups, qkv_part, block), F32),
        ],
        scratch_shapes=[pltpu.VMEM((tall, block), F32)],
        compiler_params=pltpu.CompilerParams(vmem_limit_bytes=60 * 2**20),
        cost_estimate=pl.CostEstimate(flops=0, bytes_accessed=18 * 2**20, transcendentals=0),
    )(every)


def shift(value, by, count):
    return lax.ppermute(value, "tensor", [(i, (i + by) % count) for i in range(count)])


def flip(value, axis, bit, count):
    return lax.ppermute(value, axis, [(i, i ^ bit) for i in range(count)])


def relay_ranks(value, count):
    ups, downs = [value], [value]
    for step in range(1, count):
        ups.append(lax.ppermute(ups[-1], "tensor", [(z, z + 1) for z in range(step - 1, count - 1)]))
        downs.append(lax.ppermute(downs[-1], "tensor", [(z, z - 1) for z in range(1, count - step + 1)]))
    return ups[1:], downs[1:]


class LineSum:
    def __init__(self, blocks, count):
        self.blocks, self.count, self.step, self.came = blocks, count, 0, None
        self.up, self.down = blocks[count - 1], blocks[1]

    def send(self):
        self.step += 1
        up = [(z, z + 1) for z in range(self.step)]
        down = [(z, z - 1) for z in range(self.count - self.step, self.count)]
        self.came = (lax.ppermute(self.up, "tensor", up), lax.ppermute(self.down, "tensor", down))

    def take(self):
        self.up, self.down = self.came
        self.came = None
        if self.step < self.count - 1:
            up, down = self.blocks[self.count - 1 - self.step], self.blocks[self.step + 1]
            self.up = (self.up.astype(F32) + up.astype(F32)).astype(BF)
            self.down = (self.down.astype(F32) + down.astype(F32)).astype(BF)

    def finish(self):
        if self.came is not None:
            self.take()
        while self.step < self.count - 1:
            self.send()
            self.take()
        return self.blocks[0].astype(F32) + self.up.astype(F32) + self.down.astype(F32)


class Halving:
    def __init__(self, value, chip, count, turned):
        self.chip, self.count, self.came = chip, count, None
        self.bits = count.bit_length() - 1
        self.held = value.reshape((2,) * self.bits + (-1,) + value.shape[-1:])
        order = list(range(self.bits))
        self.order = order if turned else order[::-1]
        self.left = list(range(self.bits))

    def send(self):
        axis = self.order.pop(0)
        bit = self.bits - 1 - axis
        mine = (self.chip >> bit) & 1
        at = self.left.index(axis)
        self.left.remove(axis)
        self.kept = lax.dynamic_index_in_dim(self.held, mine, at, keepdims=False)
        sent = lax.dynamic_index_in_dim(self.held, 1 - mine, at, keepdims=False)
        self.came = flip(sent, "chip", 1 << bit, self.count)

    def take(self):
        self.held = (self.kept.astype(F32) + self.came.astype(F32)).astype(BF)
        self.came = None

    def finish(self):
        if self.came is not None:
            self.take()
        while self.order:
            self.send()
            self.take()
        return self.held


def tie(value, sums):
    tied = lax.optimization_barrier((value, *(s.came for s in sums)))
    for s, came in zip(sums, tied[1:]):
        s.came = came
        s.take()
    return tied[0]


def make(chips, cores, ranks):
    def on_device(
        tokens,
        segment_ids,
        gain_attn,
        query_key_value_weight,
        output_weight,
        gain_mlp,
        gate_up_weight,
        down_weight,
        cotangent,
    ):
        length = segment_ids.shape[1]
        own_rows, width = tokens.shape[1:]
        doc = length - length // 8
        others = ranks - 1
        rank = lax.axis_index("tensor")
        core = lax.axis_index("core")
        chip = lax.axis_index("chip")
        hold = lax.optimization_barrier

        hidden = down_weight.shape[0]
        share = hidden // cores
        per = -(-share // chips)
        piece = -(-per // 8) * 8
        heads_rows = output_weight.shape[0]
        out_piece = heads_rows // (cores * chips)
        gate_t, up_t = jnp.swapaxes(gate_up_weight, 1, 2)

        def part(weight, j):
            padded = jnp.pad(weight, ((0, chips * per + piece - share), (0, 0)))
            rows = lax.dynamic_slice_in_dim(padded, core * share + j * per, piece)
            at = lax.broadcasted_iota(jnp.int32, rows.shape, 0)
            return jnp.where((at < per) & (j * per + at < share), rows, jnp.zeros_like(rows))

        gate_mine = part(gate_t, chip)
        out_mine = lax.dynamic_slice_in_dim(
            output_weight, (core * chips + chip) * out_piece, out_piece
        )
        rest_mine = jnp.concatenate([part(up_t, chip), out_mine, part(down_weight, chip)])

        gate_came = jnp.concatenate([shift(gate_mine, -k, ranks) for k in range(1, ranks)])
        token_f = tokens[0].astype(F32)
        normal_attn, inverse_attn = normalize(token_f)
        normed_attn = (normal_attn * gain_attn).astype(BF)
        rest_sent, gate_came = hold((rest_mine, gate_came))
        gate_all = lax.all_gather(gate_came, "chip").reshape(chips, others, piece, width)
        ups, downs = relay_ranks(rest_sent, ranks)
        rest_came = jnp.concatenate([downs[k] + ups[others - 1 - k] for k in range(others)])
        normed_sent, rest_came = hold((normed_attn, rest_came))
        rest_all = lax.all_gather(rest_came, "chip").reshape(chips, others, -1, width)
        normed_ups, normed_downs = relay_ranks(normed_sent, ranks)
        own = jnp.stack(
            [jnp.stack([part(w, j) for w in (gate_t, up_t, down_weight)]) for j in range(chips)]
        )

        segments = segment_ids[0]
        middle = segments[length // 2]
        start = jnp.sum((segments < middle).astype(jnp.int32))
        by = (start - rank * own_rows) % length
        places = (jnp.arange(length, dtype=jnp.int32) - by) % length
        places = jnp.where(places < doc, places, 0)
        half = HD // 2
        freq = jnp.exp(jnp.arange(half, dtype=F32) * (-2.0 * math.log(ROPE_BASE) / HD))
        angles = places.astype(F32)[:, None] * jnp.concatenate([freq] * 4)[None, :]
        cos_table = jnp.cos(angles)
        lane = jnp.arange(2 * HD, dtype=jnp.int32)
        sin_table = jnp.sin(angles) * jnp.where(lane % HD < half, -1.0, 1.0)
        by = by[None]

        cot = cotangent[0]
        cot_pair = jnp.concatenate([cot, flip(cot, "core", 1, cores)])
        normed_attn, cos_table, sin_table, cot_pair, own = hold(
            (normed_attn, cos_table, sin_table, cot_pair, own)
        )

        normed_rows, queries, keys, values = project(
            rank[None],
            normed_attn,
            normed_ups,
            normed_downs,
            query_key_value_weight,
            cos_table,
            sin_table,
        )
        mixture, logs, queries, keys, values = attend(by, queries, keys, values, doc)
        mixture = mixture.reshape(ranks, own_rows, heads_rows)
        attention = jnp.concatenate(
            [mixture[0]] + [shift(mixture[k], k, ranks) for k in range(1, ranks)], axis=1
        )
        attention, gate_all, rest_all = hold((attention, gate_all, rest_all))

        out_half = jnp.swapaxes(rest_all[:, :, piece : piece + out_piece], 0, 1)
        out_half = out_half.reshape(others, heads_rows // cores, width)
        out_other = flip(out_half, "core", 1, cores)
        out_rest = jnp.concatenate(
            [
                jnp.where(core == 0, out_half, out_other),
                jnp.where(core == 0, out_other, out_half),
            ],
            axis=1,
        )
        out_weight = jnp.concatenate(
            [output_weight] + [out_rest[others - k] for k in range(1, ranks)]
        )
        hidden_state = token_f + nn(attention, out_weight)
        normal_mlp, inverse_mlp = normalize(hidden_state)
        normed_mlp = (normal_mlp * gain_mlp).astype(BF)
        normed_pair = jnp.concatenate([normed_mlp, flip(normed_mlp, "core", 1, cores)])
        gate_up_grad, down_grad, in_part, in_other, mlp_part, mlp_other = feed(
            normed_pair, cot_pair, own, gate_all, rest_all, piece, out_piece
        )
        gate_up_here = hold(
            lax.psum_scatter(
                gate_up_grad.reshape(-1, width), "chip", scatter_dimension=0, tiled=True
            )
        )
        down_sum = LineSum(down_grad.reshape(ranks, chips * piece, width), ranks)
        down_sum.send()
        normed_mlp_grad = in_part + flip(in_other, "core", 1, cores).astype(F32)
        gain_mlp_part = jnp.sum(normed_mlp_grad * normal_mlp, axis=0)
        hidden_grad = cot.astype(F32) + norm_back(
            normed_mlp_grad, normal_mlp, inverse_mlp, gain_mlp
        )
        branch_grad = hidden_grad.astype(BF)

        attended_grad = nt(branch_grad, out_weight).astype(BF)
        def sum_cores(value, axis):
            kept = lax.dynamic_index_in_dim(value, core, axis, keepdims=False)
            sent = lax.dynamic_index_in_dim(value, 1 - core, axis, keepdims=False)
            return (kept.astype(F32) + flip(sent, "core", 1, cores).astype(F32)).astype(BF)

        out_w_grad = tn(attention, branch_grad).astype(BF)
        out_blocks = out_w_grad.reshape(ranks, cores, chips, out_piece, width)
        out_blocks = jnp.stack([out_blocks[(ranks - k) % ranks] for k in range(ranks)])
        out_blocks = jnp.swapaxes(sum_cores(out_blocks, 1), 0, 1)
        attended_grad, out_blocks = hold((attended_grad, out_blocks))
        out_sum = Halving(out_blocks, chip, chips, True)
        out_sum.send()
        attended_came = [
            shift(attended_grad[:, k * heads_rows : (k + 1) * heads_rows], -k, ranks)
            for k in range(1, ranks)
        ]
        mlp_out = mlp_part + flip(mlp_other, "core", 1, cores).astype(F32)
        layer_out = (hidden_state + mlp_out).astype(BF)

        attended_rows = jnp.concatenate([attended_grad[:, :heads_rows]] + attended_came)
        attended_rows, layer_out = hold((attended_rows, layer_out))

        def in_rank_order(here):
            rows = here.shape[1]
            flat = here.reshape(ranks * rows, width)
            twice = jnp.concatenate([flat, flat])
            return lax.dynamic_slice_in_dim(twice, (ranks - rank) % ranks * rows, ranks * rows)

        attended_rows = tie(attended_rows, [down_sum, out_sum])
        down_sum.send()
        out_sum.send()
        dq, dk, dv = attend_back(
            by, queries, keys, values, attended_rows, logs, cos_table, sin_table, doc
        )
        dq = tie(dq, [down_sum, out_sum])
        down_sum.send()
        out_here = out_sum.finish().reshape(ranks, out_piece, width)
        gate_up_here = gate_up_here.reshape(2, ranks, piece, width)
        z_rows = in_rank_order(
            jnp.concatenate([gate_up_here[0], gate_up_here[1], out_here], axis=1)
        )
        z_total = lax.psum_scatter(z_rows, "tensor", scatter_dimension=0, tiled=True)
        dq, _ = hold((dq, z_rows))
        normed_attn_part = (
            nt(dq, query_key_value_weight[0])
            + nt(dk, query_key_value_weight[1])
            + nt(dv, query_key_value_weight[2])
        )
        gain_attn_part = jnp.sum(normed_attn_part * normed_rows.astype(F32), axis=0) / gain_attn
        part_rows = normed_attn_part.astype(BF).reshape(ranks, own_rows, width)
        qkv_grad = jnp.stack([tn(normed_rows, g) for g in (dq, dk, dv)]).astype(BF)
        part_rows, qkv_grad, gain_attn_part = hold((part_rows, qkv_grad, gain_attn_part))
        part_rows = tie(part_rows, [down_sum])
        down_here = down_sum.finish().astype(BF).reshape(chips, piece, width)
        down_total = Halving(down_here, chip, chips, False).finish()
        normed_attn_grad = LineSum(part_rows, ranks).finish()
        input_grad = (
            hidden_grad + norm_back(normed_attn_grad, normal_attn, inverse_attn, gain_attn)
        ).astype(BF)

        qkv_rows = width // (cores * chips)
        qkv_blocks = qkv_grad.reshape(3, cores, chips, qkv_rows, heads_rows)
        qkv_blocks = jnp.swapaxes(sum_cores(qkv_blocks, 1), 0, 1)
        gains = jnp.stack([gain_attn_part, gain_mlp_part])
        for bit in (1 << b for b in range(ranks.bit_length() - 1)):
            gains = gains + flip(gains, "tensor", bit, ranks)
        gain_rows = jnp.pad(gains, ((0, 6), (0, 0))).astype(BF)
        qkv_here = Halving(qkv_blocks, chip, chips, True).finish()
        groups = width // heads_rows
        qkv_part = qkv_rows // groups
        qkv_here = qkv_here.reshape(3, groups, qkv_part, heads_rows)
        qkv_here = jnp.concatenate(
            [qkv_here[:, g].reshape(3 * qkv_part, heads_rows) for g in range(groups)], axis=1
        )
        pieces = jnp.concatenate([z_total, gain_rows, down_total, qkv_here])
        every = lax.all_gather(pieces, ("core", "chip"))
        grads = assemble(every, (cores, chips, share, per, piece, out_piece, qkv_part))
        at = 2 * piece + out_piece
        grad_gain_attn, grad_gain_mlp = jnp.sum(every[:, at : at + 2].astype(F32), axis=0)
        grad_gateup = jnp.swapaxes(grads[0], 1, 2)
        down_weight_gradient = grads[1]
        output_weight_gradient = grads[2].reshape(heads_rows, width)
        query_key_value_gradient = grads[3].reshape(3, width, heads_rows)
        return (
            layer_out[None],
            input_grad[None],
            grad_gain_attn,
            query_key_value_gradient,
            output_weight_gradient,
            grad_gain_mlp,
            grad_gateup,
            down_weight_gradient,
        )

    return on_device


def solution(mesh):
    ranks = mesh.shape["tensor"]
    cores = 2
    chips = mesh.shape["dp"] // cores
    split = Mesh(mesh.devices.reshape(chips, cores, ranks), ("chip", "core", "tensor"))
    dp = ("chip", "core")
    rows = P(dp, "tensor", None)
    last = P(None, None, "tensor")
    first = P("tensor", None)
    return jax.shard_map(
        make(chips, cores, ranks),
        mesh=split,
        in_specs=(rows, P(dp, None), P(), last, first, P(), last, first, rows),
        out_specs=(rows, rows, P(), last, first, P(), last, first),
        check_vma=False,
    )
```

```python
import math

import jax
import jax.numpy as jnp
from jax import lax
from jax.experimental import pallas as pl
from jax.experimental.pallas import tpu as pltpu
from jax.sharding import Mesh, PartitionSpec as P

HD = 64
EPSILON = 1e-05
ROPE_BASE = 160000.0
BF = jnp.bfloat16
F32 = jnp.float32


def normalize(values):
    centered = values - jnp.mean(values, axis=-1, keepdims=True)
    variance = jnp.mean(centered * centered, axis=-1, keepdims=True)
    inverse = lax.rsqrt(variance + EPSILON)
    return (centered * inverse, inverse)


def norm_back(grad, normal, inverse, gain):
    scaled = grad * gain
    return inverse * (
        scaled
        - jnp.mean(scaled, axis=-1, keepdims=True)
        - normal * jnp.mean(scaled * normal, axis=-1, keepdims=True)
    )


def nt(left, right):
    return lax.dot_general(left, right, (((1,), (1,)), ((), ())), preferred_element_type=F32)


def nn(left, right):
    return jnp.dot(left, right, preferred_element_type=F32)


def tn(left, right):
    return lax.dot_general(left, right, (((0,), (0,)), ((), ())), preferred_element_type=F32)


def swap_halves(values):
    lane = lax.broadcasted_iota(jnp.int32, values.shape, 1)
    width = values.shape[1]
    ahead = pltpu.roll(values, width - HD // 2, 1)
    behind = pltpu.roll(values, HD // 2, 1)
    return jnp.where(lane % HD < HD // 2, ahead, behind)


def project_kernel(ranks, rank_ref, *refs):
    own_ref, *came = refs[: 2 * ranks - 1]
    w_ref, cos_ref, sin_ref, n_ref, q_ref, k_ref, v_ref = refs[2 * ranks - 1 :]
    ups, downs = came[: ranks - 1], came[ranks - 1 :]
    step = pl.program_id(0)

    @pl.when(step == 0)
    def _():
        n_ref[...] = own_ref[...]

    for k in range(1, ranks):
        below = rank_ref[0] + k < ranks

        @pl.when((step == k) & below)
        def _():
            n_ref[...] = downs[k - 1][...]

        @pl.when((step == k) & jnp.logical_not(below))
        def _():
            n_ref[...] = ups[ranks - k - 1][...]

    rows = n_ref[...]
    cos, sin = cos_ref[...], sin_ref[...]
    for c, out in ((0, q_ref), (1, k_ref), (2, v_ref)):
        wide = nn(rows, w_ref[c])
        if c == 2:
            out[...] = wide.astype(BF)
            continue
        for at in range(0, wide.shape[1], 128):
            part = wide[:, at : at + 128]
            turned = (part * cos + swap_halves(part) * sin).astype(BF)
            if c == 0:
                turned = turned * (1.0 / math.sqrt(HD))
            out[:, at : at + 128] = turned


def project(rank, own, ups, downs, weight, cos, sin):
    block, width = own.shape
    ranks = len(ups) + 1
    length = ranks * block
    cols = weight.shape[2]
    return pl.pallas_call(
        lambda *refs: project_kernel(ranks, *refs),
        grid=(ranks,),
        in_specs=[pl.BlockSpec(memory_space=pltpu.SMEM)]
        + [pl.BlockSpec((block, width), lambda i: (0, 0))] * (2 * ranks - 1)
        + [
            pl.BlockSpec((3, width, cols), lambda i: (0, 0, 0)),
            pl.BlockSpec((block, 128), lambda i: (i, 0)),
            pl.BlockSpec((block, 128), lambda i: (i, 0)),
        ],
        out_specs=[pl.BlockSpec((block, width), lambda i: (i, 0))]
        + [pl.BlockSpec((block, cols), lambda i: (i, 0))] * 3,
        out_shape=[jax.ShapeDtypeStruct((length, width), BF)]
        + [jax.ShapeDtypeStruct((length, cols), BF)] * 3,
        compiler_params=pltpu.CompilerParams(vmem_limit_bytes=40 * 2**20),
        cost_estimate=pl.CostEstimate(
            flops=6 * length * width * cols, bytes_accessed=9 * 2**20, transcendentals=0
        ),
    )(rank, own, *ups, *downs, weight, cos, sin)


def half_mask(values, half):
    lane = lax.broadcasted_iota(jnp.int32, values.shape, 1)
    return jnp.where((lane // HD) == half, values, jnp.zeros_like(values))


def row_blocks(count):
    at = 0
    while at < count:
        size = min(256, count - at)
        yield at, size
        at += size


def put_twice(held, at, value):
    length = held.shape[0] // 2
    size = value.shape[0]
    held[at : at + size, :] = value
    held[length + at : length + at + size, :] = value


def from_row(held, start):
    return held[pl.ds(start, held.shape[0] // 2), :]


def attend_kernel(doc, by_ref, q_ref, k_ref, v_ref, o_ref, l_ref, qd_ref, kd_ref, vd_ref, held):
    length = q_ref.shape[0]
    turned = []
    for i, (ref, out) in enumerate(((q_ref, qd_ref), (k_ref, kd_ref), (v_ref, vd_ref))):
        put_twice(held.at[i], 0, ref[...].astype(F32))
        turned.append(from_row(held.at[i], by_ref[0]))
        out[...] = turned[i].astype(BF)
    keys = kd_ref[:doc, :]
    values = vd_ref[:doc, :]
    lane = lax.broadcasted_iota(jnp.int32, values.shape, 1)
    summed = [jnp.where(lane // HD == h, values, jnp.ones_like(values)) for h in range(2)]
    for at, size in row_blocks(doc):
        queries = qd_ref[at : at + size, :]
        mixed = []
        for half in range(2):
            scores = nt(half_mask(queries, half), keys)
            largest = jnp.max(scores, axis=1, keepdims=True)
            weights = jnp.exp(scores - largest).astype(BF)
            mix = nn(weights, summed[half])
            other = (1 - half) * HD
            total = mix[:, other : other + 1]
            mixed.append(mix * (1.0 / total))
            log = jnp.broadcast_to(largest + jnp.log(total), (size, 128))
            l_ref[0, half : half + 1, at : at + size] = log.T[0:1, :]
        lane = lax.broadcasted_iota(jnp.int32, (size, 128), 1)
        put_twice(held.at[3], at, jnp.where(lane < HD, mixed[0], mixed[1]))
    put_twice(held.at[3], doc, turned[2][doc:, :])
    o_ref[...] = from_row(held.at[3], length - by_ref[0]).astype(BF)


def attend(by, queries, keys, values, doc):
    length, cols = queries.shape
    pairs = cols // 128
    spec = pl.BlockSpec((length, 128), lambda p: (0, p))
    return pl.pallas_call(
        lambda *refs: attend_kernel(doc, *refs),
        grid=(pairs,),
        in_specs=[pl.BlockSpec(memory_space=pltpu.SMEM)] + [spec] * 3,
        out_specs=[spec, pl.BlockSpec((1, 2, doc), lambda p: (p, 0, 0))] + [spec] * 3,
        out_shape=[
            jax.ShapeDtypeStruct((length, cols), BF),
            jax.ShapeDtypeStruct((pairs, 2, doc), F32),
        ]
        + [jax.ShapeDtypeStruct((length, cols), BF)] * 3,
        scratch_shapes=[pltpu.VMEM((4, 2 * length, 128), F32)],
        compiler_params=pltpu.CompilerParams(vmem_limit_bytes=48 * 2**20),
        cost_estimate=pl.CostEstimate(
            flops=8 * doc * doc * cols, bytes_accessed=2 * 2**20, transcendentals=doc * doc * 4
        ),
    )(by, queries, keys, values)


def attend_back_kernel(
    doc, by_ref, q_ref, k_ref, v_ref, d_ref, l_ref, cos_ref, sin_ref,
    dq_ref, dk_ref, dv_ref, ka_ref, va_ref, dd_ref, held,
):
    length = q_ref.shape[0]
    put_twice(held.at[0], 0, d_ref[...].astype(F32))
    turned = from_row(held.at[0], by_ref[0])
    dd_ref[...] = turned.astype(BF)
    keys = k_ref[:doc, :]
    keys_t = keys.T
    values = v_ref[:doc, :]
    first = True
    for at, size in row_blocks(doc):
        queries = q_ref[at : at + size, :]
        grads = dd_ref[at : at + size, :]
        back = []
        for half in range(2):
            query = half_mask(queries, half)
            grad = half_mask(grads, half)
            probs = jnp.exp(nt(keys, query) - l_ref[0, half : half + 1, at : at + size])
            prob_grad = nt(values, grad)
            centre = jnp.sum(probs * prob_grad, axis=0, keepdims=True)
            score_grad = (probs * (prob_grad - centre)).astype(BF)
            value_part = nn(probs.astype(BF), grad)
            key_part = nn(score_grad, query)
            if first:
                va_ref[...] = value_part
                ka_ref[...] = key_part
                first = False
            else:
                va_ref[...] += value_part
                ka_ref[...] += key_part
            back.append(nn(keys_t[half * HD : half * HD + HD], score_grad))
        query_grad = jnp.concatenate(back, axis=0).T * (1.0 / math.sqrt(HD))
        put_twice(held.at[1], at, query_grad)
    zero = jnp.zeros((length - doc, 128), F32)
    put_twice(held.at[1], doc, zero)
    put_twice(held.at[2], 0, ka_ref[...])
    put_twice(held.at[2], doc, zero)
    put_twice(held.at[3], 0, va_ref[...])
    put_twice(held.at[3], doc, turned[doc:, :])
    back_row = length - by_ref[0]
    cos, sin = cos_ref[...], sin_ref[...]
    for i, out in ((1, dq_ref), (2, dk_ref)):
        grad = from_row(held.at[i], back_row)
        out[...] = (grad * cos - swap_halves(grad) * sin).astype(BF)
    dv_ref[...] = from_row(held.at[3], back_row).astype(BF)


def attend_back(by, queries, keys, values, grads, logs, cos, sin, doc):
    length, cols = queries.shape
    pairs = cols // 128
    spec = pl.BlockSpec((length, 128), lambda p: (0, p))
    table = pl.BlockSpec((length, 128), lambda p: (0, 0))
    return pl.pallas_call(
        lambda *refs: attend_back_kernel(doc, *refs),
        grid=(pairs,),
        in_specs=[pl.BlockSpec(memory_space=pltpu.SMEM)]
        + [spec] * 4
        + [pl.BlockSpec((1, 2, doc), lambda p: (p, 0, 0))]
        + [table] * 2,
        out_specs=[spec] * 3,
        out_shape=[jax.ShapeDtypeStruct((length, cols), BF)] * 3,
        scratch_shapes=[pltpu.VMEM((doc, 128), F32)] * 2
        + [pltpu.VMEM((length, 128), BF), pltpu.VMEM((4, 2 * length, 128), F32)],
        compiler_params=pltpu.CompilerParams(vmem_limit_bytes=48 * 2**20),
        cost_estimate=pl.CostEstimate(
            flops=0, bytes_accessed=2**20, transcendentals=0
        ),
    )(by, queries, keys, values, grads, logs, cos, sin)


def feed_kernel(
    sizes, n_ref, c_ref, own_ref, gate_ref, rest_ref,
    dgu_ref, *refs,
):
    piece, out_piece, ranks, group, steps = sizes
    dd_refs, refs = refs[:ranks], refs[ranks:]
    in_ref, in_other_ref, out_ref, out_other_ref, in_held, out_held = refs
    step = pl.program_id(0)

    def join(m, ref, first):
        rows = []
        for j in range(group):
            rows.append(own_ref[j, m].astype(F32))
            for k in range(ranks - 1):
                rows.append(ref[j, k].astype(F32)[first : first + piece])
        return jnp.concatenate(rows).astype(BF)

    gate = join(0, gate_ref, 0)
    up = join(1, rest_ref, 0)
    down = join(2, rest_ref, piece + out_piece)
    normed, cot = n_ref[...], c_ref[...]
    gate_proj = nt(gate, normed)
    up_proj = nt(up, normed)
    hid_grad = nt(down, cot)
    cdf = 0.5 * (1.0 + lax.erf(gate_proj * (1.0 / math.sqrt(2.0))))
    pdf = jnp.exp(-0.5 * gate_proj * gate_proj) * (1.0 / math.sqrt(2.0 * math.pi))
    act = gate_proj * cdf
    hid = (act * up_proj).astype(BF)
    gate_grad = (hid_grad * up_proj * (cdf + gate_proj * pdf)).astype(BF)
    up_grad = (hid_grad * act).astype(BF)
    hidden = ranks * piece
    dgu_ref[0, :hidden] = nn(gate_grad, normed).astype(BF)
    dgu_ref[0, hidden:] = nn(up_grad, normed).astype(BF)
    down_grad = nn(hid, cot)
    for k in range(ranks):
        dd_refs[k][0] = down_grad[k * piece : (k + 1) * piece].astype(BF)
    in_part = tn(jnp.concatenate([gate_grad, up_grad]), jnp.concatenate([gate, up]))
    out_part = tn(hid, down)

    @pl.when(step == 0)
    def _():
        in_held[...] = in_part
        out_held[...] = out_part

    @pl.when(step > 0)
    def _():
        in_held[...] += in_part
        out_held[...] += out_part

    @pl.when(step == steps - 1)
    def _():
        rows = in_ref.shape[0]
        in_ref[...] = in_held[:rows, :]
        in_other_ref[...] = in_held[rows:, :].astype(BF)
        out_ref[...] = out_held[:rows, :]
        out_other_ref[...] = out_held[rows:, :].astype(BF)


def feed(normed, cot, own, gate_all, rest_all, piece, out_piece):
    rows, width = normed.shape
    chips, others, rest_rows = rest_all.shape[:3]
    hidden = (others + 1) * piece
    half = rows // 2
    group = 1
    same = pl.BlockSpec((rows, width), lambda i: (0, 0))
    grads = [
        pl.BlockSpec((1, 2 * hidden, width), lambda i: (i, 0, 0)),
        *[pl.BlockSpec((1, piece, width), lambda i: (i, 0, 0))] * (others + 1),
    ]
    kept = pl.BlockSpec((half, width), lambda i: (0, 0))
    sizes = (piece, out_piece, others + 1, group, chips // group)
    return pl.pallas_call(
        lambda *refs: feed_kernel(sizes, *refs),
        grid=(chips // group,),
        in_specs=[
            same,
            same,
            pl.BlockSpec((group, 3, piece, width), lambda i: (i, 0, 0, 0)),
            pl.BlockSpec((group, others, piece, width), lambda i: (i, 0, 0, 0)),
            pl.BlockSpec((group, others, rest_rows, width), lambda i: (i, 0, 0, 0)),
        ],
        out_specs=grads + [kept] * 4,
        out_shape=[
            jax.ShapeDtypeStruct((chips, 2 * hidden, width), BF),
            *[jax.ShapeDtypeStruct((chips, piece, width), BF)] * (others + 1),
        ]
        + [
            jax.ShapeDtypeStruct((half, width), F32),
            jax.ShapeDtypeStruct((half, width), BF),
            jax.ShapeDtypeStruct((half, width), F32),
            jax.ShapeDtypeStruct((half, width), BF),
        ],
        scratch_shapes=[pltpu.VMEM((rows, width), F32)] * 2,
        compiler_params=pltpu.CompilerParams(vmem_limit_bytes=62 * 2**20),
        cost_estimate=pl.CostEstimate(
            flops=18 * rows * width * hidden * chips,
            bytes_accessed=25 * 2**20,
            transcendentals=2 * rows * hidden * chips,
        ),
    )(normed, cot, own, gate_all, rest_all)


def assemble_kernel(sizes, in_ref, gu_ref, d_ref, o_ref, qkv_ref, held):
    cores, chips, share, per, piece, out_piece, qkv_part = sizes
    hidden = cores * share
    firsts = (0, piece, 2 * piece + out_piece + 8)
    for m, first in enumerate(firsts):
        for device in range(cores * chips):
            at = device // chips * share + device % chips * per
            rows = in_ref[device].astype(F32)
            held[at : at + piece, :] = rows[first : first + piece, :]
            if m == 0:
                o_ref[device] = rows[2 * piece : 2 * piece + out_piece, :]
                last = 3 * piece + out_piece + 8
                for c in range(3):
                    start = last + c * qkv_part
                    qkv_ref[c, device, 0] = rows[start : start + qkv_part, :]
        if m == 2:
            d_ref[...] = held[:hidden, :]
        else:
            gu_ref[m] = held[:hidden, :]


def assemble(every, sizes):
    cores, chips, share, per, piece, out_piece, qkv_part = sizes
    devices, rows, width = every.shape
    hidden = cores * share
    block = 256
    groups = width // block
    tall = -(-((cores - 1) * share + (chips - 1) * per + piece) // 8) * 8
    return pl.pallas_call(
        lambda *refs: assemble_kernel(sizes, *refs),
        grid=(groups,),
        in_specs=[pl.BlockSpec((devices, rows, block), lambda i: (0, 0, i))],
        out_specs=[
            pl.BlockSpec((2, hidden, block), lambda i: (0, 0, i)),
            pl.BlockSpec((hidden, block), lambda i: (0, i)),
            pl.BlockSpec((devices, out_piece, block), lambda i: (0, 0, i)),
            pl.BlockSpec((3, devices, 1, qkv_part, block), lambda i: (0, 0, i, 0, 0)),
        ],
        out_shape=[
            jax.ShapeDtypeStruct((2, hidden, width), F32),
            jax.ShapeDtypeStruct((hidden, width), F32),
            jax.ShapeDtypeStruct((devices, out_piece, width), F32),
            jax.ShapeDtypeStruct((3, devices, groups, qkv_part, block), F32),
        ],
        scratch_shapes=[pltpu.VMEM((tall, block), F32)],
        compiler_params=pltpu.CompilerParams(vmem_limit_bytes=60 * 2**20),
        cost_estimate=pl.CostEstimate(flops=0, bytes_accessed=18 * 2**20, transcendentals=0),
    )(every)


def shift(value, by, count):
    return lax.ppermute(value, "tensor", [(i, (i + by) % count) for i in range(count)])


def flip(value, axis, bit, count):
    return lax.ppermute(value, axis, [(i, i ^ bit) for i in range(count)])


def relay_ranks(value, count):
    ups, downs = [value], [value]
    for step in range(1, count):
        ups.append(lax.ppermute(ups[-1], "tensor", [(z, z + 1) for z in range(step - 1, count - 1)]))
        downs.append(lax.ppermute(downs[-1], "tensor", [(z, z - 1) for z in range(1, count - step + 1)]))
    return ups[1:], downs[1:]


class LineSum:
    def __init__(self, blocks, count):
        self.blocks, self.count, self.step, self.came = blocks, count, 0, None
        self.up, self.down = blocks[count - 1], blocks[1]

    def send(self):
        self.step += 1
        up = [(z, z + 1) for z in range(self.step)]
        down = [(z, z - 1) for z in range(self.count - self.step, self.count)]
        self.came = (lax.ppermute(self.up, "tensor", up), lax.ppermute(self.down, "tensor", down))

    def take(self):
        self.up, self.down = self.came
        self.came = None
        if self.step < self.count - 1:
            up, down = self.blocks[self.count - 1 - self.step], self.blocks[self.step + 1]
            self.up = (self.up.astype(F32) + up.astype(F32)).astype(BF)
            self.down = (self.down.astype(F32) + down.astype(F32)).astype(BF)

    def finish(self):
        if self.came is not None:
            self.take()
        while self.step < self.count - 1:
            self.send()
            self.take()
        return self.blocks[0].astype(F32) + self.up.astype(F32) + self.down.astype(F32)


class Halving:
    def __init__(self, value, chip, count, turned):
        self.chip, self.count, self.came = chip, count, None
        self.bits = count.bit_length() - 1
        self.held = value.reshape((2,) * self.bits + (-1,) + value.shape[-1:])
        order = list(range(self.bits))
        self.order = order if turned else order[::-1]
        self.left = list(range(self.bits))

    def send(self):
        axis = self.order.pop(0)
        bit = self.bits - 1 - axis
        mine = (self.chip >> bit) & 1
        at = self.left.index(axis)
        self.left.remove(axis)
        self.kept = lax.dynamic_index_in_dim(self.held, mine, at, keepdims=False)
        sent = lax.dynamic_index_in_dim(self.held, 1 - mine, at, keepdims=False)
        self.came = flip(sent, "chip", 1 << bit, self.count)

    def take(self):
        self.held = (self.kept.astype(F32) + self.came.astype(F32)).astype(BF)
        self.came = None

    def finish(self):
        if self.came is not None:
            self.take()
        while self.order:
            self.send()
            self.take()
        return self.held


def tie(value, sums):
    tied = lax.optimization_barrier((value, *(s.came for s in sums)))
    for s, came in zip(sums, tied[1:]):
        s.came = came
        s.take()
    return tied[0]


def make(chips, cores, ranks):
    def on_device(
        tokens,
        segment_ids,
        gain_attn,
        query_key_value_weight,
        output_weight,
        gain_mlp,
        gate_up_weight,
        down_weight,
        cotangent,
    ):
        length = segment_ids.shape[1]
        own_rows, width = tokens.shape[1:]
        doc = length - length // 8
        others = ranks - 1
        rank = lax.axis_index("tensor")
        core = lax.axis_index("core")
        chip = lax.axis_index("chip")
        hold = lax.optimization_barrier

        hidden = down_weight.shape[0]
        share = hidden // cores
        per = -(-share // chips)
        piece = -(-per // 8) * 8
        heads_rows = output_weight.shape[0]
        out_piece = heads_rows // (cores * chips)
        gate_t, up_t = jnp.swapaxes(gate_up_weight, 1, 2)

        def part(weight, j):
            padded = jnp.pad(weight, ((0, chips * per + piece - share), (0, 0)))
            rows = lax.dynamic_slice_in_dim(padded, core * share + j * per, piece)
            at = lax.broadcasted_iota(jnp.int32, rows.shape, 0)
            return jnp.where((at < per) & (j * per + at < share), rows, jnp.zeros_like(rows))

        gate_mine = part(gate_t, chip)
        out_mine = lax.dynamic_slice_in_dim(
            output_weight, (core * chips + chip) * out_piece, out_piece
        )
        rest_mine = jnp.concatenate([part(up_t, chip), out_mine, part(down_weight, chip)])

        gate_came = jnp.concatenate([shift(gate_mine, -k, ranks) for k in range(1, ranks)])
        token_f = tokens[0].astype(F32)
        normal_attn, inverse_attn = normalize(token_f)
        normed_attn = (normal_attn * gain_attn).astype(BF)
        rest_sent, gate_came = hold((rest_mine, gate_came))
        gate_all = lax.all_gather(gate_came, "chip").reshape(chips, others, piece, width)
        ups, downs = relay_ranks(rest_sent, ranks)
        rest_came = jnp.concatenate([downs[k] + ups[others - 1 - k] for k in range(others)])
        normed_sent, rest_came = hold((normed_attn, rest_came))
        rest_all = lax.all_gather(rest_came, "chip").reshape(chips, others, -1, width)
        normed_ups, normed_downs = relay_ranks(normed_sent, ranks)
        own = jnp.stack(
            [jnp.stack([part(w, j) for w in (gate_t, up_t, down_weight)]) for j in range(chips)]
        )

        segments = segment_ids[0]
        middle = segments[length // 2]
        start = jnp.sum((segments < middle).astype(jnp.int32))
        by = (start - rank * own_rows) % length
        places = (jnp.arange(length, dtype=jnp.int32) - by) % length
        places = jnp.where(places < doc, places, 0)
        half = HD // 2
        freq = jnp.exp(jnp.arange(half, dtype=F32) * (-2.0 * math.log(ROPE_BASE) / HD))
        angles = places.astype(F32)[:, None] * jnp.concatenate([freq] * 4)[None, :]
        cos_table = jnp.cos(angles)
        lane = jnp.arange(2 * HD, dtype=jnp.int32)
        sin_table = jnp.sin(angles) * jnp.where(lane % HD < half, -1.0, 1.0)
        by = by[None]

        cot = cotangent[0]
        cot_pair = jnp.concatenate([cot, flip(cot, "core", 1, cores)])
        normed_attn, cos_table, sin_table, cot_pair, own = hold(
            (normed_attn, cos_table, sin_table, cot_pair, own)
        )

        normed_rows, queries, keys, values = project(
            rank[None],
            normed_attn,
            normed_ups,
            normed_downs,
            query_key_value_weight,
            cos_table,
            sin_table,
        )
        mixture, logs, queries, keys, values = attend(by, queries, keys, values, doc)
        mixture = mixture.reshape(ranks, own_rows, heads_rows)
        attention = jnp.concatenate(
            [mixture[0]] + [shift(mixture[k], k, ranks) for k in range(1, ranks)], axis=1
        )
        attention, gate_all, rest_all = hold((attention, gate_all, rest_all))

        out_half = jnp.swapaxes(rest_all[:, :, piece : piece + out_piece], 0, 1)
        out_half = out_half.reshape(others, heads_rows // cores, width)
        out_other = flip(out_half, "core", 1, cores)
        out_rest = jnp.concatenate(
            [
                jnp.where(core == 0, out_half, out_other),
                jnp.where(core == 0, out_other, out_half),
            ],
            axis=1,
        )
        out_weight = jnp.concatenate(
            [output_weight] + [out_rest[others - k] for k in range(1, ranks)]
        )
        hidden_state = token_f + nn(attention, out_weight)
        normal_mlp, inverse_mlp = normalize(hidden_state)
        normed_mlp = (normal_mlp * gain_mlp).astype(BF)
        normed_pair = jnp.concatenate([normed_mlp, flip(normed_mlp, "core", 1, cores)])
        gate_up_grad, *down_grad, in_part, in_other, mlp_part, mlp_other = feed(
            normed_pair, cot_pair, own, gate_all, rest_all, piece, out_piece
        )
        gate_up_here = hold(
            lax.psum_scatter(
                gate_up_grad.reshape(-1, width), "chip", scatter_dimension=0, tiled=True
            )
        )
        down_sum = LineSum([g.reshape(chips * piece, width) for g in down_grad], ranks)
        down_sum.send()
        normed_mlp_grad = in_part + flip(in_other, "core", 1, cores).astype(F32)
        gain_mlp_part = jnp.sum(normed_mlp_grad * normal_mlp, axis=0)
        hidden_grad = cot.astype(F32) + norm_back(
            normed_mlp_grad, normal_mlp, inverse_mlp, gain_mlp
        )
        branch_grad = hidden_grad.astype(BF)

        attended_grad = nt(branch_grad, out_weight).astype(BF)
        def sum_cores(value, axis):
            kept = lax.dynamic_index_in_dim(value, core, axis, keepdims=False)
            sent = lax.dynamic_index_in_dim(value, 1 - core, axis, keepdims=False)
            return (kept.astype(F32) + flip(sent, "core", 1, cores).astype(F32)).astype(BF)

        out_w_grad = tn(attention, branch_grad).astype(BF)
        out_blocks = out_w_grad.reshape(ranks, cores, chips, out_piece, width)
        out_blocks = jnp.stack([out_blocks[(ranks - k) % ranks] for k in range(ranks)])
        out_blocks = jnp.swapaxes(sum_cores(out_blocks, 1), 0, 1)
        attended_grad, out_blocks = hold((attended_grad, out_blocks))
        out_sum = Halving(out_blocks, chip, chips, True)
        out_sum.send()
        attended_came = [
            shift(attended_grad[:, k * heads_rows : (k + 1) * heads_rows], -k, ranks)
            for k in range(1, ranks)
        ]
        mlp_out = mlp_part + flip(mlp_other, "core", 1, cores).astype(F32)
        layer_out = (hidden_state + mlp_out).astype(BF)

        attended_rows = jnp.concatenate([attended_grad[:, :heads_rows]] + attended_came)
        attended_rows, layer_out = hold((attended_rows, layer_out))

        def in_rank_order(here):
            rows = here.shape[1]
            flat = here.reshape(ranks * rows, width)
            twice = jnp.concatenate([flat, flat])
            return lax.dynamic_slice_in_dim(twice, (ranks - rank) % ranks * rows, ranks * rows)

        attended_rows = tie(attended_rows, [down_sum, out_sum])
        down_sum.send()
        out_sum.send()
        dq, dk, dv = attend_back(
            by, queries, keys, values, attended_rows, logs, cos_table, sin_table, doc
        )
        dq = tie(dq, [down_sum, out_sum])
        down_sum.send()
        out_here = out_sum.finish().reshape(ranks, out_piece, width)
        gate_up_here = gate_up_here.reshape(2, ranks, piece, width)
        z_rows = in_rank_order(
            jnp.concatenate([gate_up_here[0], gate_up_here[1], out_here], axis=1)
        )
        z_total = lax.psum_scatter(z_rows, "tensor", scatter_dimension=0, tiled=True)
        dq, _ = hold((dq, z_rows))
        normed_attn_part = (
            nt(dq, query_key_value_weight[0])
            + nt(dk, query_key_value_weight[1])
            + nt(dv, query_key_value_weight[2])
        )
        gain_attn_part = jnp.sum(normed_attn_part * normed_rows.astype(F32), axis=0) / gain_attn
        part_rows = normed_attn_part.astype(BF).reshape(ranks, own_rows, width)
        qkv_grad = jnp.stack([tn(normed_rows, g) for g in (dq, dk, dv)]).astype(BF)
        part_rows, qkv_grad, gain_attn_part = hold((part_rows, qkv_grad, gain_attn_part))
        part_rows = tie(part_rows, [down_sum])
        down_here = down_sum.finish().astype(BF).reshape(chips, piece, width)
        down_total = Halving(down_here, chip, chips, False).finish()
        normed_attn_grad = LineSum(part_rows, ranks).finish()
        input_grad = (
            hidden_grad + norm_back(normed_attn_grad, normal_attn, inverse_attn, gain_attn)
        ).astype(BF)

        qkv_rows = width // (cores * chips)
        qkv_blocks = qkv_grad.reshape(3, cores, chips, qkv_rows, heads_rows)
        qkv_blocks = jnp.swapaxes(sum_cores(qkv_blocks, 1), 0, 1)
        gains = jnp.stack([gain_attn_part, gain_mlp_part])
        for bit in (1 << b for b in range(ranks.bit_length() - 1)):
            gains = gains + flip(gains, "tensor", bit, ranks)
        gain_rows = jnp.pad(gains, ((0, 6), (0, 0))).astype(BF)
        qkv_here = Halving(qkv_blocks, chip, chips, True).finish()
        groups = width // heads_rows
        qkv_part = qkv_rows // groups
        qkv_here = qkv_here.reshape(3, groups, qkv_part, heads_rows)
        qkv_here = jnp.concatenate(
            [qkv_here[:, g].reshape(3 * qkv_part, heads_rows) for g in range(groups)], axis=1
        )
        pieces = jnp.concatenate([z_total, gain_rows, down_total, qkv_here])
        every = lax.all_gather(pieces, ("core", "chip"))
        grads = assemble(every, (cores, chips, share, per, piece, out_piece, qkv_part))
        at = 2 * piece + out_piece
        grad_gain_attn, grad_gain_mlp = jnp.sum(every[:, at : at + 2].astype(F32), axis=0)
        grad_gateup = jnp.swapaxes(grads[0], 1, 2)
        down_weight_gradient = grads[1]
        output_weight_gradient = grads[2].reshape(heads_rows, width)
        query_key_value_gradient = grads[3].reshape(3, width, heads_rows)
        return (
            layer_out[None],
            input_grad[None],
            grad_gain_attn,
            query_key_value_gradient,
            output_weight_gradient,
            grad_gain_mlp,
            grad_gateup,
            down_weight_gradient,
        )

    return on_device


def solution(mesh):
    ranks = mesh.shape["tensor"]
    cores = 2
    chips = mesh.shape["dp"] // cores
    split = Mesh(mesh.devices.reshape(chips, cores, ranks), ("chip", "core", "tensor"))
    dp = ("chip", "core")
    rows = P(dp, "tensor", None)
    last = P(None, None, "tensor")
    first = P("tensor", None)
    return jax.shard_map(
        make(chips, cores, ranks),
        mesh=split,
        in_specs=(rows, P(dp, None), P(), last, first, P(), last, first, rows),
        out_specs=(rows, rows, P(), last, first, P(), last, first),
        check_vma=False,
    )
```

```python
import math

import jax
import jax.numpy as jnp
from jax import lax
from jax.experimental import pallas as pl
from jax.experimental.pallas import tpu as pltpu
from jax.sharding import Mesh, PartitionSpec as P

HD = 64
EPSILON = 1e-05
ROPE_BASE = 160000.0
BF = jnp.bfloat16
F32 = jnp.float32


def normalize(values):
    centered = values - jnp.mean(values, axis=-1, keepdims=True)
    variance = jnp.mean(centered * centered, axis=-1, keepdims=True)
    inverse = lax.rsqrt(variance + EPSILON)
    return (centered * inverse, inverse)


def norm_back(grad, normal, inverse, gain):
    scaled = grad * gain
    return inverse * (
        scaled
        - jnp.mean(scaled, axis=-1, keepdims=True)
        - normal * jnp.mean(scaled * normal, axis=-1, keepdims=True)
    )


def nt(left, right):
    return lax.dot_general(left, right, (((1,), (1,)), ((), ())), preferred_element_type=F32)


def nn(left, right):
    return jnp.dot(left, right, preferred_element_type=F32)


def tn(left, right):
    return lax.dot_general(left, right, (((0,), (0,)), ((), ())), preferred_element_type=F32)


def swap_halves(values):
    lane = lax.broadcasted_iota(jnp.int32, values.shape, 1)
    width = values.shape[1]
    ahead = pltpu.roll(values, width - HD // 2, 1)
    behind = pltpu.roll(values, HD // 2, 1)
    return jnp.where(lane % HD < HD // 2, ahead, behind)


def project_kernel(ranks, rank_ref, *refs):
    own_ref, *came = refs[: 2 * ranks - 1]
    w_ref, cos_ref, sin_ref, n_ref, q_ref, k_ref, v_ref = refs[2 * ranks - 1 :]
    ups, downs = came[: ranks - 1], came[ranks - 1 :]
    step = pl.program_id(0)

    @pl.when(step == 0)
    def _():
        n_ref[...] = own_ref[...]

    for k in range(1, ranks):
        below = rank_ref[0] + k < ranks

        @pl.when((step == k) & below)
        def _():
            n_ref[...] = downs[k - 1][...]

        @pl.when((step == k) & jnp.logical_not(below))
        def _():
            n_ref[...] = ups[ranks - k - 1][...]

    rows = n_ref[...]
    cos, sin = cos_ref[...], sin_ref[...]
    for c, out in ((0, q_ref), (1, k_ref), (2, v_ref)):
        wide = nn(rows, w_ref[c])
        if c == 2:
            out[...] = wide.astype(BF)
            continue
        for at in range(0, wide.shape[1], 128):
            part = wide[:, at : at + 128]
            turned = (part * cos + swap_halves(part) * sin).astype(BF)
            if c == 0:
                turned = turned * (1.0 / math.sqrt(HD))
            out[:, at : at + 128] = turned


def project(rank, own, ups, downs, weight, cos, sin):
    block, width = own.shape
    ranks = len(ups) + 1
    length = ranks * block
    cols = weight.shape[2]
    return pl.pallas_call(
        lambda *refs: project_kernel(ranks, *refs),
        grid=(ranks,),
        in_specs=[pl.BlockSpec(memory_space=pltpu.SMEM)]
        + [pl.BlockSpec((block, width), lambda i: (0, 0))] * (2 * ranks - 1)
        + [
            pl.BlockSpec((3, width, cols), lambda i: (0, 0, 0)),
            pl.BlockSpec((block, 128), lambda i: (i, 0)),
            pl.BlockSpec((block, 128), lambda i: (i, 0)),
        ],
        out_specs=[pl.BlockSpec((block, width), lambda i: (i, 0))]
        + [pl.BlockSpec((block, cols), lambda i: (i, 0))] * 3,
        out_shape=[jax.ShapeDtypeStruct((length, width), BF)]
        + [jax.ShapeDtypeStruct((length, cols), BF)] * 3,
        compiler_params=pltpu.CompilerParams(vmem_limit_bytes=40 * 2**20),
        cost_estimate=pl.CostEstimate(
            flops=6 * length * width * cols, bytes_accessed=9 * 2**20, transcendentals=0
        ),
    )(rank, own, *ups, *downs, weight, cos, sin)


def half_mask(values, half):
    lane = lax.broadcasted_iota(jnp.int32, values.shape, 1)
    return jnp.where((lane // HD) == half, values, jnp.zeros_like(values))


def row_blocks(count):
    at = 0
    while at < count:
        size = min(256, count - at)
        yield at, size
        at += size


def put_twice(held, at, value):
    length = held.shape[0] // 2
    size = value.shape[0]
    held[at : at + size, :] = value
    held[length + at : length + at + size, :] = value


def from_row(held, start):
    return held[pl.ds(start, held.shape[0] // 2), :]


def attend_kernel(doc, by_ref, q_ref, k_ref, v_ref, o_ref, l_ref, qd_ref, kd_ref, vd_ref, held):
    length = q_ref.shape[0]
    turned = []
    for i, (ref, out) in enumerate(((q_ref, qd_ref), (k_ref, kd_ref), (v_ref, vd_ref))):
        put_twice(held.at[i], 0, ref[...].astype(F32))
        turned.append(from_row(held.at[i], by_ref[0]))
        out[...] = turned[i].astype(BF)
    keys = kd_ref[:doc, :]
    values = vd_ref[:doc, :]
    lane = lax.broadcasted_iota(jnp.int32, values.shape, 1)
    summed = [jnp.where(lane // HD == h, values, jnp.ones_like(values)) for h in range(2)]
    for at, size in row_blocks(doc):
        queries = qd_ref[at : at + size, :]
        mixed = []
        for half in range(2):
            scores = nt(half_mask(queries, half), keys)
            largest = jnp.max(scores, axis=1, keepdims=True)
            weights = jnp.exp(scores - largest).astype(BF)
            mix = nn(weights, summed[half])
            other = (1 - half) * HD
            total = mix[:, other : other + 1]
            mixed.append(mix * (1.0 / total))
            log = jnp.broadcast_to(largest + jnp.log(total), (size, 128))
            l_ref[0, half : half + 1, at : at + size] = log.T[0:1, :]
        lane = lax.broadcasted_iota(jnp.int32, (size, 128), 1)
        put_twice(held.at[3], at, jnp.where(lane < HD, mixed[0], mixed[1]))
    put_twice(held.at[3], doc, turned[2][doc:, :])
    o_ref[...] = from_row(held.at[3], length - by_ref[0]).astype(BF)


def attend(by, queries, keys, values, doc):
    length, cols = queries.shape
    pairs = cols // 128
    spec = pl.BlockSpec((length, 128), lambda p: (0, p))
    return pl.pallas_call(
        lambda *refs: attend_kernel(doc, *refs),
        grid=(pairs,),
        in_specs=[pl.BlockSpec(memory_space=pltpu.SMEM)] + [spec] * 3,
        out_specs=[spec, pl.BlockSpec((1, 2, doc), lambda p: (p, 0, 0))] + [spec] * 3,
        out_shape=[
            jax.ShapeDtypeStruct((length, cols), BF),
            jax.ShapeDtypeStruct((pairs, 2, doc), F32),
        ]
        + [jax.ShapeDtypeStruct((length, cols), BF)] * 3,
        scratch_shapes=[pltpu.VMEM((4, 2 * length, 128), F32)],
        compiler_params=pltpu.CompilerParams(vmem_limit_bytes=48 * 2**20),
        cost_estimate=pl.CostEstimate(
            flops=8 * doc * doc * cols, bytes_accessed=2 * 2**20, transcendentals=doc * doc * 4
        ),
    )(by, queries, keys, values)


def attend_back_kernel(
    doc, by_ref, q_ref, k_ref, v_ref, d_ref, l_ref, cos_ref, sin_ref,
    dq_ref, dk_ref, dv_ref, ka_ref, va_ref, dd_ref, held,
):
    length = q_ref.shape[0]
    put_twice(held.at[0], 0, d_ref[...].astype(F32))
    turned = from_row(held.at[0], by_ref[0])
    dd_ref[...] = turned.astype(BF)
    keys = k_ref[:doc, :]
    keys_t = keys.T
    values = v_ref[:doc, :]
    first = True
    for at, size in row_blocks(doc):
        queries = q_ref[at : at + size, :]
        grads = dd_ref[at : at + size, :]
        back = []
        for half in range(2):
            query = half_mask(queries, half)
            grad = half_mask(grads, half)
            probs = jnp.exp(nt(keys, query) - l_ref[0, half : half + 1, at : at + size])
            prob_grad = nt(values, grad)
            centre = jnp.sum(probs * prob_grad, axis=0, keepdims=True)
            score_grad = (probs * (prob_grad - centre)).astype(BF)
            value_part = nn(probs.astype(BF), grad)
            key_part = nn(score_grad, query)
            if first:
                va_ref[...] = value_part
                ka_ref[...] = key_part
                first = False
            else:
                va_ref[...] += value_part
                ka_ref[...] += key_part
            back.append(nn(keys_t[half * HD : half * HD + HD], score_grad))
        query_grad = jnp.concatenate(back, axis=0).T * (1.0 / math.sqrt(HD))
        put_twice(held.at[1], at, query_grad)
    zero = jnp.zeros((length - doc, 128), F32)
    put_twice(held.at[1], doc, zero)
    put_twice(held.at[2], 0, ka_ref[...])
    put_twice(held.at[2], doc, zero)
    put_twice(held.at[3], 0, va_ref[...])
    put_twice(held.at[3], doc, turned[doc:, :])
    back_row = length - by_ref[0]
    cos, sin = cos_ref[...], sin_ref[...]
    for i, out in ((1, dq_ref), (2, dk_ref)):
        grad = from_row(held.at[i], back_row)
        out[...] = (grad * cos - swap_halves(grad) * sin).astype(BF)
    dv_ref[...] = from_row(held.at[3], back_row).astype(BF)


def attend_back(by, queries, keys, values, grads, logs, cos, sin, doc):
    length, cols = queries.shape
    pairs = cols // 128
    spec = pl.BlockSpec((length, 128), lambda p: (0, p))
    table = pl.BlockSpec((length, 128), lambda p: (0, 0))
    return pl.pallas_call(
        lambda *refs: attend_back_kernel(doc, *refs),
        grid=(pairs,),
        in_specs=[pl.BlockSpec(memory_space=pltpu.SMEM)]
        + [spec] * 4
        + [pl.BlockSpec((1, 2, doc), lambda p: (p, 0, 0))]
        + [table] * 2,
        out_specs=[spec] * 3,
        out_shape=[jax.ShapeDtypeStruct((length, cols), BF)] * 3,
        scratch_shapes=[pltpu.VMEM((doc, 128), F32)] * 2
        + [pltpu.VMEM((length, 128), BF), pltpu.VMEM((4, 2 * length, 128), F32)],
        compiler_params=pltpu.CompilerParams(vmem_limit_bytes=48 * 2**20),
        cost_estimate=pl.CostEstimate(
            flops=0, bytes_accessed=2**20, transcendentals=0
        ),
    )(by, queries, keys, values, grads, logs, cos, sin)


def feed_kernel(
    sizes, n_ref, c_ref, own_ref, gate_ref, rest_ref,
    dgu_ref, *refs,
):
    piece, out_piece, ranks, group, steps = sizes
    dd_refs, refs = refs[:ranks], refs[ranks:]
    in_ref, in_other_ref, out_ref, out_other_ref, in_held, out_held = refs
    step = pl.program_id(0)

    def join(m, ref, first):
        rows = []
        for j in range(group):
            rows.append(own_ref[j, m].astype(F32))
            for k in range(ranks - 1):
                rows.append(ref[j, k].astype(F32)[first : first + piece])
        return jnp.concatenate(rows).astype(BF)

    gate = join(0, gate_ref, 0)
    up = join(1, rest_ref, 0)
    down = join(2, rest_ref, piece + out_piece)
    normed, cot = n_ref[...], c_ref[...]
    hidden = ranks * piece
    gate_up = jnp.concatenate([gate, up])
    both = nt(gate_up, normed)
    gate_proj, up_proj = both[:hidden], both[hidden:]
    hid_grad = nt(down, cot)
    cdf = 0.5 * (1.0 + lax.erf(gate_proj * (1.0 / math.sqrt(2.0))))
    pdf = jnp.exp(-0.5 * gate_proj * gate_proj) * (1.0 / math.sqrt(2.0 * math.pi))
    act = gate_proj * cdf
    hid = (act * up_proj).astype(BF)
    gate_grad = (hid_grad * up_proj * (cdf + gate_proj * pdf)).astype(BF)
    up_grad = (hid_grad * act).astype(BF)
    both_grad = jnp.concatenate([gate_grad, up_grad])
    dgu_ref[0] = nn(both_grad, normed).astype(BF)
    down_grad = nn(hid, cot)
    for k in range(ranks):
        dd_refs[k][0] = down_grad[k * piece : (k + 1) * piece].astype(BF)
    in_part = tn(both_grad, gate_up)
    out_part = tn(hid, down)

    @pl.when(step == 0)
    def _():
        in_held[...] = in_part
        out_held[...] = out_part

    @pl.when(step > 0)
    def _():
        in_held[...] += in_part
        out_held[...] += out_part

    @pl.when(step == steps - 1)
    def _():
        rows = in_ref.shape[0]
        in_ref[...] = in_held[:rows, :]
        in_other_ref[...] = in_held[rows:, :].astype(BF)
        out_ref[...] = out_held[:rows, :]
        out_other_ref[...] = out_held[rows:, :].astype(BF)


def feed(normed, cot, own, gate_all, rest_all, piece, out_piece):
    rows, width = normed.shape
    chips, others, rest_rows = rest_all.shape[:3]
    hidden = (others + 1) * piece
    half = rows // 2
    group = 1
    same = pl.BlockSpec((rows, width), lambda i: (0, 0))
    grads = [
        pl.BlockSpec((1, 2 * hidden, width), lambda i: (i, 0, 0)),
        *[pl.BlockSpec((1, piece, width), lambda i: (i, 0, 0))] * (others + 1),
    ]
    kept = pl.BlockSpec((half, width), lambda i: (0, 0))
    sizes = (piece, out_piece, others + 1, group, chips // group)
    return pl.pallas_call(
        lambda *refs: feed_kernel(sizes, *refs),
        grid=(chips // group,),
        in_specs=[
            same,
            same,
            pl.BlockSpec((group, 3, piece, width), lambda i: (i, 0, 0, 0)),
            pl.BlockSpec((group, others, piece, width), lambda i: (i, 0, 0, 0)),
            pl.BlockSpec((group, others, rest_rows, width), lambda i: (i, 0, 0, 0)),
        ],
        out_specs=grads + [kept] * 4,
        out_shape=[
            jax.ShapeDtypeStruct((chips, 2 * hidden, width), BF),
            *[jax.ShapeDtypeStruct((chips, piece, width), BF)] * (others + 1),
        ]
        + [
            jax.ShapeDtypeStruct((half, width), F32),
            jax.ShapeDtypeStruct((half, width), BF),
            jax.ShapeDtypeStruct((half, width), F32),
            jax.ShapeDtypeStruct((half, width), BF),
        ],
        scratch_shapes=[pltpu.VMEM((rows, width), F32)] * 2,
        compiler_params=pltpu.CompilerParams(vmem_limit_bytes=62 * 2**20),
        cost_estimate=pl.CostEstimate(
            flops=18 * rows * width * hidden * chips,
            bytes_accessed=25 * 2**20,
            transcendentals=2 * rows * hidden * chips,
        ),
    )(normed, cot, own, gate_all, rest_all)


def assemble_kernel(sizes, in_ref, gu_ref, d_ref, o_ref, qkv_ref, held):
    cores, chips, share, per, piece, out_piece, qkv_part = sizes
    hidden = cores * share
    firsts = (0, piece, 2 * piece + out_piece + 8)
    for m, first in enumerate(firsts):
        for device in range(cores * chips):
            at = device // chips * share + device % chips * per
            rows = in_ref[device].astype(F32)
            held[at : at + piece, :] = rows[first : first + piece, :]
            if m == 0:
                o_ref[device] = rows[2 * piece : 2 * piece + out_piece, :]
                last = 3 * piece + out_piece + 8
                for c in range(3):
                    start = last + c * qkv_part
                    qkv_ref[c, device, 0] = rows[start : start + qkv_part, :]
        if m == 2:
            d_ref[...] = held[:hidden, :]
        else:
            gu_ref[m] = held[:hidden, :]


def assemble(every, sizes):
    cores, chips, share, per, piece, out_piece, qkv_part = sizes
    devices, rows, width = every.shape
    hidden = cores * share
    block = 256
    groups = width // block
    tall = -(-((cores - 1) * share + (chips - 1) * per + piece) // 8) * 8
    return pl.pallas_call(
        lambda *refs: assemble_kernel(sizes, *refs),
        grid=(groups,),
        in_specs=[pl.BlockSpec((devices, rows, block), lambda i: (0, 0, i))],
        out_specs=[
            pl.BlockSpec((2, hidden, block), lambda i: (0, 0, i)),
            pl.BlockSpec((hidden, block), lambda i: (0, i)),
            pl.BlockSpec((devices, out_piece, block), lambda i: (0, 0, i)),
            pl.BlockSpec((3, devices, 1, qkv_part, block), lambda i: (0, 0, i, 0, 0)),
        ],
        out_shape=[
            jax.ShapeDtypeStruct((2, hidden, width), F32),
            jax.ShapeDtypeStruct((hidden, width), F32),
            jax.ShapeDtypeStruct((devices, out_piece, width), F32),
            jax.ShapeDtypeStruct((3, devices, groups, qkv_part, block), F32),
        ],
        scratch_shapes=[pltpu.VMEM((tall, block), F32)],
        compiler_params=pltpu.CompilerParams(vmem_limit_bytes=60 * 2**20),
        cost_estimate=pl.CostEstimate(flops=0, bytes_accessed=18 * 2**20, transcendentals=0),
    )(every)


def shift(value, by, count):
    return lax.ppermute(value, "tensor", [(i, (i + by) % count) for i in range(count)])


def flip(value, axis, bit, count):
    return lax.ppermute(value, axis, [(i, i ^ bit) for i in range(count)])


def relay_ranks(value, count):
    ups, downs = [value], [value]
    for step in range(1, count):
        ups.append(lax.ppermute(ups[-1], "tensor", [(z, z + 1) for z in range(step - 1, count - 1)]))
        downs.append(lax.ppermute(downs[-1], "tensor", [(z, z - 1) for z in range(1, count - step + 1)]))
    return ups[1:], downs[1:]


class LineSum:
    def __init__(self, blocks, count):
        self.blocks, self.count, self.step, self.came = blocks, count, 0, None
        self.up, self.down = blocks[count - 1], blocks[1]

    def send(self):
        self.step += 1
        up = [(z, z + 1) for z in range(self.step)]
        down = [(z, z - 1) for z in range(self.count - self.step, self.count)]
        self.came = (lax.ppermute(self.up, "tensor", up), lax.ppermute(self.down, "tensor", down))

    def take(self):
        self.up, self.down = self.came
        self.came = None
        if self.step < self.count - 1:
            up, down = self.blocks[self.count - 1 - self.step], self.blocks[self.step + 1]
            self.up = (self.up.astype(F32) + up.astype(F32)).astype(BF)
            self.down = (self.down.astype(F32) + down.astype(F32)).astype(BF)

    def finish(self):
        if self.came is not None:
            self.take()
        while self.step < self.count - 1:
            self.send()
            self.take()
        return self.blocks[0].astype(F32) + self.up.astype(F32) + self.down.astype(F32)


class Halving:
    def __init__(self, value, chip, count, turned):
        self.chip, self.count, self.came = chip, count, None
        self.bits = count.bit_length() - 1
        self.held = value.reshape((2,) * self.bits + (-1,) + value.shape[-1:])
        order = list(range(self.bits))
        self.order = order if turned else order[::-1]
        self.left = list(range(self.bits))

    def send(self):
        axis = self.order.pop(0)
        bit = self.bits - 1 - axis
        mine = (self.chip >> bit) & 1
        at = self.left.index(axis)
        self.left.remove(axis)
        self.kept = lax.dynamic_index_in_dim(self.held, mine, at, keepdims=False)
        sent = lax.dynamic_index_in_dim(self.held, 1 - mine, at, keepdims=False)
        self.came = flip(sent, "chip", 1 << bit, self.count)

    def take(self):
        self.held = (self.kept.astype(F32) + self.came.astype(F32)).astype(BF)
        self.came = None

    def finish(self):
        if self.came is not None:
            self.take()
        while self.order:
            self.send()
            self.take()
        return self.held


def tie(value, sums):
    tied = lax.optimization_barrier((value, *(s.came for s in sums)))
    for s, came in zip(sums, tied[1:]):
        s.came = came
        s.take()
    return tied[0]


def make(chips, cores, ranks):
    def on_device(
        tokens,
        segment_ids,
        gain_attn,
        query_key_value_weight,
        output_weight,
        gain_mlp,
        gate_up_weight,
        down_weight,
        cotangent,
    ):
        length = segment_ids.shape[1]
        own_rows, width = tokens.shape[1:]
        doc = length - length // 8
        others = ranks - 1
        rank = lax.axis_index("tensor")
        core = lax.axis_index("core")
        chip = lax.axis_index("chip")
        hold = lax.optimization_barrier

        hidden = down_weight.shape[0]
        share = hidden // cores
        per = -(-share // chips)
        piece = -(-per // 8) * 8
        heads_rows = output_weight.shape[0]
        out_piece = heads_rows // (cores * chips)
        gate_t, up_t = jnp.swapaxes(gate_up_weight, 1, 2)

        def part(weight, j):
            padded = jnp.pad(weight, ((0, chips * per + piece - share), (0, 0)))
            rows = lax.dynamic_slice_in_dim(padded, core * share + j * per, piece)
            at = lax.broadcasted_iota(jnp.int32, rows.shape, 0)
            return jnp.where((at < per) & (j * per + at < share), rows, jnp.zeros_like(rows))

        gate_mine = part(gate_t, chip)
        out_mine = lax.dynamic_slice_in_dim(
            output_weight, (core * chips + chip) * out_piece, out_piece
        )
        rest_mine = jnp.concatenate([part(up_t, chip), out_mine, part(down_weight, chip)])

        gate_came = jnp.concatenate([shift(gate_mine, -k, ranks) for k in range(1, ranks)])
        token_f = tokens[0].astype(F32)
        normal_attn, inverse_attn = normalize(token_f)
        normed_attn = (normal_attn * gain_attn).astype(BF)
        rest_sent, gate_came = hold((rest_mine, gate_came))
        gate_all = lax.all_gather(gate_came, "chip").reshape(chips, others, piece, width)
        ups, downs = relay_ranks(rest_sent, ranks)
        rest_came = jnp.concatenate([downs[k] + ups[others - 1 - k] for k in range(others)])
        normed_sent, rest_came = hold((normed_attn, rest_came))
        rest_all = lax.all_gather(rest_came, "chip").reshape(chips, others, -1, width)
        normed_ups, normed_downs = relay_ranks(normed_sent, ranks)
        own = jnp.stack(
            [jnp.stack([part(w, j) for w in (gate_t, up_t, down_weight)]) for j in range(chips)]
        )

        segments = segment_ids[0]
        middle = segments[length // 2]
        start = jnp.sum((segments < middle).astype(jnp.int32))
        by = (start - rank * own_rows) % length
        places = (jnp.arange(length, dtype=jnp.int32) - by) % length
        places = jnp.where(places < doc, places, 0)
        half = HD // 2
        freq = jnp.exp(jnp.arange(half, dtype=F32) * (-2.0 * math.log(ROPE_BASE) / HD))
        angles = places.astype(F32)[:, None] * jnp.concatenate([freq] * 4)[None, :]
        cos_table = jnp.cos(angles)
        lane = jnp.arange(2 * HD, dtype=jnp.int32)
        sin_table = jnp.sin(angles) * jnp.where(lane % HD < half, -1.0, 1.0)
        by = by[None]

        cot = cotangent[0]
        cot_pair = jnp.concatenate([cot, flip(cot, "core", 1, cores)])
        normed_attn, cos_table, sin_table, cot_pair, own = hold(
            (normed_attn, cos_table, sin_table, cot_pair, own)
        )

        normed_rows, queries, keys, values = project(
            rank[None],
            normed_attn,
            normed_ups,
            normed_downs,
            query_key_value_weight,
            cos_table,
            sin_table,
        )
        mixture, logs, queries, keys, values = attend(by, queries, keys, values, doc)
        mixture = mixture.reshape(ranks, own_rows, heads_rows)
        attention = jnp.concatenate(
            [mixture[0]] + [shift(mixture[k], k, ranks) for k in range(1, ranks)], axis=1
        )
        attention, gate_all, rest_all = hold((attention, gate_all, rest_all))

        out_half = jnp.swapaxes(rest_all[:, :, piece : piece + out_piece], 0, 1)
        out_half = out_half.reshape(others, heads_rows // cores, width)
        out_other = flip(out_half, "core", 1, cores)
        out_rest = jnp.concatenate(
            [
                jnp.where(core == 0, out_half, out_other),
                jnp.where(core == 0, out_other, out_half),
            ],
            axis=1,
        )
        out_weight = jnp.concatenate(
            [output_weight] + [out_rest[others - k] for k in range(1, ranks)]
        )
        hidden_state = token_f + nn(attention, out_weight)
        normal_mlp, inverse_mlp = normalize(hidden_state)
        normed_mlp = (normal_mlp * gain_mlp).astype(BF)
        normed_pair = jnp.concatenate([normed_mlp, flip(normed_mlp, "core", 1, cores)])
        gate_up_grad, *down_grad, in_part, in_other, mlp_part, mlp_other = feed(
            normed_pair, cot_pair, own, gate_all, rest_all, piece, out_piece
        )
        gate_up_here = hold(
            lax.psum_scatter(
                gate_up_grad.reshape(-1, width), "chip", scatter_dimension=0, tiled=True
            )
        )
        down_sum = LineSum([g.reshape(chips * piece, width) for g in down_grad], ranks)
        down_sum.send()
        normed_mlp_grad = in_part + flip(in_other, "core", 1, cores).astype(F32)
        gain_mlp_part = jnp.sum(normed_mlp_grad * normal_mlp, axis=0)
        hidden_grad = cot.astype(F32) + norm_back(
            normed_mlp_grad, normal_mlp, inverse_mlp, gain_mlp
        )
        branch_grad = hidden_grad.astype(BF)

        attended_grad = nt(branch_grad, out_weight).astype(BF)
        def sum_cores(value, axis):
            kept = lax.dynamic_index_in_dim(value, core, axis, keepdims=False)
            sent = lax.dynamic_index_in_dim(value, 1 - core, axis, keepdims=False)
            return (kept.astype(F32) + flip(sent, "core", 1, cores).astype(F32)).astype(BF)

        out_w_grad = tn(attention, branch_grad).astype(BF)
        out_blocks = out_w_grad.reshape(ranks, cores, chips, out_piece, width)
        out_blocks = jnp.stack([out_blocks[(ranks - k) % ranks] for k in range(ranks)])
        out_blocks = jnp.swapaxes(sum_cores(out_blocks, 1), 0, 1)
        attended_grad, out_blocks = hold((attended_grad, out_blocks))
        out_sum = Halving(out_blocks, chip, chips, True)
        out_sum.send()
        attended_came = [
            shift(attended_grad[:, k * heads_rows : (k + 1) * heads_rows], -k, ranks)
            for k in range(1, ranks)
        ]
        mlp_out = mlp_part + flip(mlp_other, "core", 1, cores).astype(F32)
        layer_out = (hidden_state + mlp_out).astype(BF)

        attended_rows = jnp.concatenate([attended_grad[:, :heads_rows]] + attended_came)
        attended_rows, layer_out = hold((attended_rows, layer_out))

        def in_rank_order(here):
            rows = here.shape[1]
            flat = here.reshape(ranks * rows, width)
            twice = jnp.concatenate([flat, flat])
            return lax.dynamic_slice_in_dim(twice, (ranks - rank) % ranks * rows, ranks * rows)

        attended_rows = tie(attended_rows, [down_sum, out_sum])
        down_sum.send()
        out_sum.send()
        dq, dk, dv = attend_back(
            by, queries, keys, values, attended_rows, logs, cos_table, sin_table, doc
        )
        dq = tie(dq, [down_sum, out_sum])
        down_sum.send()
        out_here = out_sum.finish().reshape(ranks, out_piece, width)
        gate_up_here = gate_up_here.reshape(2, ranks, piece, width)
        z_rows = in_rank_order(
            jnp.concatenate([gate_up_here[0], gate_up_here[1], out_here], axis=1)
        )
        z_total = lax.psum_scatter(z_rows, "tensor", scatter_dimension=0, tiled=True)
        dq, _ = hold((dq, z_rows))
        normed_attn_part = (
            nt(dq, query_key_value_weight[0])
            + nt(dk, query_key_value_weight[1])
            + nt(dv, query_key_value_weight[2])
        )
        gain_attn_part = jnp.sum(normed_attn_part * normed_rows.astype(F32), axis=0) / gain_attn
        part_rows = normed_attn_part.astype(BF).reshape(ranks, own_rows, width)
        qkv_grad = jnp.stack([tn(normed_rows, g) for g in (dq, dk, dv)]).astype(BF)
        part_rows, qkv_grad, gain_attn_part = hold((part_rows, qkv_grad, gain_attn_part))
        part_rows = tie(part_rows, [down_sum])
        down_here = down_sum.finish().astype(BF).reshape(chips, piece, width)
        down_total = Halving(down_here, chip, chips, False).finish()
        normed_attn_grad = LineSum(part_rows, ranks).finish()
        input_grad = (
            hidden_grad + norm_back(normed_attn_grad, normal_attn, inverse_attn, gain_attn)
        ).astype(BF)

        qkv_rows = width // (cores * chips)
        qkv_blocks = qkv_grad.reshape(3, cores, chips, qkv_rows, heads_rows)
        qkv_blocks = jnp.swapaxes(sum_cores(qkv_blocks, 1), 0, 1)
        gains = jnp.stack([gain_attn_part, gain_mlp_part])
        for bit in (1 << b for b in range(ranks.bit_length() - 1)):
            gains = gains + flip(gains, "tensor", bit, ranks)
        gain_rows = jnp.pad(gains, ((0, 6), (0, 0))).astype(BF)
        qkv_here = Halving(qkv_blocks, chip, chips, True).finish()
        groups = width // heads_rows
        qkv_part = qkv_rows // groups
        qkv_here = qkv_here.reshape(3, groups, qkv_part, heads_rows)
        qkv_here = jnp.concatenate(
            [qkv_here[:, g].reshape(3 * qkv_part, heads_rows) for g in range(groups)], axis=1
        )
        pieces = jnp.concatenate([z_total, gain_rows, down_total, qkv_here])
        every = lax.all_gather(pieces, ("core", "chip"))
        grads = assemble(every, (cores, chips, share, per, piece, out_piece, qkv_part))
        at = 2 * piece + out_piece
        grad_gain_attn, grad_gain_mlp = jnp.sum(every[:, at : at + 2].astype(F32), axis=0)
        grad_gateup = jnp.swapaxes(grads[0], 1, 2)
        down_weight_gradient = grads[1]
        output_weight_gradient = grads[2].reshape(heads_rows, width)
        query_key_value_gradient = grads[3].reshape(3, width, heads_rows)
        return (
            layer_out[None],
            input_grad[None],
            grad_gain_attn,
            query_key_value_gradient,
            output_weight_gradient,
            grad_gain_mlp,
            grad_gateup,
            down_weight_gradient,
        )

    return on_device


def solution(mesh):
    ranks = mesh.shape["tensor"]
    cores = 2
    chips = mesh.shape["dp"] // cores
    split = Mesh(mesh.devices.reshape(chips, cores, ranks), ("chip", "core", "tensor"))
    dp = ("chip", "core")
    rows = P(dp, "tensor", None)
    last = P(None, None, "tensor")
    first = P("tensor", None)
    return jax.shard_map(
        make(chips, cores, ranks),
        mesh=split,
        in_specs=(rows, P(dp, None), P(), last, first, P(), last, first, rows),
        out_specs=(rows, rows, P(), last, first, P(), last, first),
        check_vma=False,
    )
```
